256 devices in a mesh: tm: 32 (over x, z_lo, y), batch: 8 (over z_hi, core).
Axes of the slice: x: 4, y: 4, z: 8 (z_hi: 4, z_lo: 2; z = z_hi * 2 + z_lo), core: 2. Of those that a mesh axis runs over, the one named last changes fastest.
Arguments:
- inputs: bfloat16 [8, 8192, 512], P('batch', 'tm'), may hold values from -6 to 6
- cotangent: bfloat16 [8, 8192, 512], P('batch', 'tm'), may hold values from -6 to 6
- w_pos: float32 [64, 64], replicated, may hold values from -0.75 to 0.75
- w_filt: float32 [64, 512], replicated, may hold values from -0.75 to 0.75
- log_rates: float32 [512], replicated, may hold values from -9.5 to -3.5
- skip_gain: float32 [512], replicated, may hold values from 0.5 to 1.5
- w_conv: bfloat16 [512, 5, 512], replicated, may hold values from -0.125 to 0.125
Outputs:
- mixed: bfloat16 [8, 8192, 512], P('batch', 'tm')
- input_grad: bfloat16 [8, 8192, 512], P('batch', 'tm')
- conv_grad: float32 [512, 5, 512], P('tm')
- pos_grad: float32 [64, 64], replicated
- filt_grad: float32 [64, 512], replicated
- rates_grad: float32 [512], replicated
- skip_grad: float32 [512], replicated
The draws below stay inside these ranges and needn't reach their ends.
All inputs are finite; a program needn't handle non-finite values.
Results may differ from the reference program's by a relative error of at most 0.0051.
Values may be sent and summed in bfloat16 or wider, within the bound.
No kernel may reach another device: no remote copies, remote signals or barrier semaphores. Data moves between devices by JAX's collectives and lax.ppermute only.
A program may use at most 64 MiB of HBM per device.

```python
import math
import jax
import jax.numpy as jnp
import numpy as np
from jax import lax

CH = 512
FEAT = 64
ORDER = 64
KS = 5
SEQ = 8192
SEQS = 8


def block_levels(rng, shape, split, low, top_value):
    loudness, own = 1.0, jax.random.fold_in(rng, 6)
    for axis_at, blocks in split:
        steps = jnp.exp(jax.random.uniform(jax.random.fold_in(own, axis_at), (blocks,), jnp.float32, low / len(split), top_value / len(split)))
        loudness = loudness * jnp.repeat(steps, shape[axis_at] // blocks).reshape([-1 if axis == axis_at else 1 for axis in range(len(shape))])
    return loudness


def normal_values(rng, dims, scale, reach, split=(), kind=jnp.bfloat16):
    result = jax.random.normal(rng, dims, jnp.float32) * scale
    if len(split) > 0:
        result = block_levels(rng, dims, split, -0.22, 0.18) * result
    return jnp.clip(result, min=-reach, max=reach).astype(kind)


def setup_inputs(seed: int = 0) -> dict:
    arg_keys = jax.random.split(jax.random.key(seed), 8)
    inputs = normal_values(arg_keys[0], (SEQS, SEQ, CH), 1.0, 6.0, ((0, 8), (1, 32)))
    cotangent = normal_values(arg_keys[1], (SEQS, SEQ, CH), 1.0, 6.0, ((0, 8), (1, 32)))
    w_pos = normal_values(arg_keys[2], (FEAT, ORDER), FEAT ** -0.5, 0.75, (), jnp.float32)
    w_filt = normal_values(arg_keys[3], (ORDER, CH), ORDER ** -0.5, 0.75, (), jnp.float32)
    log_rates = jnp.clip(jax.random.uniform(arg_keys[4], (CH,), jnp.float32, -9.5, -3.5), -9.5, -3.5)
    skip_gain = jnp.clip(jax.random.uniform(arg_keys[5], (CH,), jnp.float32, 0.5, 1.5), 0.5, 1.5)
    w_conv = normal_values(arg_keys[6], (CH, KS, CH), (KS * CH) ** -0.5, 0.125)
    return dict(inputs=inputs, cotangent=cotangent, w_pos=w_pos, w_filt=w_filt, log_rates=log_rates, skip_gain=skip_gain, w_conv=w_conv)


PRECISE = lax.Precision.HIGHEST

def multipliers(half_width, length):
    return np.array([1 + index * index * length // (2 * half_width * half_width) for index in range(half_width)], dtype=np.int32)

def features(positions, length, width):
    half_width = width // 2
    factor = jnp.asarray(multipliers(half_width, length))
    phase_int = positions[:, None] * factor[None, :] % length
    angles = 2.0 * math.pi / length * phase_int.astype(jnp.float32)
    return jnp.concatenate([jnp.sin(angles), jnp.cos(angles)], axis=1)

def filter_taps(w_pos, w_filt, log_rates, positions, length):
    hidden = jnp.sin(jnp.dot(features(positions, length, w_pos.shape[0]), w_pos, precision=PRECISE))
    shaped = jnp.dot(hidden, w_filt, precision=PRECISE)
    decay_rates = jnp.exp(log_rates)
    step_times = positions.astype(jnp.float32)
    return shaped * jnp.sqrt(decay_rates)[None, :] * jnp.exp(-step_times[:, None] * decay_rates[None, :])

def gelu_value(values):
    return jax.nn.gelu(values, approximate=True)

def long_conv(signal, kernel_taps, conjugate):
    length = signal.shape[0]
    first_spec = jnp.fft.rfft(signal, n=2 * length, axis=0)
    second_spec = jnp.fft.rfft(kernel_taps, n=2 * length, axis=0)
    if conjugate:
        second_spec = jnp.conj(second_spec)
    return jnp.fft.irfft(first_spec * second_spec, n=2 * length, axis=0)[:length]

def reference(inputs, cotangent, w_pos, w_filt, log_rates, skip_gain, w_conv):
    positions = jnp.arange(SEQ, dtype=jnp.int32)
    tap_rounded = filter_taps(w_pos, w_filt, log_rates, positions, SEQ).astype(jnp.bfloat16)
    tap_values = lax.optimization_barrier(tap_rounded).astype(jnp.float32)
    outputs = []
    input_grads = []
    grad_taps = jnp.zeros((SEQ, CH), jnp.float32)
    grad_skip = jnp.zeros((CH,), jnp.float32)
    grad_conv = jnp.zeros((CH, KS, CH), jnp.float32)
    for member in range(SEQS):
        signal = inputs[member].astype(jnp.float32)
        before = long_conv(signal, tap_values, False) + skip_gain[None, :] * signal
        active = gelu_value(before).astype(jnp.bfloat16)
        padded = jnp.pad(active, ((KS - 1, 0), (0, 0)))
        upstream = cotangent[member]
        reaching = jnp.pad(upstream, ((0, KS - 1), (0, 0)))
        mixed = jnp.zeros((SEQ, CH), jnp.float32)
        grad_active = jnp.zeros((SEQ, CH), jnp.float32)
        for offset in range(KS):
            window = padded[KS - 1 - offset:KS - 1 - offset + SEQ]
            mixed = mixed + jnp.dot(window, w_conv[:, offset, :], preferred_element_type=jnp.float32)
            grad_conv = grad_conv.at[:, offset, :].add(jnp.dot(window.T, upstream, preferred_element_type=jnp.float32))
            grad_active = grad_active + jnp.dot(reaching[offset:offset + SEQ], w_conv[:, offset, :].T, preferred_element_type=jnp.float32)
        outputs.append(mixed.astype(jnp.bfloat16))
        grad_rounded = jax.vjp(gelu_value, before)[1](grad_active)[0].astype(jnp.bfloat16)
        grad_wide = lax.optimization_barrier(grad_rounded).astype(jnp.float32)
        long_grad = long_conv(grad_wide, tap_values, True)
        input_grads.append((long_grad + skip_gain[None, :] * grad_wide).astype(jnp.bfloat16))
        grad_taps = grad_taps + long_conv(grad_wide, signal, True)
        grad_skip = grad_skip + lax.optimization_barrier(jnp.sum(grad_wide * signal, axis=0))

    def taps_of(pos_weight, filt_weight, rate_logs):
        return filter_taps(pos_weight, filt_weight, rate_logs, positions, SEQ)
    pullback = jax.vjp(taps_of, w_pos, w_filt, log_rates)[1]
    grad_pos, grad_filt, grad_rates = pullback(grad_taps)
    scale = 1.0 / math.sqrt(SEQS * SEQ)
    return (jnp.stack(outputs), jnp.stack(input_grads), grad_conv * scale, grad_pos * scale, grad_filt * scale, grad_rates * scale, grad_skip * scale)
```

```python
import math

import jax
import jax.numpy as jnp
import ml_dtypes
import numpy as np
from jax import lax
from jax.experimental import pallas as pl
from jax.experimental.pallas import tpu as pltpu
from jax.sharding import PartitionSpec as P

F32 = jnp.float32
BF16 = jnp.bfloat16

SHARDS = 32
ROWS = 256
LENGTH = SHARDS * ROWS
WIDTH = 512
KERNEL = 5
FEAT = 64
OWN = WIDTH // SHARDS
LANES = 128
STEPS = LENGTH // LANES
STACK = STEPS * OWN
HALO = LANES
SPAN = ROWS + HALO
HALF = WIDTH // 2
CONV = KERNEL * HALF
BLOCK = 1024


def split_table(values):
    high = values.astype(ml_dtypes.bfloat16)
    low = (values - high.astype(np.float64)).astype(ml_dtypes.bfloat16)
    return high, low


def feature_tables():
    half = FEAT // 2
    factor = np.array([1 + i * i * LENGTH // (2 * half * half) for i in range(half)], dtype=np.int64)
    steps = np.arange(LENGTH, dtype=np.int64)
    angles = 2.0 * np.pi * ((factor[:, None] * steps[None, :]) % LENGTH) / LENGTH
    return split_table(np.concatenate([np.sin(angles), np.cos(angles)], axis=0))


def transform_tables():
    order = np.array([2 * p + h for h in range(2) for p in range(STEPS // 2)])
    k1 = np.arange(STEPS)
    alpha = np.pi * order[None, :] / STEPS / 2 - 2.0 * np.pi * ((order[None, :] * k1[:, None]) % STEPS) / STEPS
    outer = np.concatenate([np.cos(alpha), np.sin(alpha)], axis=0)
    outer_high, outer_low = split_table(outer)
    first = np.concatenate([outer_high, outer_low], axis=1)
    back_high, back_low = split_table(outer.T / LENGTH)
    last = np.concatenate([back_high, back_low, back_high], axis=1)
    b = np.arange(LANES)
    beta = np.pi * b[None, :] / (2 * LENGTH) - 2.0 * np.pi * ((b[None, :] * k1[:, None]) % LENGTH) / LENGTH
    twist_cos = np.cos(beta).astype(np.float32)
    twist_sin = np.sin(beta).astype(np.float32)
    gamma = 2.0 * np.pi * ((b[:, None] * b[None, :]) % LANES) / LANES
    cos, sin = np.cos(gamma), np.sin(gamma)
    ahead = split_table(np.block([[cos, -sin], [sin, cos]]))
    behind = split_table(np.block([[cos, sin], [-sin, cos]]))
    return (first, last, twist_cos, twist_sin, *ahead, *behind)


def split(values):
    high = values.astype(BF16)
    return high, (values - high.astype(F32)).astype(BF16)


def mul(left, right, dims=((1,), (0,))):
    return lax.dot_general(left, right, (dims, ((), ())), preferred_element_type=F32)


def mul3(left, right, dims=((1,), (0,))):
    lh, ll = left
    rh, rl = right
    return mul(lh, rh, dims) + mul(ll, rh, dims) + mul(lh, rl, dims)


def spectrum(stack_ref, high_ref, low_ref, tabs):
    first, _, tc_ref, ts_ref, ahead_high, ahead_low, _, _ = tabs
    tc, ts = tc_ref[...], ts_ref[...]
    for c in range(0, OWN, 2):
        pair = [stack_ref[pl.ds(c + k, STEPS, stride=OWN), :] for k in range(2)]
        wide = jnp.concatenate(pair, axis=1).astype(BF16)
        u = mul(first[...], jnp.concatenate([wide, wide], axis=0))
        for k in range(2):
            ur = u[:STEPS, k * LANES : (k + 1) * LANES]
            ui = u[STEPS:, k * LANES : (k + 1) * LANES]
            v = jnp.concatenate([ur * tc - ui * ts, ur * ts + ui * tc], axis=1)
            high, low = split(v)
            high_ref[(c + k) * STEPS : (c + k + 1) * STEPS, :] = high
            low_ref[(c + k) * STEPS : (c + k + 1) * STEPS, :] = low
    return mul3((high_ref[...], low_ref[...]), (ahead_high[...], ahead_low[...]))


def from_spectrum(values, stack_ref, tabs):
    _, last, tc_ref, ts_ref, _, _, behind_high, behind_low = tabs
    tc, ts = tc_ref[...], ts_ref[...]
    q = mul3(split(values), (behind_high[...], behind_low[...]))
    for c in range(0, OWN, 2):
        pair = []
        for k in range(2):
            rows = q[(c + k) * STEPS : (c + k + 1) * STEPS]
            qr, qi = rows[:, :LANES], rows[:, LANES:]
            pair.append(jnp.concatenate([qr * tc + qi * ts, qi * tc - qr * ts], axis=0))
        high, low = split(jnp.concatenate(pair, axis=1))
        y = mul(last[...], jnp.concatenate([high, high, low], axis=0))
        for k in range(2):
            stack_ref[pl.ds(c + k, STEPS, stride=OWN), :] = y[:, k * LANES : (k + 1) * LANES]


def product(left, right, conjugate):
    lr, li = left[:, :LANES], left[:, LANES:]
    rr, ri = right[:, :LANES], right[:, LANES:]
    if conjugate:
        return jnp.concatenate([lr * rr + li * ri, lr * ri - li * rr], axis=1)
    return jnp.concatenate([lr * rr - li * ri, lr * ri + li * rr], axis=1)


def sin_cos(x):
    turns = jnp.floor(x * (2.0 / math.pi) + 0.5)
    r = x - turns * 1.5703125
    r = r - turns * 4.837512969970703125e-4
    r = r - turns * 7.549789948768648e-8
    z = r * r
    s = r + r * z * (-1.6666654611e-1 + z * (8.3321608736e-3 - z * 1.9515295891e-4))
    c = 1.0 - 0.5 * z + z * z * (4.166664568298827e-2 + z * (-1.388731625493765e-3 + z * 2.443315711809948e-5))
    quad = turns.astype(jnp.int32)
    odd = (quad & 1) == 1
    sin = jnp.where(odd, c, s)
    cos = jnp.where(odd, s, c)
    sin = jnp.where((quad & 2) == 2, -sin, sin)
    cos = jnp.where(((quad + 1) & 2) == 2, -cos, cos)
    return sin, cos


def envelope(rates, start, size):
    steps = (start + lax.broadcasted_iota(jnp.int32, (OWN, size), 1)).astype(F32)
    return jnp.sqrt(rates) * jnp.exp(-steps * rates), steps


def prep_kernel(x_ref, cot_ref, w_ref, out_ref, pad_ref, shift_ref):
    out_ref[:, :ROWS] = jnp.transpose(x_ref[...].astype(F32)).astype(BF16)
    pad_ref[:HALO, :] = jnp.zeros((HALO, WIDTH), F32)
    pad_ref[HALO + ROWS :, :] = jnp.zeros((8, WIDTH), F32)
    pad_ref[HALO : HALO + ROWS, :] = cot_ref[...].astype(F32)
    for i in range(KERNEL):
        shift_ref[i] = pad_ref[i : i + SPAN, :].astype(BF16)
    for c in range(0, WIDTH, 128):
        total = jnp.zeros((128, SPAN), F32)
        for i in range(KERNEL):
            total = total + mul(w_ref[i, c : c + 128, :], shift_ref[i], ((1,), (1,)))
        out_ref[c : c + 128, ROWS:] = total.astype(BF16)


def taps_kernel(
    wp_ref, wf_ref, lr_ref, fh_ref, fl_ref, *rest
):
    tabs = rest[:8]
    hh_ref, hl_ref, cos_ref, taps_ref, spec_ref, stack_ref, vh_ref, vl_ref = rest[8:]
    wp = split(wp_ref[...])
    wf = split(wf_ref[...])
    rates = jnp.exp(lr_ref[...])
    for start in range(0, LENGTH, BLOCK):
        cut = slice(start, start + BLOCK)
        sin, cos = sin_cos(mul3(wp, (fh_ref[:, cut], fl_ref[:, cut])))
        high, low = split(sin)
        hh_ref[:, cut] = high
        hl_ref[:, cut] = low
        cos_ref[:, cut] = cos
        decay, _ = envelope(rates, start, BLOCK)
        taps = mul3(wf, (high, low)) * decay
        taps_ref[:, cut] = taps
        rounded = taps.astype(BF16).astype(F32)
        for j in range(BLOCK // LANES):
            a = start // LANES + j
            row = ((a % 2) * SHARDS + a // 2) * OWN
            stack_ref[row : row + OWN, :] = rounded[:, j * LANES : (j + 1) * LANES]
    spec_ref[...] = spectrum(stack_ref, vh_ref, vl_ref, tabs)


def forward_kernel(recv_ref, tspec_ref, gain_ref, *rest):
    tabs = rest[:8]
    act_ref, gb_ref, xspec_ref, skip_ref, x_ref, y_ref, vh_ref, vl_ref = rest[8:]
    for h in range(2):
        part = recv_ref[:, :, h * LANES : (h + 1) * LANES].astype(F32)
        x_ref[h * STACK // 2 : (h + 1) * STACK // 2, :] = part.reshape(STACK // 2, LANES)
    spec = spectrum(x_ref, vh_ref, vl_ref, tabs)
    xspec_ref[...] = spec
    from_spectrum(product(tspec_ref[...], spec, False), y_ref, tabs)
    gain = gain_ref[...][None]
    x = x_ref[...].reshape(STEPS, OWN, LANES)
    before = y_ref[...].reshape(STEPS, OWN, LANES) + gain * x
    root = math.sqrt(2.0 / math.pi)
    square = before * before
    th = jnp.tanh(root * (before + 0.044715 * square * before))
    half_cdf = 0.5 * (1.0 + th)
    active = (before * half_cdf).astype(BF16)
    slope = half_cdf + 0.5 * before * (1.0 - th * th) * (root * (1.0 + 3.0 * 0.044715 * square))
    early = recv_ref[:, :, ROWS + HALO : ROWS + HALO + LANES].astype(F32)
    late = recv_ref[:, :, ROWS + HALO + LANES : ROWS + HALO + 2 * LANES].astype(F32)
    edge = recv_ref[:, :, ROWS : ROWS + HALO].astype(F32)
    edge = jnp.concatenate([edge[1:], jnp.zeros((1, OWN, LANES), F32)], axis=0)
    grad_active = jnp.concatenate([early, late + edge], axis=0)
    grad_before = (grad_active * slope).astype(BF16).astype(F32)
    gb_ref[...] = grad_before.reshape(STACK, LANES)
    skip_ref[...] = jnp.sum(grad_before * x, axis=0)
    first, second = active[:SHARDS], active[SHARDS:]
    act_ref[:, :, HALO : HALO + LANES] = first
    act_ref[:, :, HALO + LANES :] = second
    act_ref[:, :, :HALO] = jnp.concatenate([jnp.zeros((1, OWN, LANES), BF16), second[:-1]], axis=0)


def backward_kernel(
    gb_ref, xspec_ref, tspec_ref, gain_ref, skip_ref, hh_ref, hl_ref, cos_ref, fh_ref, fl_ref, taps_ref, wf_ref, lr_ref, *rest
):
    tabs = rest[:8]
    ig_ref, small_ref, y_ref, vh_ref, vl_ref, g_ref = rest[8:]
    spec = spectrum(gb_ref, vh_ref, vl_ref, tabs)
    from_spectrum(product(tspec_ref[...], spec, True), y_ref, tabs)
    gain = gain_ref[...][None]
    grad = gb_ref[...].reshape(STEPS, OWN, LANES)
    result = (y_ref[...].reshape(STEPS, OWN, LANES) + gain * grad).astype(BF16)
    ig_ref[:, :, :LANES] = result[:SHARDS]
    ig_ref[:, :, LANES:] = result[SHARDS:]
    from_spectrum(product(xspec_ref[...], spec, True), y_ref, tabs)
    for a in range(STEPS):
        row = ((a % 2) * SHARDS + a // 2) * OWN
        g_ref[:, a * LANES : (a + 1) * LANES] = y_ref[row : row + OWN, :]
    wf = split(wf_ref[...])
    rates = jnp.exp(lr_ref[...])
    filt = jnp.zeros((OWN, FEAT), F32)
    pos = jnp.zeros((FEAT, FEAT), F32)
    rate = jnp.zeros((OWN, 1), F32)
    for start in range(0, LENGTH, BLOCK):
        cut = slice(start, start + BLOCK)
        grad_taps = g_ref[:, cut]
        decay, steps = envelope(rates, start, BLOCK)
        shaped = split(grad_taps * decay)
        rate = rate + jnp.sum(grad_taps * taps_ref[:, cut] * (0.5 - rates * steps), axis=1, keepdims=True)
        filt = filt + mul3(shaped, (hh_ref[:, cut], hl_ref[:, cut]), ((1,), (1,)))
        inner = split(mul3(wf, shaped, ((0,), (0,))) * cos_ref[:, cut])
        pos = pos + mul3((fh_ref[:, cut], fl_ref[:, cut]), inner, ((1,), (1,)))
    small_ref[...] = jnp.zeros((48, LANES), F32)
    small_ref[:32, :FEAT] = pos[:32]
    small_ref[:32, FEAT:] = pos[32:]
    small_ref[32:, :FEAT] = filt
    small_ref[32:, 64:65] = rate
    small_ref[32:, 65:66] = jnp.sum(skip_ref[...], axis=1, keepdims=True)


def conv_kernel(act_ref, peer_act_ref, cot_ref, peer_cot_ref, ig_ref, small_ref, out_ref, pad_ref):
    pad_ref[:, :HALO, :] = jnp.zeros((2, HALO, HALF), F32)
    pad_ref[:, HALO + ROWS :, :] = jnp.zeros((2, 8, HALF), F32)
    pad_ref[0, HALO : HALO + ROWS, :] = cot_ref[...].astype(F32)
    pad_ref[1, HALO : HALO + ROWS, :] = peer_cot_ref[...].astype(F32)
    for i in range(KERNEL):
        own = pad_ref[0, i : i + SPAN, :].astype(BF16)
        peer = pad_ref[1, i : i + SPAN, :].astype(BF16)
        part = mul(act_ref[...], own) + mul(peer_act_ref[...], peer)
        out_ref[:, i * HALF : (i + 1) * HALF] = part.astype(BF16)
    out_ref[:, CONV : CONV + ROWS] = ig_ref[...]
    small = small_ref[...]
    pos = jnp.concatenate(split(small[:16]), axis=1)
    filt = jnp.concatenate([v.astype(F32) for v in split(small[16:])], axis=0).astype(BF16)
    tile = jnp.concatenate([pos, filt], axis=1)
    for p in range(SHARDS):
        out_ref[p * OWN : (p + 1) * OWN, CONV + ROWS :] = tile


def mixed_kernel(act_ref, w_ref, out_ref, part_ref):
    act = jnp.transpose(act_ref[...].astype(F32)).astype(BF16)[HALO - 16 :]
    total = jnp.zeros((ROWS, WIDTH), F32)
    for i in range(KERNEL):
        part_ref[...] = mul(act, w_ref[i])
        total = total + part_ref[16 - i : 16 - i + ROWS, :]
    out_ref[...] = total.astype(BF16)


def gather_kernel(recv_ref, ig_ref, out_ref):
    conv = jnp.sum(recv_ref[:, :, :CONV].astype(F32), axis=0)
    out_ref[:, :CONV] = conv.astype(BF16)
    ig = recv_ref[:, :, CONV : CONV + ROWS].astype(F32).reshape(WIDTH, ROWS)
    ig_ref[...] = jnp.transpose(ig).astype(BF16)
    base = CONV + ROWS
    pos = jnp.sum(
        recv_ref[:, :, base : base + LANES].astype(F32) + recv_ref[:, :, base + LANES : base + 2 * LANES].astype(F32), axis=0
    )
    pos_high, pos_low = split(pos)
    out_ref[:, CONV : CONV + LANES] = pos_high
    out_ref[:, CONV + LANES : CONV + 2 * LANES] = pos_low
    both = recv_ref[:, :, base + 2 * LANES : base + 3 * LANES].astype(F32)
    filt = both[:, :8] + both[:, 8:]
    for j in range(16):
        block = filt[2 * j : 2 * j + 2].reshape(16, LANES)
        out_ref[:, CONV + (2 + j) * LANES : CONV + (3 + j) * LANES] = block.astype(BF16)


def final_kernel(recv_ref, conv_ref, rest_ref):
    scale = 1.0 / math.sqrt(8 * LENGTH)
    total = jnp.sum(recv_ref[...].astype(F32), axis=0) * scale
    conv_ref[...] = total[:, :CONV]
    rest_ref[:16, :] = total[:, CONV : CONV + LANES] + total[:, CONV + LANES : CONV + 2 * LANES]
    for j in range(16):
        rest_ref[16 + 16 * j : 32 + 16 * j, :] = total[:, CONV + (2 + j) * LANES : CONV + (3 + j) * LANES]


def call(kernel, out_shape, args, scratch=(), flops=0, name=None):
    vmem = pl.BlockSpec(memory_space=pltpu.VMEM)
    single = not isinstance(out_shape, (list, tuple))
    outs = [out_shape] if single else out_shape
    moved = sum(math.prod(a.shape) * a.dtype.itemsize for a in (*args, *outs))
    return pl.pallas_call(
        kernel,
        out_shape=out_shape,
        in_specs=[vmem] * len(args),
        out_specs=vmem if single else [vmem] * len(outs),
        scratch_shapes=list(scratch),
        compiler_params=pltpu.CompilerParams(vmem_limit_bytes=48 * 1024 * 1024),
        cost_estimate=pl.CostEstimate(flops=flops, bytes_accessed=moved, transcendentals=0),
        name=name,
    )(*args)


def shape(dims, kind=F32):
    return jax.ShapeDtypeStruct(dims, kind)


def on_device(inputs, cotangent, w_pos, w_filt, log_rates, skip_gain, w_conv):
    rank = lax.axis_index("tm")
    core = lax.axis_index("batch") % 2
    swap = [(i, i ^ 1) for i in range(lax.axis_size("batch"))]
    signal, upstream = inputs[0], cotangent[0]
    w_taps = jnp.transpose(w_conv, (1, 0, 2))
    tabs = tuple(jnp.asarray(t) for t in transform_tables())
    feat = tuple(jnp.asarray(t) for t in feature_tables())

    def exchange(low, high):
        mine = jnp.where(core == 0, low, high)
        theirs = jnp.where(core == 0, high, low)
        return mine, lax.ppermute(theirs, "batch", swap)

    message = call(
        prep_kernel,
        shape((WIDTH, ROWS + SPAN), BF16),
        (signal, upstream, w_taps),
        [pltpu.VMEM((HALO + ROWS + 8, WIDTH), F32), pltpu.VMEM((KERNEL, SPAN, WIDTH), BF16)],
        flops=2 * KERNEL * WIDTH * WIDTH * SPAN,
        name="prep",
    )
    received = lax.all_to_all(
        message.reshape(SHARDS, OWN, ROWS + SPAN), "tm", split_axis=0, concat_axis=0, tiled=True
    )
    cot_mine, cot_peer = exchange(upstream[:, :HALF], upstream[:, HALF:])

    own = rank * OWN
    wf_own = lax.dynamic_slice(w_filt, (0, own), (FEAT, OWN)).T
    lr_own = lax.dynamic_slice(log_rates, (own,), (OWN,))[:, None]
    gain_own = lax.dynamic_slice(skip_gain, (own,), (OWN,))[:, None]
    stack = pltpu.VMEM((STACK, LANES), F32)
    wide = pltpu.VMEM((STACK, 2 * LANES), BF16)
    flops = 2 * 3 * (2 * STACK * LANES * LANES + STACK * 4 * LANES * LANES)
    hid_high, hid_low, cosines, taps, tap_spec = call(
        taps_kernel,
        [
            shape((FEAT, LENGTH), BF16),
            shape((FEAT, LENGTH), BF16),
            shape((FEAT, LENGTH)),
            shape((OWN, LENGTH)),
            shape((STACK, 2 * LANES)),
        ],
        (w_pos.T, wf_own, lr_own, *feat, *tabs),
        [stack, wide, wide],
        flops=flops * 2,
        name="taps",
    )
    act_message, grad_before, sig_spec, skip_part = call(
        forward_kernel,
        [
            shape((SHARDS, OWN, SPAN), BF16),
            shape((STACK, LANES)),
            shape((STACK, 2 * LANES)),
            shape((OWN, LANES)),
        ],
        (received, tap_spec, gain_own, *tabs),
        [stack, stack, wide, wide],
        flops=flops * 2,
        name="forward",
    )
    act = lax.all_to_all(act_message, "tm", split_axis=0, concat_axis=0, tiled=True).reshape(WIDTH, SPAN)
    ig_message, small = call(
        backward_kernel,
        [shape((SHARDS, OWN, ROWS), BF16), shape((48, LANES))],
        (
            grad_before,
            sig_spec,
            tap_spec,
            gain_own,
            skip_part,
            hid_high,
            hid_low,
            cosines,
            *feat,
            taps,
            wf_own,
            lr_own,
            *tabs,
        ),
        [stack, wide, wide, pltpu.VMEM((OWN, LENGTH), F32)],
        flops=flops * 4,
        name="backward",
    )
    mine, theirs = exchange(
        jnp.concatenate([small[:16], small[32:40]], axis=0), jnp.concatenate([small[16:32], small[40:]], axis=0)
    )
    small_half = mine + theirs
    act_peer = lax.ppermute(act, "batch", swap)
    lanes = CONV + ROWS + 3 * LANES
    sums = call(
        conv_kernel,
        shape((WIDTH, lanes), BF16),
        (act, act_peer, cot_mine, cot_peer, ig_message.reshape(WIDTH, ROWS), small_half),
        [pltpu.VMEM((2, HALO + ROWS + 8, HALF), F32)],
        flops=2 * KERNEL * WIDTH * HALF * 2 * SPAN,
        name="conv_grad",
    )
    sums = lax.all_to_all(sums.reshape(SHARDS, OWN, lanes), "tm", split_axis=0, concat_axis=0, tiled=True)
    mixed = call(
        mixed_kernel,
        shape((ROWS, WIDTH), BF16),
        (act, w_taps),
        [pltpu.VMEM((ROWS + 16, WIDTH), F32)],
        flops=2 * KERNEL * WIDTH * WIDTH * (ROWS + 16),
        name="mixed",
    )
    payload_lanes = CONV + 18 * LANES
    input_grad, payload = call(
        gather_kernel,
        [shape((ROWS, WIDTH), BF16), shape((OWN, payload_lanes), BF16)],
        (sums,),
        name="gather",
    )
    groups = [[2 * z + e for z in range(4)] for e in range(2)]
    spread = lax.all_to_all(
        jnp.broadcast_to(payload[None], (4, OWN, payload_lanes)),
        "batch",
        split_axis=0,
        concat_axis=0,
        tiled=True,
        axis_index_groups=groups,
    )
    conv_half, rest = call(final_kernel, [shape((OWN, CONV)), shape((16 + HALF, LANES))], (spread,), name="final")
    conv_other = lax.ppermute(conv_half, "batch", swap)
    rest_other = lax.ppermute(rest, "batch", swap)

    def ordered(mine, other):
        return jnp.where(core == 0, mine, other), jnp.where(core == 0, other, mine)

    conv_low, conv_high = ordered(conv_half, conv_other)
    conv_grad = jnp.concatenate([v.reshape(OWN, KERNEL, HALF) for v in (conv_low, conv_high)], axis=2)
    rest_low, rest_high = ordered(rest, rest_other)
    pos_grad = jnp.concatenate([rest_low[:16, :FEAT], rest_high[:16, :FEAT], rest_low[:16, FEAT:], rest_high[:16, FEAT:]], axis=0)
    filt = jnp.concatenate([v[16:].reshape(SHARDS, 8, LANES) for v in (rest_low, rest_high)], axis=1).reshape(WIDTH, LANES)
    return (
        mixed[None],
        input_grad[None],
        conv_grad,
        pos_grad,
        filt[:, :FEAT].T,
        filt[:, 64],
        filt[:, 65],
    )


def solution(mesh):
    in_specs = (P("batch", "tm", None), P("batch", "tm", None), P(), P(), P(), P(), P())
    out_specs = (P("batch", "tm", None), P("batch", "tm", None), P("tm", None, None), P(), P(), P(), P())
    return jax.shard_map(on_device, mesh=mesh, in_specs=in_specs, out_specs=out_specs, check_vma=False)
```

```python
import math

import jax
import jax.numpy as jnp
import ml_dtypes
import numpy as np
from jax import lax
from jax.experimental import pallas as pl
from jax.experimental.pallas import tpu as pltpu
from jax.sharding import PartitionSpec as P

F32 = jnp.float32
BF16 = jnp.bfloat16

SHARDS = 32
ROWS = 256
LENGTH = SHARDS * ROWS
WIDTH = 512
KERNEL = 5
FEAT = 64
OWN = WIDTH // SHARDS
LANES = 128
STEPS = LENGTH // LANES
STACK = STEPS * OWN
HALO = LANES
SPAN = ROWS + HALO
HALF = WIDTH // 2
CONV = KERNEL * HALF
BLOCK = 1024


def split_table(values):
    high = values.astype(ml_dtypes.bfloat16)
    low = (values - high.astype(np.float64)).astype(ml_dtypes.bfloat16)
    return high, low


def feature_tables():
    half = FEAT // 2
    factor = np.array([1 + i * i * LENGTH // (2 * half * half) for i in range(half)], dtype=np.int64)
    steps = np.arange(LENGTH, dtype=np.int64)
    angles = 2.0 * np.pi * ((factor[:, None] * steps[None, :]) % LENGTH) / LENGTH
    return split_table(np.concatenate([np.sin(angles), np.cos(angles)], axis=0))


def transform_tables():
    order = np.array([2 * p + h for h in range(2) for p in range(STEPS // 2)])
    k1 = np.arange(STEPS)
    alpha = np.pi * order[None, :] / STEPS / 2 - 2.0 * np.pi * ((order[None, :] * k1[:, None]) % STEPS) / STEPS
    outer = np.concatenate([np.cos(alpha), np.sin(alpha)], axis=0)
    outer_high, outer_low = split_table(outer)
    first = np.concatenate([outer_high, outer_low], axis=1)
    back_high, back_low = split_table(outer.T / LENGTH)
    last = np.concatenate([back_high, back_low, back_high], axis=1)
    b = np.arange(LANES)
    beta = np.pi * b[None, :] / (2 * LENGTH) - 2.0 * np.pi * ((b[None, :] * k1[:, None]) % LENGTH) / LENGTH
    twist_cos = np.cos(beta).astype(np.float32)
    twist_sin = np.sin(beta).astype(np.float32)
    gamma = 2.0 * np.pi * ((b[:, None] * b[None, :]) % LANES) / LANES
    cos, sin = np.cos(gamma), np.sin(gamma)
    ahead = split_table(np.block([[cos, -sin], [sin, cos]]))
    behind = split_table(np.block([[cos, sin], [-sin, cos]]))
    return (first, last, twist_cos, twist_sin, *ahead, *behind)


def split(values):
    high = values.astype(BF16)
    return high, (values - high.astype(F32)).astype(BF16)


def mul(left, right, dims=((1,), (0,))):
    return lax.dot_general(left, right, (dims, ((), ())), preferred_element_type=F32)


def mul3(left, right, dims=((1,), (0,))):
    lh, ll = left
    rh, rl = right
    return mul(lh, rh, dims) + mul(ll, rh, dims) + mul(lh, rl, dims)


def wait_for(loads, *which):
    for k in which:
        if loads is not None:
            loads[k].wait()


def spectrum(stack_ref, high_ref, low_ref, tabs, loads=None):
    first, _, tc_ref, ts_ref, ahead_high, ahead_low, _, _ = tabs
    wait_for(loads, 0, 2, 3)
    tc, ts = tc_ref[...], ts_ref[...]
    for c in range(0, OWN, 2):
        pair = [stack_ref[pl.ds(c + k, STEPS, stride=OWN), :] for k in range(2)]
        wide = jnp.concatenate(pair, axis=1).astype(BF16)
        u = mul(first[...], jnp.concatenate([wide, wide], axis=0))
        for k in range(2):
            ur = u[:STEPS, k * LANES : (k + 1) * LANES]
            ui = u[STEPS:, k * LANES : (k + 1) * LANES]
            v = jnp.concatenate([ur * tc - ui * ts, ur * ts + ui * tc], axis=1)
            high, low = split(v)
            high_ref[(c + k) * STEPS : (c + k + 1) * STEPS, :] = high
            low_ref[(c + k) * STEPS : (c + k + 1) * STEPS, :] = low
    wait_for(loads, 4, 5)
    return mul3((high_ref[...], low_ref[...]), (ahead_high[...], ahead_low[...]))


def from_spectrum(values, stack_ref, tabs, loads=None):
    _, last, tc_ref, ts_ref, _, _, behind_high, behind_low = tabs
    wait_for(loads, 6, 7, 1)
    tc, ts = tc_ref[...], ts_ref[...]
    q = mul3(split(values), (behind_high[...], behind_low[...]))
    for c in range(0, OWN, 2):
        pair = []
        for k in range(2):
            rows = q[(c + k) * STEPS : (c + k + 1) * STEPS]
            qr, qi = rows[:, :LANES], rows[:, LANES:]
            pair.append(jnp.concatenate([qr * tc + qi * ts, qi * tc - qr * ts], axis=0))
        high, low = split(jnp.concatenate(pair, axis=1))
        y = mul(last[...], jnp.concatenate([high, high, low], axis=0))
        for k in range(2):
            stack_ref[pl.ds(c + k, STEPS, stride=OWN), :] = y[:, k * LANES : (k + 1) * LANES]


def product(left, right, conjugate):
    lr, li = left[:, :LANES], left[:, LANES:]
    rr, ri = right[:, :LANES], right[:, LANES:]
    if conjugate:
        return jnp.concatenate([lr * rr + li * ri, lr * ri - li * rr], axis=1)
    return jnp.concatenate([lr * rr - li * ri, lr * ri + li * rr], axis=1)


def sin_cos(x):
    turns = jnp.floor(x * (2.0 / math.pi) + 0.5)
    r = x - turns * 1.5703125
    r = r - turns * 4.837512969970703125e-4
    r = r - turns * 7.549789948768648e-8
    z = r * r
    s = r + r * z * (-1.6666654611e-1 + z * (8.3321608736e-3 - z * 1.9515295891e-4))
    c = 1.0 - 0.5 * z + z * z * (4.166664568298827e-2 + z * (-1.388731625493765e-3 + z * 2.443315711809948e-5))
    quad = turns.astype(jnp.int32)
    odd = (quad & 1) == 1
    sin = jnp.where(odd, c, s)
    cos = jnp.where(odd, s, c)
    sin = jnp.where((quad & 2) == 2, -sin, sin)
    cos = jnp.where(((quad + 1) & 2) == 2, -cos, cos)
    return sin, cos


def envelope(rates, start, size):
    steps = (start + lax.broadcasted_iota(jnp.int32, (OWN, size), 1)).astype(F32)
    return jnp.sqrt(rates) * jnp.exp(-steps * rates), steps


def prep_kernel(x_hbm, cot_hbm, w_hbm, out_hbm, x_ref, cot_ref, w_ref, pad_ref, sum_ref, xt_ref, ga_ref, sems):
    x_copy = pltpu.make_async_copy(x_hbm, x_ref, sems.at[0])
    x_copy.start()
    cot_copy = pltpu.make_async_copy(cot_hbm, cot_ref, sems.at[1])
    cot_copy.start()
    w_copies = [pltpu.make_async_copy(w_hbm.at[i], w_ref.at[i], sems.at[2 + i]) for i in range(KERNEL)]
    for copy in w_copies:
        copy.start()
    pad_ref[:HALO, :] = jnp.zeros((HALO, WIDTH), F32)
    pad_ref[HALO + ROWS :, :] = jnp.zeros((8, WIDTH), F32)
    x_copy.wait()
    xt_ref[...] = jnp.transpose(x_ref[...].astype(F32)).astype(BF16)
    x_out = pltpu.make_async_copy(xt_ref, out_hbm.at[:, pl.ds(0, ROWS)], sems.at[2 + KERNEL])
    x_out.start()
    cot_copy.wait()
    pad_ref[HALO : HALO + ROWS, :] = cot_ref[...].astype(F32)
    for i in range(KERNEL):
        shifted = pad_ref[i : i + SPAN, :].astype(BF16)
        w_copies[i].wait()
        part = mul(w_ref[i], shifted, ((1,), (1,)))
        if i == 0:
            sum_ref[...] = part
        elif i < KERNEL - 1:
            sum_ref[...] += part
        else:
            ga_ref[...] = (sum_ref[...] + part).astype(BF16)
    ga_out = pltpu.make_async_copy(ga_ref, out_hbm.at[:, pl.ds(ROWS, SPAN)], sems.at[3 + KERNEL])
    ga_out.start()
    x_out.wait()
    ga_out.wait()


def taps_kernel(wp_ref, wf_ref, lr_ref, gain_ref, feat_ref, *rest):
    tabs = rest[:8]
    hid_out, cos_out, taps_out, spec_ref, par_ref, hid_ref, cos_ref, taps_ref, stack_ref, vh_ref, vl_ref, sems = rest[8:]
    first = lax.axis_index("tm") * OWN
    lane = lax.broadcasted_iota(jnp.int32, (OWN, WIDTH), 1)
    chosen = lane == first + lax.broadcasted_iota(jnp.int32, (OWN, WIDTH), 0)
    wf_own = lax.dot_general(
        chosen.astype(F32),
        wf_ref[...],
        (((1,), (1,)), ((), ())),
        precision=lax.Precision.HIGHEST,
        preferred_element_type=F32,
    )
    rates = jnp.exp(jnp.sum(jnp.where(chosen, lr_ref[...], 0.0), axis=1, keepdims=True))
    gain = jnp.sum(jnp.where(chosen, gain_ref[...], 0.0), axis=1, keepdims=True)
    spot = lax.broadcasted_iota(jnp.int32, (OWN, LANES), 1)
    par_ref[...] = jnp.where(spot == FEAT, rates, jnp.where(spot == FEAT + 1, gain, 0.0))
    par_ref[:, :FEAT] = wf_own
    wp_high, wp_low = split(wp_ref[...])
    wp = jnp.concatenate([wp_high, wp_low, wp_high], axis=0)
    wf_high, wf_low = split(wf_own)
    for start in range(0, LENGTH, BLOCK):
        cut = slice(start, start + BLOCK)
        feat = feat_ref[:, cut]
        sin, cos = sin_cos(mul(wp, jnp.concatenate([feat[:FEAT], feat], axis=0), ((0,), (0,))))
        high, low = split(sin)
        hid_ref[:FEAT, cut] = high
        hid_ref[FEAT:, cut] = low
        cos_ref[:, cut] = cos
        decay, _ = envelope(rates, start, BLOCK)
        taps = mul3((wf_high, wf_low), (high, low)) * decay
        taps_ref[:, cut] = taps
        rounded = taps.astype(BF16).astype(F32)
        for j in range(BLOCK // LANES):
            a = start // LANES + j
            row = ((a % 2) * SHARDS + a // 2) * OWN
            stack_ref[row : row + OWN, :] = rounded[:, j * LANES : (j + 1) * LANES]
    saves = [
        pltpu.make_async_copy(source, target, sems.at[k])
        for k, (source, target) in enumerate(((hid_ref, hid_out), (cos_ref, cos_out), (taps_ref, taps_out)))
    ]
    for save in saves:
        save.start()
    spec_ref[...] = spectrum(stack_ref, vh_ref, vl_ref, tabs)
    for save in saves:
        save.wait()


def forward_kernel(recv_hbm, tspec_hbm, par_hbm, *rest):
    tabs_hbm = rest[:8]
    act_hbm, gb_hbm, xspec_hbm, skip_ref = rest[8:12]
    xin_ref, gain_ref, tspec_ref, spec_ref, act_ref, gb_ref = rest[12:18]
    tabs = rest[18:26]
    x_ref, y_ref, vh_ref, vl_ref, par_ref, sems = rest[26:]
    par_load = pltpu.make_async_copy(par_hbm, par_ref, sems.at[14])
    par_load.start()
    x_load = pltpu.make_async_copy(recv_hbm.at[:, :, pl.ds(0, ROWS)], xin_ref, sems.at[0])
    x_load.start()
    loads = [pltpu.make_async_copy(tabs_hbm[k], tabs[k], sems.at[1 + k]) for k in range(8)]
    for k in (0, 2, 3, 4, 5, 6, 7, 1):
        loads[k].start()
    tspec_load = pltpu.make_async_copy(tspec_hbm, tspec_ref, sems.at[9])
    tspec_load.start()
    ga_load = pltpu.make_async_copy(recv_hbm.at[:, :, pl.ds(ROWS, SPAN)], gain_ref, sems.at[10])
    ga_load.start()
    x_load.wait()
    for h in range(2):
        part = xin_ref[:, :, h * LANES : (h + 1) * LANES].astype(F32)
        x_ref[h * STACK // 2 : (h + 1) * STACK // 2, :] = part.reshape(STACK // 2, LANES)
    spec = spectrum(x_ref, vh_ref, vl_ref, tabs, loads)
    spec_ref[...] = spec
    spec_save = pltpu.make_async_copy(spec_ref, xspec_hbm, sems.at[11])
    spec_save.start()
    tspec_load.wait()
    from_spectrum(product(tspec_ref[...], spec, False), y_ref, tabs, loads)
    par_load.wait()
    gain = par_ref[:, FEAT + 1 : FEAT + 2][None]
    x = x_ref[...].reshape(STEPS, OWN, LANES)
    before = y_ref[...].reshape(STEPS, OWN, LANES) + gain * x
    root = math.sqrt(2.0 / math.pi)
    square = before * before
    th = jnp.tanh(root * (before + 0.044715 * square * before))
    half_cdf = 0.5 * (1.0 + th)
    active = (before * half_cdf).astype(BF16)
    first, second = active[:SHARDS], active[SHARDS:]
    act_ref[:, :, HALO : HALO + LANES] = first
    act_ref[:, :, HALO + LANES :] = second
    act_ref[:, :, :HALO] = jnp.concatenate([jnp.zeros((1, OWN, LANES), BF16), second[:-1]], axis=0)
    act_save = pltpu.make_async_copy(act_ref, act_hbm, sems.at[12])
    act_save.start()
    slope = half_cdf + 0.5 * before * (1.0 - th * th) * (root * (1.0 + 3.0 * 0.044715 * square))
    ga_load.wait()
    early = gain_ref[:, :, HALO : HALO + LANES].astype(F32)
    late = gain_ref[:, :, HALO + LANES :].astype(F32)
    edge = gain_ref[:, :, :HALO].astype(F32)
    edge = jnp.concatenate([edge[1:], jnp.zeros((1, OWN, LANES), F32)], axis=0)
    grad_active = jnp.concatenate([early, late + edge], axis=0)
    grad_before = (grad_active * slope).astype(BF16).astype(F32)
    gb_ref[...] = grad_before.reshape(STACK, LANES)
    gb_save = pltpu.make_async_copy(gb_ref, gb_hbm, sems.at[13])
    gb_save.start()
    skip_ref[...] = jnp.sum(grad_before * x, axis=0)
    spec_save.wait()
    act_save.wait()
    gb_save.wait()


def backward_kernel(*rest):
    arrays_hbm, tabs_hbm = rest[:9], rest[9:17]
    ig_hbm, small_ref = rest[17:19]
    arrays, tabs = rest[19:28], rest[28:36]
    gb_ref, xspec_ref, tspec_ref, par_ref, skip_ref, hid_ref, cos_ref, feat_ref, taps_ref = arrays
    ig_ref, y_ref, vh_ref, vl_ref, g_ref, sems = rest[36:]
    first = [pltpu.make_async_copy(arrays_hbm[k], arrays[k], sems.at[k]) for k in range(9)]
    table = [pltpu.make_async_copy(tabs_hbm[k], tabs[k], sems.at[9 + k]) for k in range(8)]
    for copy in (first[0], *table, *first[1:]):
        copy.start()
    first[0].wait()
    spec = spectrum(gb_ref, vh_ref, vl_ref, tabs, table)
    wait_for(first, 1, 2, 3, 4)
    from_spectrum(product(tspec_ref[...], spec, True), y_ref, tabs, table)
    gain = par_ref[:, FEAT + 1 : FEAT + 2][None]
    grad = gb_ref[...].reshape(STEPS, OWN, LANES)
    result = (y_ref[...].reshape(STEPS, OWN, LANES) + gain * grad).astype(BF16)
    ig_ref[:, :, :LANES] = result[:SHARDS]
    ig_ref[:, :, LANES:] = result[SHARDS:]
    save = pltpu.make_async_copy(ig_ref, ig_hbm, sems.at[17])
    save.start()
    from_spectrum(product(xspec_ref[...], spec, True), y_ref, tabs)
    for a in range(STEPS):
        row = ((a % 2) * SHARDS + a // 2) * OWN
        g_ref[:, a * LANES : (a + 1) * LANES] = y_ref[row : row + OWN, :]
    wf_high, wf_low = split(par_ref[:, :FEAT])
    wf = jnp.concatenate([wf_high, wf_low, wf_high], axis=0)
    rates = par_ref[:, FEAT : FEAT + 1]
    wait_for(first, 5, 6, 7, 8)
    filt = jnp.zeros((2 * OWN, 2 * FEAT), F32)
    pos = jnp.zeros((2 * FEAT, 2 * FEAT), F32)
    rate = jnp.zeros((OWN, 1), F32)
    for start in range(0, LENGTH, BLOCK):
        cut = slice(start, start + BLOCK)
        grad_taps = g_ref[:, cut]
        decay, steps = envelope(rates, start, BLOCK)
        high, low = split(grad_taps * decay)
        rate = rate + jnp.sum(grad_taps * taps_ref[:, cut] * (0.5 - rates * steps), axis=1, keepdims=True)
        filt = filt + mul(jnp.concatenate([high, low], axis=0), hid_ref[:, cut], ((1,), (1,)))
        inner = mul(wf, jnp.concatenate([high, high, low], axis=0), ((0,), (0,))) * cos_ref[:, cut]
        pos = pos + mul(feat_ref[:, cut], jnp.concatenate(split(inner), axis=0), ((1,), (1,)))
    filt = filt[:OWN, :FEAT] + filt[OWN:, :FEAT] + filt[:OWN, FEAT:]
    pos = pos[:FEAT, :FEAT] + pos[FEAT:, :FEAT] + pos[:FEAT, FEAT:]
    skip = jnp.sum(skip_ref[...], axis=1, keepdims=True)
    small_ref[...] = jnp.zeros((2, 2 * OWN, LANES), F32)
    for e, stat in enumerate((rate, skip)):
        small_ref[e, :OWN, :32] = filt[:, 32 * e : 32 * e + 32]
        small_ref[e, :OWN, 32:33] = stat
        small_ref[e, OWN:, :FEAT] = pos[32 * e : 32 * e + 16]
        small_ref[e, OWN:, FEAT:] = pos[32 * e + 16 : 32 * e + 32]
    save.wait()


def conv_kernel(
    act_hbm, peer_act_hbm, cot_hbm, peer_cot_hbm, ig_hbm, small_hbm, peer_small_hbm, out_hbm,
    act_ref, cot_ref, ig_ref, small_ref, pad_ref, part_ref, tile_ref, sems,
):
    core = lax.axis_index("batch") % 2
    half = pl.ds(pl.multiple_of(core * HALF, HALF), HALF)
    sources = [
        (cot_hbm.at[:, half], cot_ref.at[0]),
        (peer_cot_hbm.at[:, half], cot_ref.at[1]),
        (act_hbm, act_ref.at[0]),
        (ig_hbm, ig_ref),
        (small_hbm.at[core], small_ref.at[0]),
        (peer_act_hbm, act_ref.at[1]),
        (peer_small_hbm.at[core], small_ref.at[1]),
    ]
    loads = [pltpu.make_async_copy(a, b, sems.at[k]) for k, (a, b) in enumerate(sources)]
    for load in loads:
        load.start()
    pad_ref[:, :HALO, :] = jnp.zeros((2, HALO, HALF), F32)
    pad_ref[:, HALO + ROWS :, :] = jnp.zeros((2, 8, HALF), F32)
    wait_for(loads, 0, 1)
    pad_ref[:, HALO : HALO + ROWS, :] = cot_ref[...].astype(F32)
    wait_for(loads, 2, 5)
    copies = []
    for i in range(KERNEL):
        own = pad_ref[0, i : i + SPAN, :].astype(BF16)
        peer = pad_ref[1, i : i + SPAN, :].astype(BF16)
        part_ref[i] = (mul(act_ref[0], own) + mul(act_ref[1], peer)).astype(BF16)
        copy = pltpu.make_async_copy(part_ref.at[i], out_hbm.at[:, pl.ds(i * HALF, HALF)], sems.at[7 + i])
        copy.start()
        copies.append(copy)
        if i == 0:
            wait_for(loads, 3, 4, 6)
            tile_ref[:, :ROWS] = ig_ref[...]
            small = small_ref[0] + small_ref[1]
            high, low = split(small[:OWN])
            filt = high.astype(F32) + pltpu.roll(low.astype(F32), FEAT, 1)
            tile = jnp.concatenate([filt, small[OWN:]], axis=1).astype(BF16)
            for p in range(SHARDS):
                tile_ref[p * OWN : (p + 1) * OWN, ROWS:] = tile
            copy = pltpu.make_async_copy(tile_ref, out_hbm.at[:, pl.ds(CONV, ROWS + 2 * LANES)], sems.at[7 + KERNEL])
            copy.start()
            copies.append(copy)
    for copy in copies:
        copy.wait()


def mixed_kernel(act_ref, w_ref, _, out_ref, part_ref):
    act = jnp.transpose(act_ref[...].astype(F32)).astype(BF16)[HALO - 16 :]
    total = jnp.zeros((ROWS, WIDTH), F32)
    for i in range(KERNEL):
        part_ref[...] = mul(act, w_ref[i])
        total = total + part_ref[16 - i : 16 - i + ROWS, :]
    out_ref[...] = total.astype(BF16)


def gather_kernel(recv_ref, _, out_hbm, out_ref, sems):
    conv = jnp.sum(recv_ref[:, :, :CONV].astype(F32), axis=0).astype(BF16)
    for j in range(2):
        out_ref[16 * j : 16 * j + 16, :] = conv[:, j * WIDTH : (j + 1) * WIDTH]
    out_ref[32:48, :HALF] = conv[:, 2 * WIDTH :]
    base = CONV + ROWS
    both = recv_ref[:, :, base : base + LANES].astype(F32).reshape(WIDTH, LANES)
    filt = jnp.transpose(both + pltpu.roll(both, FEAT, 1))
    out_ref[48:80, :] = filt[:32].astype(BF16)
    pos = jnp.sum(recv_ref[:, :, base + LANES : base + 2 * LANES].astype(F32), axis=0)
    out_ref[32:48, HALF : HALF + LANES] = pos.astype(BF16)
    stat = filt[32:33]
    pieces = [stat[:, j * LANES : (j + 1) * LANES] for j in range(4)]
    stat = jnp.concatenate([*pieces, jnp.zeros((12, LANES), F32)], axis=0)
    out_ref[32:48, HALF + LANES :] = stat.astype(BF16)
    copies = [pltpu.make_async_copy(out_ref, out_hbm.at[z], sems.at[z]) for z in range(4)]
    for copy in copies:
        copy.start()
    for copy in copies:
        copy.wait()


def input_kernel(recv_ref, _, out_ref):
    out_ref[...] = jnp.transpose(recv_ref[:, :, CONV : CONV + ROWS].astype(F32).reshape(WIDTH, ROWS)).astype(BF16)


def final_kernel(recv_ref, _, out_ref):
    out_ref[...] = jnp.sum(recv_ref[...].astype(F32), axis=0) * (1.0 / math.sqrt(8 * LENGTH))


def join_kernel(core_ref, mine_ref, other_ref, conv_ref, pos_ref, filt_ref, rates_ref, skip_ref):
    def write(low, high):
        for e, part in enumerate((low, high)):
            for i in range(KERNEL):
                row, lane = 16 * (i // 2), HALF * (i % 2)
                conv_ref[i, :, e * HALF : (e + 1) * HALF] = part[row : row + 16, lane : lane + HALF]
            pos = part[32:48, HALF : HALF + LANES]
            pos_ref[32 * e : 32 * e + 16, :] = pos[:, :FEAT]
            pos_ref[32 * e + 16 : 32 * e + 32, :] = pos[:, FEAT:]
            filt_ref[32 * e : 32 * e + 32, :] = part[48:80, :]
            stat_ref = (rates_ref, skip_ref)[e]
            for j in range(4):
                stat_ref[:, j * LANES : (j + 1) * LANES] = part[32 + j : 33 + j, HALF + LANES :]

    @pl.when(core_ref[0] == 0)
    def _():
        write(mine_ref, other_ref)

    @pl.when(core_ref[0] == 1)
    def _():
        write(other_ref, mine_ref)


VMEM = pl.BlockSpec(memory_space=pltpu.VMEM)
SMEM = pl.BlockSpec(memory_space=pltpu.SMEM)
ANY = pl.BlockSpec(memory_space=pl.ANY)


def call(kernel, out_shape, args, scratch=(), flops=0, name=None, specs=None, out_specs=None, limit=60):
    single = not isinstance(out_shape, (list, tuple))
    outs = [out_shape] if single else out_shape
    moved = sum(math.prod(a.shape) * a.dtype.itemsize for a in (*args, *outs))
    return pl.pallas_call(
        kernel,
        out_shape=out_shape,
        in_specs=specs or [VMEM] * len(args),
        out_specs=out_specs or (VMEM if single else [VMEM] * len(outs)),
        scratch_shapes=list(scratch),
        compiler_params=pltpu.CompilerParams(vmem_limit_bytes=limit * 1024 * 1024),
        cost_estimate=pl.CostEstimate(flops=flops, bytes_accessed=moved, transcendentals=0),
        name=name,
    )(*args)


def shape(dims, kind=F32):
    return jax.ShapeDtypeStruct(dims, kind)


def regroup(blocks):
    return lax.all_to_all(blocks, "tm", split_axis=0, concat_axis=0, tiled=True)


def on_device(inputs, cotangent, w_pos, w_filt, log_rates, skip_gain, w_conv):
    core = lax.axis_index("batch") % 2
    swap = [(i, i ^ 1) for i in range(lax.axis_size("batch"))]
    signal, upstream = inputs[0], cotangent[0]
    w_taps = jnp.transpose(w_conv, (1, 0, 2))
    tabs = tuple(jnp.asarray(t) for t in transform_tables())
    feat = jnp.asarray(np.concatenate(feature_tables(), axis=0))

    message = call(
        prep_kernel,
        shape((WIDTH, ROWS + SPAN), BF16),
        (signal, upstream, w_taps),
        [
            pltpu.VMEM((ROWS, WIDTH), BF16),
            pltpu.VMEM((ROWS, WIDTH), BF16),
            pltpu.VMEM((KERNEL, WIDTH, WIDTH), BF16),
            pltpu.VMEM((HALO + ROWS + 8, WIDTH), F32),
            pltpu.VMEM((WIDTH, SPAN), F32),
            pltpu.VMEM((WIDTH, ROWS), BF16),
            pltpu.VMEM((WIDTH, SPAN), BF16),
            pltpu.SemaphoreType.DMA((4 + KERNEL,)),
        ],
        flops=2 * KERNEL * WIDTH * WIDTH * SPAN,
        name="prep",
        specs=[ANY] * 3,
        out_specs=ANY,
    )
    received = regroup(message.reshape(SHARDS, OWN, ROWS + SPAN))
    cot_peer = lax.ppermute(upstream, "batch", swap)
    received, cot_peer = lax.optimization_barrier((received, cot_peer))

    stack = pltpu.VMEM((STACK, LANES), F32)
    wide = pltpu.VMEM((STACK, 2 * LANES), BF16)
    saved = [pltpu.VMEM((2 * FEAT, LENGTH), BF16), pltpu.VMEM((FEAT, LENGTH), F32), pltpu.VMEM((OWN, LENGTH), F32)]
    flops = 2 * 3 * (2 * STACK * LANES * LANES + STACK * 4 * LANES * LANES)
    hidden, cosines, taps, tap_spec, par = call(
        taps_kernel,
        [
            shape((2 * FEAT, LENGTH), BF16),
            shape((FEAT, LENGTH)),
            shape((OWN, LENGTH)),
            shape((STACK, 2 * LANES)),
            shape((OWN, LANES)),
        ],
        (w_pos, w_filt, log_rates[None], skip_gain[None], feat, *tabs),
        [*saved, stack, wide, wide, pltpu.SemaphoreType.DMA((3,))],
        flops=flops * 2,
        name="taps",
        out_specs=[ANY, ANY, ANY, VMEM, VMEM],
    )
    act_message, grad_before, sig_spec, skip_part = call(
        forward_kernel,
        [
            shape((SHARDS, OWN, SPAN), BF16),
            shape((STACK, LANES)),
            shape((STACK, 2 * LANES)),
            shape((OWN, LANES)),
        ],
        (received, tap_spec, par, *tabs),
        [
            pltpu.VMEM((SHARDS, OWN, ROWS), BF16),
            pltpu.VMEM((SHARDS, OWN, SPAN), BF16),
            pltpu.VMEM((STACK, 2 * LANES), F32),
            pltpu.VMEM((STACK, 2 * LANES), F32),
            pltpu.VMEM((SHARDS, OWN, SPAN), BF16),
            stack,
            *[pltpu.VMEM(t.shape, t.dtype) for t in tabs],
            stack,
            stack,
            wide,
            wide,
            pltpu.VMEM((OWN, LANES), F32),
            pltpu.SemaphoreType.DMA((15,)),
        ],
        flops=flops * 2,
        name="forward",
        specs=[ANY] * 11,
        out_specs=[ANY, ANY, ANY, VMEM],
    )
    act = regroup(act_message).reshape(WIDTH, SPAN)
    ig_message, small = call(
        backward_kernel,
        [shape((SHARDS, OWN, ROWS), BF16), shape((2, 2 * OWN, LANES))],
        (grad_before, sig_spec, tap_spec, par, skip_part, hidden, cosines, feat, taps, *tabs),
        [
            stack,
            pltpu.VMEM((STACK, 2 * LANES), F32),
            pltpu.VMEM((STACK, 2 * LANES), F32),
            pltpu.VMEM((OWN, LANES), F32),
            pltpu.VMEM((OWN, LANES), F32),
            *saved[:2],
            saved[0],
            saved[2],
            *[pltpu.VMEM(t.shape, t.dtype) for t in tabs],
            pltpu.VMEM((SHARDS, OWN, ROWS), BF16),
            stack,
            wide,
            wide,
            pltpu.VMEM((OWN, LENGTH), F32),
            pltpu.SemaphoreType.DMA((18,)),
        ],
        flops=flops * 4,
        name="backward",
        specs=[ANY] * 17,
        out_specs=[ANY, VMEM],
    )
    act, ig_message, small = lax.optimization_barrier((act, ig_message, small))
    act_peer = lax.ppermute(act, "batch", swap)
    small_peer = lax.ppermute(small, "batch", swap)
    lanes = CONV + ROWS + 2 * LANES
    sums = call(
        conv_kernel,
        shape((WIDTH, lanes), BF16),
        (act, act_peer, upstream, cot_peer, ig_message.reshape(WIDTH, ROWS), small, small_peer),
        [
            pltpu.VMEM((2, WIDTH, SPAN), BF16),
            pltpu.VMEM((2, ROWS, HALF), BF16),
            pltpu.VMEM((WIDTH, ROWS), BF16),
            pltpu.VMEM((2, 2 * OWN, LANES), F32),
            pltpu.VMEM((2, HALO + ROWS + 8, HALF), F32),
            pltpu.VMEM((KERNEL, WIDTH, HALF), BF16),
            pltpu.VMEM((WIDTH, ROWS + 2 * LANES), BF16),
            pltpu.SemaphoreType.DMA((8 + KERNEL,)),
        ],
        flops=2 * KERNEL * WIDTH * HALF * 2 * SPAN,
        name="conv_grad",
        specs=[ANY] * 7,
        out_specs=ANY,
    )
    spread = regroup(sums.reshape(SHARDS, OWN, lanes))
    mixed = call(
        mixed_kernel,
        shape((ROWS, WIDTH), BF16),
        (act, w_taps, sums),
        [pltpu.VMEM((ROWS + 16, WIDTH), F32)],
        flops=2 * KERNEL * WIDTH * WIDTH * (ROWS + 16),
        name="mixed",
        specs=[VMEM, VMEM, ANY],
        limit=16,
    )
    payload = call(
        gather_kernel,
        shape((4, 80, WIDTH), BF16),
        (spread, mixed),
        [pltpu.VMEM((80, WIDTH), BF16), pltpu.SemaphoreType.DMA((4,))],
        name="gather",
        specs=[VMEM, ANY],
        out_specs=ANY,
        limit=12,
    )
    input_grad = call(input_kernel, shape((ROWS, WIDTH), BF16), (spread, payload), name="input", specs=[VMEM, ANY], limit=12)
    groups = [[2 * z + e for z in range(4)] for e in range(2)]
    parts = lax.all_to_all(
        payload,
        "batch",
        split_axis=0,
        concat_axis=0,
        tiled=True,
        axis_index_groups=groups,
    )
    total = call(final_kernel, shape((80, WIDTH)), (parts, input_grad), name="final", specs=[VMEM, ANY], limit=12)
    other = lax.ppermute(total, "batch", swap)
    conv_grad, pos_grad, filt_grad, rates_grad, skip_grad = call(
        join_kernel,
        [
            shape((KERNEL, OWN, WIDTH)),
            shape((FEAT, FEAT)),
            shape((FEAT, WIDTH)),
            shape((1, WIDTH)),
            shape((1, WIDTH)),
        ],
        (core.astype(jnp.int32)[None], total, other),
        name="join",
        specs=[SMEM, VMEM, VMEM],
        limit=12,
    )
    return (
        mixed[None],
        input_grad[None],
        jnp.transpose(conv_grad, (1, 0, 2)),
        pos_grad,
        filt_grad,
        rates_grad[0],
        skip_grad[0],
    )


def solution(mesh):
    in_specs = (P("batch", "tm", None), P("batch", "tm", None), P(), P(), P(), P(), P())
    out_specs = (P("batch", "tm", None), P("batch", "tm", None), P("tm", None, None), P(), P(), P(), P())
    return jax.shard_map(on_device, mesh=mesh, in_specs=in_specs, out_specs=out_specs, check_vma=False)
```

```python
import math

import jax
import jax.numpy as jnp
import ml_dtypes
import numpy as np
from jax import lax
from jax.experimental import pallas as pl
from jax.experimental.pallas import tpu as pltpu
from jax.sharding import PartitionSpec as P

F32 = jnp.float32
BF16 = jnp.bfloat16

SHARDS = 32
ROWS = 256
LENGTH = SHARDS * ROWS
WIDTH = 512
KERNEL = 5
FEAT = 64
OWN = WIDTH // SHARDS
LANES = 128
STEPS = LENGTH // LANES
STACK = STEPS * OWN
HALO = LANES
SPAN = ROWS + HALO
HALF = WIDTH // 2
EDGE = 16
CONV = KERNEL * HALF
BLOCK = 1024
SCALE = 1.0 / math.sqrt(8 * LENGTH)


def split_table(values):
    high = values.astype(ml_dtypes.bfloat16)
    low = (values - high.astype(np.float64)).astype(ml_dtypes.bfloat16)
    return high, low


def feature_tables():
    half = FEAT // 2
    factor = np.array([1 + i * i * LENGTH // (2 * half * half) for i in range(half)], dtype=np.int64)
    steps = np.arange(LENGTH, dtype=np.int64)
    angles = 2.0 * np.pi * ((factor[:, None] * steps[None, :]) % LENGTH) / LENGTH
    return split_table(np.concatenate([np.sin(angles), np.cos(angles)], axis=0))


def transform_tables():
    order = np.array([2 * p + h for h in range(2) for p in range(STEPS // 2)])
    k1 = np.arange(STEPS)
    alpha = np.pi * order[None, :] / STEPS / 2 - 2.0 * np.pi * ((order[None, :] * k1[:, None]) % STEPS) / STEPS
    outer = np.concatenate([np.cos(alpha), np.sin(alpha)], axis=0)
    outer_high, outer_low = split_table(outer)
    first = np.concatenate([outer_high, outer_low], axis=1)
    back_high, back_low = split_table(outer.T / LENGTH)
    last = np.concatenate([back_high, back_low, back_high], axis=1)
    b = np.arange(LANES)
    beta = np.pi * b[None, :] / (2 * LENGTH) - 2.0 * np.pi * ((b[None, :] * k1[:, None]) % LENGTH) / LENGTH
    twist_cos = np.cos(beta).astype(np.float32)
    twist_sin = np.sin(beta).astype(np.float32)
    gamma = 2.0 * np.pi * ((b[:, None] * b[None, :]) % LANES) / LANES
    cos, sin = np.cos(gamma), np.sin(gamma)
    ahead = split_table(np.block([[cos, -sin], [sin, cos]]))
    behind = split_table(np.block([[cos, sin], [-sin, cos]]))
    return (first, last, twist_cos, twist_sin, *ahead, *behind)


def split(values):
    high = values.astype(BF16)
    return high, (values - high.astype(F32)).astype(BF16)


def mul(left, right, dims=((1,), (0,))):
    return lax.dot_general(left, right, (dims, ((), ())), preferred_element_type=F32)


def mul3(left, right, dims=((1,), (0,))):
    lh, ll = left
    rh, rl = right
    return mul(lh, rh, dims) + mul(ll, rh, dims) + mul(lh, rl, dims)


def wait_for(loads, *which):
    for k in which:
        if loads is not None:
            loads[k].wait()


def spectrum(stack_ref, high_ref, low_ref, tabs, loads=None):
    first, _, tc_ref, ts_ref, ahead_high, ahead_low, _, _ = tabs
    wait_for(loads, 0, 2, 3)
    tc, ts = tc_ref[...], ts_ref[...]
    for c in range(0, OWN, 2):
        pair = [stack_ref[pl.ds(c + k, STEPS, stride=OWN), :] for k in range(2)]
        wide = jnp.concatenate(pair, axis=1).astype(BF16)
        u = mul(first[...], jnp.concatenate([wide, wide], axis=0))
        for k in range(2):
            ur = u[:STEPS, k * LANES : (k + 1) * LANES]
            ui = u[STEPS:, k * LANES : (k + 1) * LANES]
            v = jnp.concatenate([ur * tc - ui * ts, ur * ts + ui * tc], axis=1)
            high, low = split(v)
            high_ref[(c + k) * STEPS : (c + k + 1) * STEPS, :] = high
            low_ref[(c + k) * STEPS : (c + k + 1) * STEPS, :] = low
    wait_for(loads, 4, 5)
    return mul3((high_ref[...], low_ref[...]), (ahead_high[...], ahead_low[...]))


def from_spectrum(values, stack_ref, tabs, loads=None):
    _, last, tc_ref, ts_ref, _, _, behind_high, behind_low = tabs
    wait_for(loads, 6, 7, 1)
    tc, ts = tc_ref[...], ts_ref[...]
    q = mul3(split(values), (behind_high[...], behind_low[...]))
    for c in range(0, OWN, 2):
        pair = []
        for k in range(2):
            rows = q[(c + k) * STEPS : (c + k + 1) * STEPS]
            qr, qi = rows[:, :LANES], rows[:, LANES:]
            pair.append(jnp.concatenate([qr * tc + qi * ts, qi * tc - qr * ts], axis=0))
        high, low = split(jnp.concatenate(pair, axis=1))
        y = mul(last[...], jnp.concatenate([high, high, low], axis=0))
        for k in range(2):
            stack_ref[pl.ds(c + k, STEPS, stride=OWN), :] = y[:, k * LANES : (k + 1) * LANES]


def product(left, right, conjugate):
    lr, li = left[:, :LANES], left[:, LANES:]
    rr, ri = right[:, :LANES], right[:, LANES:]
    if conjugate:
        return jnp.concatenate([lr * rr + li * ri, lr * ri - li * rr], axis=1)
    return jnp.concatenate([lr * rr - li * ri, lr * ri + li * rr], axis=1)


def sin_cos(x):
    turns = jnp.floor(x * (2.0 / math.pi) + 0.5)
    r = x - turns * 1.5703125
    r = r - turns * 4.837512969970703125e-4
    r = r - turns * 7.549789948768648e-8
    z = r * r
    s = r + r * z * (-1.6666654611e-1 + z * (8.3321608736e-3 - z * 1.9515295891e-4))
    c = 1.0 - 0.5 * z + z * z * (4.166664568298827e-2 + z * (-1.388731625493765e-3 + z * 2.443315711809948e-5))
    quad = turns.astype(jnp.int32)
    odd = (quad & 1) == 1
    sin = jnp.where(odd, c, s)
    cos = jnp.where(odd, s, c)
    sin = jnp.where((quad & 2) == 2, -sin, sin)
    cos = jnp.where(((quad + 1) & 2) == 2, -cos, cos)
    return sin, cos


def envelope(rates, start, size):
    steps = (start + lax.broadcasted_iota(jnp.int32, (OWN, size), 1)).astype(F32)
    return jnp.sqrt(rates) * jnp.exp(-steps * rates), steps


def prep_kernel(x_hbm, cot_hbm, w_hbm, out_hbm, x_ref, cot_ref, w_ref, pad_ref, sum_ref, xt_ref, ga_ref, sems):
    x_copy = pltpu.make_async_copy(x_hbm, x_ref, sems.at[0])
    x_copy.start()
    cot_copy = pltpu.make_async_copy(cot_hbm, cot_ref, sems.at[1])
    cot_copy.start()
    w_copies = [pltpu.make_async_copy(w_hbm.at[i], w_ref.at[i], sems.at[2 + i]) for i in range(KERNEL)]
    for copy in w_copies:
        copy.start()
    pad_ref[:EDGE, :] = jnp.zeros((EDGE, WIDTH), F32)
    pad_ref[EDGE + ROWS :, :] = jnp.zeros((8, WIDTH), F32)
    x_copy.wait()
    xt_ref[...] = jnp.transpose(x_ref[...].astype(F32)).astype(BF16)
    x_out = pltpu.make_async_copy(xt_ref, out_hbm.at[:, pl.ds(0, ROWS)], sems.at[2 + KERNEL])
    x_out.start()
    cot_copy.wait()
    pad_ref[EDGE : EDGE + ROWS, :] = cot_ref[...].astype(F32)
    for i in range(KERNEL):
        shifted = pad_ref[i : i + EDGE + ROWS, :].astype(BF16)
        w_copies[i].wait()
        part = mul(shifted, w_ref[i], ((1,), (1,)))
        if i == 0:
            sum_ref[HALO - EDGE :, :] = part
        else:
            sum_ref[HALO - EDGE :, :] += part
    sum_ref[: HALO - EDGE, :] = jnp.zeros((HALO - EDGE, WIDTH), F32)
    ga_ref[...] = jnp.transpose(sum_ref[...]).astype(BF16)
    ga_out = pltpu.make_async_copy(ga_ref, out_hbm.at[:, pl.ds(ROWS, SPAN)], sems.at[3 + KERNEL])
    ga_out.start()
    x_out.wait()
    ga_out.wait()


def taps_kernel(wp_ref, wf_ref, lr_ref, gain_ref, feat_ref, *rest):
    tabs = rest[:8]
    hid_out, cos_out, taps_out, spec_out, par_out = rest[8:13]
    hid_ref, cos_ref, taps_ref, spec_ref, par_ref, stack_ref, vh_ref, vl_ref, sems = rest[13:]
    first = lax.axis_index("tm") * OWN
    lane = lax.broadcasted_iota(jnp.int32, (OWN, WIDTH), 1)
    chosen = lane == first + lax.broadcasted_iota(jnp.int32, (OWN, WIDTH), 0)
    wf_own = lax.dot_general(
        chosen.astype(F32),
        wf_ref[...],
        (((1,), (1,)), ((), ())),
        precision=lax.Precision.HIGHEST,
        preferred_element_type=F32,
    )
    rates = jnp.exp(jnp.sum(jnp.where(chosen, lr_ref[...], 0.0), axis=1, keepdims=True))
    gain = jnp.sum(jnp.where(chosen, gain_ref[...], 0.0), axis=1, keepdims=True)
    spot = lax.broadcasted_iota(jnp.int32, (OWN, LANES), 1)
    par_ref[...] = jnp.where(spot == FEAT, rates, jnp.where(spot == FEAT + 1, gain, 0.0))
    par_ref[:, :FEAT] = wf_own
    wp_high, wp_low = split(wp_ref[...])
    wp = jnp.concatenate([wp_high, wp_low, wp_high], axis=0)
    wf_high, wf_low = split(wf_own)
    for start in range(0, LENGTH, BLOCK):
        cut = slice(start, start + BLOCK)
        feat = feat_ref[:, cut]
        sin, cos = sin_cos(mul(wp, jnp.concatenate([feat[:FEAT], feat], axis=0), ((0,), (0,))))
        high, low = split(sin)
        hid_ref[:FEAT, cut] = high
        hid_ref[FEAT:, cut] = low
        cos_ref[:, cut] = cos
        decay, _ = envelope(rates, start, BLOCK)
        taps = mul3((wf_high, wf_low), (high, low)) * decay
        taps_ref[:, cut] = taps
        rounded = taps.astype(BF16).astype(F32)
        for j in range(BLOCK // LANES):
            a = start // LANES + j
            row = ((a % 2) * SHARDS + a // 2) * OWN
            stack_ref[row : row + OWN, :] = rounded[:, j * LANES : (j + 1) * LANES]
    saves = [
        pltpu.make_async_copy(source, target, sems.at[k])
        for k, (source, target) in enumerate(((hid_ref, hid_out), (cos_ref, cos_out), (taps_ref, taps_out), (par_ref, par_out)))
    ]
    for save in saves:
        save.start()
    spec_ref[...] = spectrum(stack_ref, vh_ref, vl_ref, tabs)
    saves.append(pltpu.make_async_copy(spec_ref, spec_out, sems.at[4]))
    saves[-1].start()
    for save in saves:
        save.wait()


def gelu_parts(before):
    root = math.sqrt(2.0 / math.pi)
    square = before * before
    th = jnp.tanh(root * (before + 0.044715 * square * before))
    half_cdf = 0.5 * (1.0 + th)
    slope = half_cdf + 0.5 * before * (1.0 - th * th) * (root * (1.0 + 3.0 * 0.044715 * square))
    return before * half_cdf, slope


def forward_kernel(recv_hbm, tspec_hbm, par_hbm, *rest):
    tabs_hbm = rest[:8]
    act_hbm, before_hbm, xspec_hbm = rest[8:11]
    xin_ref, tspec_ref, spec_ref, act_ref = rest[11:15]
    tabs = rest[15:23]
    x_ref, y_ref, vh_ref, vl_ref, par_ref, sems = rest[23:]
    x_load = pltpu.make_async_copy(recv_hbm.at[:, :, pl.ds(0, ROWS)], xin_ref, sems.at[0])
    x_load.start()
    loads = [pltpu.make_async_copy(tabs_hbm[k], tabs[k], sems.at[1 + k]) for k in range(8)]
    for k in (0, 2, 3, 4, 5, 6, 7, 1):
        loads[k].start()
    tspec_load = pltpu.make_async_copy(tspec_hbm, tspec_ref, sems.at[9])
    tspec_load.start()
    par_load = pltpu.make_async_copy(par_hbm, par_ref, sems.at[10])
    par_load.start()
    x_load.wait()
    for h in range(2):
        part = xin_ref[:, :, h * LANES : (h + 1) * LANES].astype(F32)
        x_ref[h * STACK // 2 : (h + 1) * STACK // 2, :] = part.reshape(STACK // 2, LANES)
    spec = spectrum(x_ref, vh_ref, vl_ref, tabs, loads)
    spec_ref[...] = spec
    spec_save = pltpu.make_async_copy(spec_ref, xspec_hbm, sems.at[11])
    spec_save.start()
    tspec_load.wait()
    from_spectrum(product(tspec_ref[...], spec, False), y_ref, tabs, loads)
    par_load.wait()
    gain = par_ref[:, FEAT + 1 : FEAT + 2][None]
    before = y_ref[...].reshape(STEPS, OWN, LANES) + gain * x_ref[...].reshape(STEPS, OWN, LANES)
    y_ref[...] = before.reshape(STACK, LANES)
    before_save = pltpu.make_async_copy(y_ref, before_hbm, sems.at[12])
    before_save.start()
    active = gelu_parts(before)[0].astype(BF16)
    act_ref[:, :, HALO : HALO + LANES] = active[:SHARDS]
    act_ref[:, :, HALO + LANES :] = active[SHARDS:]
    act_ref[:, :, :HALO] = jnp.concatenate([jnp.zeros((1, OWN, LANES), BF16), active[SHARDS:-1]], axis=0)
    act_save = pltpu.make_async_copy(act_ref, act_hbm, sems.at[13])
    act_save.start()
    spec_save.wait()
    before_save.wait()
    act_save.wait()


def backward_kernel(*rest):
    arrays_hbm, tabs_hbm = rest[:9], rest[9:17]
    ig_hbm, small_hbm = rest[17:19]
    arrays, tabs = rest[19:28], rest[28:36]
    recv_ref, before_ref, xspec_ref, tspec_ref, par_ref, hid_ref, cos_ref, feat_ref, taps_ref = arrays
    gb_ref, ig_ref, small_ref, y_ref, vh_ref, vl_ref, g_ref, sems = rest[36:]
    first = [pltpu.make_async_copy(arrays_hbm[k], arrays[k], sems.at[k]) for k in range(9)]
    table = [pltpu.make_async_copy(tabs_hbm[k], tabs[k], sems.at[9 + k]) for k in range(8)]
    for copy in (*first[:2], *table, *first[2:]):
        copy.start()
    wait_for(first, 0, 1)
    early = recv_ref[:, :, ROWS + HALO : ROWS + HALO + LANES].astype(F32)
    late = recv_ref[:, :, ROWS + HALO + LANES :].astype(F32)
    edge = recv_ref[:, :, ROWS : ROWS + HALO].astype(F32)
    edge = jnp.concatenate([edge[1:], jnp.zeros((1, OWN, LANES), F32)], axis=0)
    grad_active = jnp.concatenate([early, late + edge], axis=0)
    slope = gelu_parts(before_ref[...])[1].reshape(STEPS, OWN, LANES)
    grad = (grad_active * slope).astype(BF16).astype(F32)
    gb_ref[...] = grad.reshape(STACK, LANES)
    x = jnp.concatenate([recv_ref[:, :, :LANES].astype(F32), recv_ref[:, :, LANES:ROWS].astype(F32)], axis=0)
    skip = jnp.sum(jnp.sum(grad * x, axis=0), axis=1, keepdims=True)
    spec = spectrum(gb_ref, vh_ref, vl_ref, tabs, table)
    wait_for(first, 2, 3, 4)
    from_spectrum(product(tspec_ref[...], spec, True), y_ref, tabs, table)
    gain = par_ref[:, FEAT + 1 : FEAT + 2][None]
    result = (y_ref[...].reshape(STEPS, OWN, LANES) + gain * grad).astype(BF16)
    ig_ref[:, :, :LANES] = result[:SHARDS]
    ig_ref[:, :, LANES:] = result[SHARDS:]
    save = pltpu.make_async_copy(ig_ref, ig_hbm, sems.at[17])
    save.start()
    from_spectrum(product(xspec_ref[...], spec, True), y_ref, tabs)
    for a in range(STEPS):
        row = ((a % 2) * SHARDS + a // 2) * OWN
        g_ref[:, a * LANES : (a + 1) * LANES] = y_ref[row : row + OWN, :]
    wf_high, wf_low = split(par_ref[:, :FEAT])
    wf = jnp.concatenate([wf_high, wf_low, wf_high], axis=0)
    rates = par_ref[:, FEAT : FEAT + 1]
    wait_for(first, 5, 6, 7, 8)
    filt = jnp.zeros((2 * OWN, 2 * FEAT), F32)
    pos = jnp.zeros((2 * FEAT, 2 * FEAT), F32)
    rate = jnp.zeros((OWN, 1), F32)
    for start in range(0, LENGTH, BLOCK):
        cut = slice(start, start + BLOCK)
        grad_taps = g_ref[:, cut]
        decay, steps = envelope(rates, start, BLOCK)
        high, low = split(grad_taps * decay)
        rate = rate + jnp.sum(grad_taps * taps_ref[:, cut] * (0.5 - rates * steps), axis=1, keepdims=True)
        filt = filt + mul(jnp.concatenate([high, low], axis=0), hid_ref[:, cut], ((1,), (1,)))
        inner = mul(wf, jnp.concatenate([high, high, low], axis=0), ((0,), (0,))) * cos_ref[:, cut]
        pos = pos + mul(feat_ref[:, cut], jnp.concatenate(split(inner), axis=0), ((1,), (1,)))
    filt = filt[:OWN, :FEAT] + filt[OWN:, :FEAT] + filt[:OWN, FEAT:]
    pos = pos[:FEAT, :FEAT] + pos[FEAT:, :FEAT] + pos[:FEAT, FEAT:]
    small_ref[...] = jnp.zeros((2, 2 * OWN, LANES), F32)
    for e, stat in enumerate((rate, skip)):
        small_ref[e, :OWN, :32] = filt[:, 32 * e : 32 * e + 32]
        small_ref[e, :OWN, 32:33] = stat
        small_ref[e, OWN:, :FEAT] = pos[32 * e : 32 * e + 16]
        small_ref[e, OWN:, FEAT:] = pos[32 * e + 16 : 32 * e + 32]
    small_save = pltpu.make_async_copy(small_ref, small_hbm, sems.at[18])
    small_save.start()
    save.wait()
    small_save.wait()


def conv_kernel(
    act_hbm, peer_act_hbm, cot_hbm, peer_cot_hbm, ig_hbm, small_hbm, peer_small_hbm, out_hbm,
    act_ref, cot_ref, ig_ref, small_ref, pad_ref, part_ref, tile_ref, sems,
):
    core = lax.axis_index("batch") % 2
    half = pl.ds(pl.multiple_of(core * HALF, HALF), HALF)
    sources = [
        (cot_hbm.at[:, half], cot_ref.at[0]),
        (peer_cot_hbm.at[:, half], cot_ref.at[1]),
        (act_hbm, act_ref.at[0]),
        (peer_act_hbm, act_ref.at[1]),
        (ig_hbm, ig_ref),
        (small_hbm.at[core], small_ref.at[0]),
        (peer_small_hbm.at[core], small_ref.at[1]),
    ]
    loads = [pltpu.make_async_copy(a, b, sems.at[k]) for k, (a, b) in enumerate(sources)]
    for load in loads:
        load.start()
    pad_ref[:, :HALO, :] = jnp.zeros((2, HALO, HALF), F32)
    pad_ref[:, HALO + ROWS :, :] = jnp.zeros((2, 8, HALF), F32)
    wait_for(loads, 0, 1)
    pad_ref[:, HALO : HALO + ROWS, :] = cot_ref[...].astype(F32)
    wait_for(loads, 2, 3)
    copies = []
    for i in range(KERNEL):
        own = pad_ref[0, i : i + SPAN, :].astype(BF16)
        peer = pad_ref[1, i : i + SPAN, :].astype(BF16)
        part_ref[i] = (mul(act_ref[0], own) + mul(act_ref[1], peer)).astype(BF16)
        copies.append(pltpu.make_async_copy(part_ref.at[i], out_hbm.at[:, pl.ds(i * HALF, HALF)], sems.at[9 + i]))
        copies[-1].start()
        if i == 0:
            wait_for(loads, 4, 5, 6)
            tile_ref[:, :ROWS] = ig_ref[...]
            small = small_ref[0] + small_ref[1]
            high, low = split(small[:OWN])
            filt = high.astype(F32) + pltpu.roll(low.astype(F32), FEAT, 1)
            tile = jnp.concatenate([filt, small[OWN:]], axis=1).astype(BF16)
            for p in range(SHARDS):
                tile_ref[p * OWN : (p + 1) * OWN, ROWS:] = tile
            target = out_hbm.at[:, pl.ds(CONV, ROWS + 2 * LANES)]
            copies.append(pltpu.make_async_copy(tile_ref, target, sems.at[9 + KERNEL]))
            copies[-1].start()
    for copy in copies:
        copy.wait()


def mixed_kernel(act_hbm, w_hbm, _, out_hbm, act_ref, w_ref, part_ref, out_ref, sems):
    loads = [pltpu.make_async_copy(w_hbm.at[i], w_ref.at[i], sems.at[i]) for i in range(KERNEL)]
    loads.append(pltpu.make_async_copy(act_hbm, act_ref, sems.at[KERNEL]))
    for load in loads:
        load.start()
    wait_for(loads, KERNEL)
    act = jnp.transpose(act_ref[...].astype(F32)).astype(BF16)[HALO - EDGE :]
    total = jnp.zeros((ROWS, WIDTH), F32)
    for i in range(KERNEL):
        wait_for(loads, i)
        part_ref[...] = mul(act, w_ref[i])
        total = total + part_ref[EDGE - i : EDGE - i + ROWS, :]
    out_ref[...] = total.astype(BF16)
    save = pltpu.make_async_copy(out_ref, out_hbm, sems.at[KERNEL + 1])
    save.start()
    save.wait()


def fold(block):
    return jnp.concatenate([block[:8], block[8:]], axis=1)


def gather_kernel(recv_ref, out_ref):
    conv = jnp.sum(recv_ref[:, :, :CONV].astype(F32), axis=0)
    blocks = [conv[:, :WIDTH], conv[:, WIDTH : 2 * WIDTH], fold(conv[:, 2 * WIDTH :])]
    base = CONV + ROWS
    both = recv_ref[:, :, base : base + LANES].astype(F32).reshape(WIDTH, LANES)
    filt = jnp.transpose(both + pltpu.roll(both, FEAT, 1))
    pos = jnp.sum(recv_ref[:, :, base + LANES : base + 2 * LANES].astype(F32), axis=0)
    stat = filt[32:33]
    pieces = [stat[:, j * LANES : (j + 1) * LANES] for j in range(4)]
    stat = jnp.concatenate([*pieces, jnp.zeros((4, LANES), F32)], axis=0)
    last = jnp.concatenate([fold(pos), stat, jnp.zeros((8, LANES), F32)], axis=1)
    out_ref[...] = jnp.concatenate([*blocks, filt[:32], last], axis=0).astype(BF16)


def final_kernel(own_ref, first_ref, second_ref, third_ref, out_ref):
    across = own_ref[...].astype(F32) + second_ref[...].astype(F32)
    beside = first_ref[...].astype(F32) + third_ref[...].astype(F32)
    out_ref[...] = (across + beside) * SCALE


def input_kernel(recv_ref, out_hbm, out_ref, sem):
    out_ref[...] = jnp.transpose(recv_ref[:, :, CONV : CONV + ROWS].astype(F32).reshape(WIDTH, ROWS)).astype(BF16)
    save = pltpu.make_async_copy(out_ref, out_hbm, sem)
    save.start()
    save.wait()


def join_kernel(mine_ref, other_ref, conv_ref, pos_ref, filt_ref, rates_ref, skip_ref):
    core = lax.axis_index("batch") % 2

    def write(low, high):
        for e, part in enumerate((low, high)):
            lanes = slice(e * HALF, (e + 1) * HALF)
            for i in range(KERNEL - 1):
                row, lane = 16 * (i // 2), HALF * (i % 2)
                conv_ref[i, :, lanes] = part[row : row + 16, lane : lane + HALF]
            conv_ref[KERNEL - 1, :8, lanes] = part[32:40, :HALF]
            conv_ref[KERNEL - 1, 8:, lanes] = part[32:40, HALF:]
            filt_ref[32 * e : 32 * e + 32, :] = part[40:72, :]
            for j in range(2):
                pos = part[72:80, j * LANES : (j + 1) * LANES]
                pos_ref[32 * e + 8 * j : 32 * e + 8 * j + 8, :] = pos[:, :FEAT]
                pos_ref[32 * e + 16 + 8 * j : 32 * e + 24 + 8 * j, :] = pos[:, FEAT:]
            for j in range(4):
                (rates_ref, skip_ref)[e][:, j * LANES : (j + 1) * LANES] = part[72 + j : 73 + j, HALF : HALF + LANES]

    @pl.when(core == 0)
    def _():
        write(mine_ref, other_ref)

    @pl.when(core == 1)
    def _():
        write(other_ref, mine_ref)


VMEM = pl.BlockSpec(memory_space=pltpu.VMEM)
HBM = pl.BlockSpec(memory_space=pltpu.HBM)


def call(kernel, out_shape, args, scratch=(), flops=0, name=None, specs=None, out_specs=None, limit=60):
    single = not isinstance(out_shape, (list, tuple))
    outs = [out_shape] if single else out_shape
    moved = sum(math.prod(a.shape) * a.dtype.itemsize for a in (*args, *outs))
    return pl.pallas_call(
        kernel,
        out_shape=out_shape,
        in_specs=specs or [VMEM] * len(args),
        out_specs=out_specs or (VMEM if single else [VMEM] * len(outs)),
        scratch_shapes=list(scratch),
        compiler_params=pltpu.CompilerParams(vmem_limit_bytes=limit * 1024 * 1024),
        cost_estimate=pl.CostEstimate(flops=flops, bytes_accessed=moved, transcendentals=0),
        name=name,
    )(*args)


def shape(dims, kind=F32):
    return jax.ShapeDtypeStruct(dims, kind)


def regroup(blocks):
    return lax.all_to_all(blocks, "tm", split_axis=0, concat_axis=0, tiled=True)


def on_device(inputs, cotangent, w_pos, w_filt, log_rates, skip_gain, w_conv):
    swap = [(i, i ^ 1) for i in range(lax.axis_size("batch"))]
    signal, upstream = inputs[0], cotangent[0]
    w_taps = jnp.transpose(w_conv, (1, 0, 2))
    tabs = tuple(jnp.asarray(t) for t in transform_tables())
    feat = jnp.asarray(np.concatenate(feature_tables(), axis=0))

    message = call(
        prep_kernel,
        shape((WIDTH, ROWS + SPAN), BF16),
        (signal, upstream, w_taps),
        [
            pltpu.VMEM((ROWS, WIDTH), BF16),
            pltpu.VMEM((ROWS, WIDTH), BF16),
            pltpu.VMEM((KERNEL, WIDTH, WIDTH), BF16),
            pltpu.VMEM((EDGE + ROWS + 8, WIDTH), F32),
            pltpu.VMEM((SPAN, WIDTH), F32),
            pltpu.VMEM((WIDTH, ROWS), BF16),
            pltpu.VMEM((WIDTH, SPAN), BF16),
            pltpu.SemaphoreType.DMA((4 + KERNEL,)),
        ],
        flops=2 * KERNEL * WIDTH * WIDTH * (ROWS + EDGE),
        name="prep",
        specs=[HBM] * 3,
        out_specs=HBM,
    )
    received = regroup(message.reshape(SHARDS, OWN, ROWS + SPAN))
    cot_peer = lax.ppermute(upstream, "batch", swap)
    received, cot_peer = lax.optimization_barrier((received, cot_peer))

    stack = pltpu.VMEM((STACK, LANES), F32)
    wide = pltpu.VMEM((STACK, 2 * LANES), BF16)
    saved = [pltpu.VMEM((2 * FEAT, LENGTH), BF16), pltpu.VMEM((FEAT, LENGTH), F32), pltpu.VMEM((OWN, LENGTH), F32)]
    flops = 2 * 3 * (2 * STACK * LANES * LANES + STACK * 4 * LANES * LANES)
    hidden, cosines, taps, tap_spec, par = call(
        taps_kernel,
        [
            shape((2 * FEAT, LENGTH), BF16),
            shape((FEAT, LENGTH)),
            shape((OWN, LENGTH)),
            shape((STACK, 2 * LANES)),
            shape((OWN, LANES)),
        ],
        (w_pos, w_filt, log_rates[None], skip_gain[None], feat, *tabs),
        [*saved, pltpu.VMEM((STACK, 2 * LANES), F32), pltpu.VMEM((OWN, LANES), F32), stack, wide, wide, pltpu.SemaphoreType.DMA((5,))],
        flops=flops * 2,
        name="taps",
        out_specs=[HBM] * 5,
    )
    act_message, before, sig_spec = call(
        forward_kernel,
        [shape((SHARDS, OWN, SPAN), BF16), shape((STACK, LANES)), shape((STACK, 2 * LANES))],
        (received, tap_spec, par, *tabs),
        [
            pltpu.VMEM((SHARDS, OWN, ROWS), BF16),
            pltpu.VMEM((STACK, 2 * LANES), F32),
            pltpu.VMEM((STACK, 2 * LANES), F32),
            pltpu.VMEM((SHARDS, OWN, SPAN), BF16),
            *[pltpu.VMEM(t.shape, t.dtype) for t in tabs],
            stack,
            stack,
            wide,
            wide,
            pltpu.VMEM((OWN, LANES), F32),
            pltpu.SemaphoreType.DMA((14,)),
        ],
        flops=flops * 2,
        name="forward",
        specs=[HBM] * 11,
        out_specs=[HBM] * 3,
    )
    act = regroup(act_message).reshape(WIDTH, SPAN)
    ig_message, small = call(
        backward_kernel,
        [shape((SHARDS, OWN, ROWS), BF16), shape((2, 2 * OWN, LANES))],
        (received, before, sig_spec, tap_spec, par, hidden, cosines, feat, taps, *tabs),
        [
            pltpu.VMEM((SHARDS, OWN, ROWS + SPAN), BF16),
            stack,
            pltpu.VMEM((STACK, 2 * LANES), F32),
            pltpu.VMEM((STACK, 2 * LANES), F32),
            pltpu.VMEM((OWN, LANES), F32),
            *saved[:2],
            saved[0],
            saved[2],
            *[pltpu.VMEM(t.shape, t.dtype) for t in tabs],
            stack,
            pltpu.VMEM((SHARDS, OWN, ROWS), BF16),
            pltpu.VMEM((2, 2 * OWN, LANES), F32),
            stack,
            wide,
            wide,
            pltpu.VMEM((OWN, LENGTH), F32),
            pltpu.SemaphoreType.DMA((19,)),
        ],
        flops=flops * 4,
        name="backward",
        specs=[HBM] * 17,
        out_specs=[HBM] * 2,
    )
    act, ig_message, small = lax.optimization_barrier((act, ig_message, small))
    act_peer = lax.ppermute(act, "batch", swap)
    small_peer = lax.ppermute(small, "batch", swap)
    lanes = CONV + ROWS + 2 * LANES
    sums = call(
        conv_kernel,
        shape((WIDTH, lanes), BF16),
        (act, act_peer, upstream, cot_peer, ig_message.reshape(WIDTH, ROWS), small, small_peer),
        [
            pltpu.VMEM((2, WIDTH, SPAN), BF16),
            pltpu.VMEM((2, ROWS, HALF), BF16),
            pltpu.VMEM((WIDTH, ROWS), BF16),
            pltpu.VMEM((2, 2 * OWN, LANES), F32),
            pltpu.VMEM((2, HALO + ROWS + 8, HALF), F32),
            pltpu.VMEM((KERNEL, WIDTH, HALF), BF16),
            pltpu.VMEM((WIDTH, ROWS + 2 * LANES), BF16),
            pltpu.SemaphoreType.DMA((10 + KERNEL,)),
        ],
        flops=2 * KERNEL * WIDTH * HALF * 2 * ROWS,
        name="conv_grad",
        specs=[HBM] * 7,
        out_specs=HBM,
    )
    spread = regroup(sums.reshape(SHARDS, OWN, lanes))
    mixed = call(
        mixed_kernel,
        shape((ROWS, WIDTH), BF16),
        (act, w_taps, sums),
        [
            pltpu.VMEM((WIDTH, SPAN), BF16),
            pltpu.VMEM((KERNEL, WIDTH, WIDTH), BF16),
            pltpu.VMEM((ROWS + EDGE, WIDTH), F32),
            pltpu.VMEM((ROWS, WIDTH), BF16),
            pltpu.SemaphoreType.DMA((2 + KERNEL,)),
        ],
        flops=2 * KERNEL * WIDTH * WIDTH * (ROWS + EDGE),
        name="mixed",
        specs=[HBM] * 3,
        out_specs=HBM,
    )
    spread, mixed = lax.optimization_barrier((spread, mixed))
    payload = call(gather_kernel, shape((80, WIDTH), BF16), (spread,), name="gather", limit=12)
    rounds = [[(i, (i + 2 * d) % 8) for i in range(8)] for d in range(1, 4)]
    others = [lax.ppermute(payload, "batch", route) for route in rounds]
    spread, payload = lax.optimization_barrier((spread, payload))
    input_grad = call(
        input_kernel,
        shape((ROWS, WIDTH), BF16),
        (spread,),
        [pltpu.VMEM((ROWS, WIDTH), BF16), pltpu.SemaphoreType.DMA],
        name="input",
        out_specs=HBM,
        limit=12,
    )
    payload, input_grad = lax.optimization_barrier((payload, input_grad))
    mine = call(final_kernel, shape((80, WIDTH)), (payload, *others), name="final", limit=12)
    other = lax.ppermute(mine, "batch", swap)
    conv_grad, pos_grad, filt_grad, rates_grad, skip_grad = call(
        join_kernel,
        [
            shape((KERNEL, OWN, WIDTH)),
            shape((FEAT, FEAT)),
            shape((FEAT, WIDTH)),
            shape((1, WIDTH)),
            shape((1, WIDTH)),
        ],
        (mine, other),
        name="join",
        limit=12,
    )
    return (
        mixed[None],
        input_grad[None],
        jnp.transpose(conv_grad, (1, 0, 2)),
        pos_grad,
        filt_grad,
        rates_grad[0],
        skip_grad[0],
    )


def solution(mesh):
    in_specs = (P("batch", "tm", None), P("batch", "tm", None), P(), P(), P(), P(), P())
    out_specs = (P("batch", "tm", None), P("batch", "tm", None), P("tm", None, None), P(), P(), P(), P())
    return jax.shard_map(on_device, mesh=mesh, in_specs=in_specs, out_specs=out_specs, check_vma=False)
```

```python
import math

import jax
import jax.numpy as jnp
import ml_dtypes
import numpy as np
from jax import lax
from jax.experimental import pallas as pl
from jax.experimental.pallas import tpu as pltpu
from jax.sharding import PartitionSpec as P

F32 = jnp.float32
BF16 = jnp.bfloat16

SHARDS = 32
ROWS = 256
LENGTH = SHARDS * ROWS
WIDTH = 512
KERNEL = 5
FEAT = 64
OWN = WIDTH // SHARDS
LANES = 128
STEPS = LENGTH // LANES
STACK = STEPS * OWN
HALO = LANES
SPAN = ROWS + HALO
HALF = WIDTH // 2
EDGE = 16
CONV = KERNEL * HALF
BLOCK = 1024
SCALE = 1.0 / math.sqrt(8 * LENGTH)


def split_table(values):
    high = values.astype(ml_dtypes.bfloat16)
    low = (values - high.astype(np.float64)).astype(ml_dtypes.bfloat16)
    return high, low


def feature_tables():
    half = FEAT // 2
    factor = np.array([1 + i * i * LENGTH // (2 * half * half) for i in range(half)], dtype=np.int64)
    steps = np.arange(LENGTH, dtype=np.int64)
    angles = 2.0 * np.pi * ((factor[:, None] * steps[None, :]) % LENGTH) / LENGTH
    return split_table(np.concatenate([np.sin(angles), np.cos(angles)], axis=0))


def transform_tables():
    order = np.array([2 * p + h for h in range(2) for p in range(STEPS // 2)])
    k1 = np.arange(STEPS)
    alpha = np.pi * order[None, :] / STEPS / 2 - 2.0 * np.pi * ((order[None, :] * k1[:, None]) % STEPS) / STEPS
    outer = np.concatenate([np.cos(alpha), np.sin(alpha)], axis=0)
    outer_high, outer_low = split_table(outer)
    first = np.concatenate([outer_high, outer_low], axis=1)
    back_high, back_low = split_table(outer.T / LENGTH)
    last = np.concatenate([back_high, back_low, back_high], axis=1)
    b = np.arange(LANES)
    beta = np.pi * b[None, :] / (2 * LENGTH) - 2.0 * np.pi * ((b[None, :] * k1[:, None]) % LENGTH) / LENGTH
    twist_cos = np.cos(beta).astype(np.float32)
    twist_sin = np.sin(beta).astype(np.float32)
    gamma = 2.0 * np.pi * ((b[:, None] * b[None, :]) % LANES) / LANES
    cos, sin = np.cos(gamma), np.sin(gamma)
    ahead = split_table(np.block([[cos, -sin], [sin, cos]]))
    behind = split_table(np.block([[cos, sin], [-sin, cos]]))
    return (first, last, twist_cos, twist_sin, *ahead, *behind)


def split(values):
    high = values.astype(BF16)
    return high, (values - high.astype(F32)).astype(BF16)


def mul(left, right, dims=((1,), (0,))):
    return lax.dot_general(left, right, (dims, ((), ())), preferred_element_type=F32)


def mul3(left, right, dims=((1,), (0,))):
    lh, ll = left
    rh, rl = right
    return mul(lh, rh, dims) + mul(ll, rh, dims) + mul(lh, rl, dims)


def wait_for(loads, *which):
    for k in which:
        if loads is not None:
            loads[k].wait()


def spectrum(stack_ref, high_ref, low_ref, tabs, loads=None):
    first, _, tc_ref, ts_ref, ahead_high, ahead_low, _, _ = tabs
    wait_for(loads, 0, 2, 3)
    tc, ts = tc_ref[...], ts_ref[...]
    for c in range(0, OWN, 2):
        pair = [stack_ref[pl.ds(c + k, STEPS, stride=OWN), :] for k in range(2)]
        wide = jnp.concatenate(pair, axis=1).astype(BF16)
        u = mul(first[...], jnp.concatenate([wide, wide], axis=0))
        for k in range(2):
            ur = u[:STEPS, k * LANES : (k + 1) * LANES]
            ui = u[STEPS:, k * LANES : (k + 1) * LANES]
            v = jnp.concatenate([ur * tc - ui * ts, ur * ts + ui * tc], axis=1)
            high, low = split(v)
            high_ref[(c + k) * STEPS : (c + k + 1) * STEPS, :] = high
            low_ref[(c + k) * STEPS : (c + k + 1) * STEPS, :] = low
    wait_for(loads, 4, 5)
    return mul3((high_ref[...], low_ref[...]), (ahead_high[...], ahead_low[...]))


def from_spectrum(values, stack_ref, tabs, loads=None):
    _, last, tc_ref, ts_ref, _, _, behind_high, behind_low = tabs
    wait_for(loads, 6, 7, 1)
    tc, ts = tc_ref[...], ts_ref[...]
    q = mul3(split(values), (behind_high[...], behind_low[...]))
    for c in range(0, OWN, 2):
        pair = []
        for k in range(2):
            rows = q[(c + k) * STEPS : (c + k + 1) * STEPS]
            qr, qi = rows[:, :LANES], rows[:, LANES:]
            pair.append(jnp.concatenate([qr * tc + qi * ts, qi * tc - qr * ts], axis=0))
        high, low = split(jnp.concatenate(pair, axis=1))
        y = mul(last[...], jnp.concatenate([high, high, low], axis=0))
        for k in range(2):
            stack_ref[pl.ds(c + k, STEPS, stride=OWN), :] = y[:, k * LANES : (k + 1) * LANES]


def product(left, right, conjugate):
    lr, li = left[:, :LANES], left[:, LANES:]
    rr, ri = right[:, :LANES], right[:, LANES:]
    if conjugate:
        return jnp.concatenate([lr * rr + li * ri, lr * ri - li * rr], axis=1)
    return jnp.concatenate([lr * rr - li * ri, lr * ri + li * rr], axis=1)


def sin_cos(x):
    turns = jnp.floor(x * (2.0 / math.pi) + 0.5)
    r = x - turns * 1.5703125
    r = r - turns * 4.837512969970703125e-4
    r = r - turns * 7.549789948768648e-8
    z = r * r
    s = r + r * z * (-1.6666654611e-1 + z * (8.3321608736e-3 - z * 1.9515295891e-4))
    c = 1.0 - 0.5 * z + z * z * (4.166664568298827e-2 + z * (-1.388731625493765e-3 + z * 2.443315711809948e-5))
    quad = turns.astype(jnp.int32)
    odd = (quad & 1) == 1
    sin = jnp.where(odd, c, s)
    cos = jnp.where(odd, s, c)
    sin = jnp.where((quad & 2) == 2, -sin, sin)
    cos = jnp.where(((quad + 1) & 2) == 2, -cos, cos)
    return sin, cos


def envelope(rates, start, size):
    steps = (start + lax.broadcasted_iota(jnp.int32, (OWN, size), 1)).astype(F32)
    return jnp.sqrt(rates) * jnp.exp(-steps * rates), steps


def prep_kernel(x_hbm, cot_hbm, w_hbm, out_hbm, x_ref, cot_ref, w_ref, pad_ref, sum_ref, xt_ref, ga_ref, sems):
    x_copy = pltpu.make_async_copy(x_hbm, x_ref, sems.at[0])
    x_copy.start()
    cot_copy = pltpu.make_async_copy(cot_hbm, cot_ref, sems.at[1])
    cot_copy.start()
    w_copies = [pltpu.make_async_copy(w_hbm.at[i], w_ref.at[i], sems.at[2 + i]) for i in range(KERNEL)]
    for copy in w_copies:
        copy.start()
    pad_ref[:EDGE, :] = jnp.zeros((EDGE, WIDTH), F32)
    pad_ref[EDGE + ROWS :, :] = jnp.zeros((8, WIDTH), F32)
    x_copy.wait()
    xt_ref[...] = jnp.transpose(x_ref[...].astype(F32)).astype(BF16)
    x_out = pltpu.make_async_copy(xt_ref, out_hbm.at[:, pl.ds(0, ROWS)], sems.at[2 + KERNEL])
    x_out.start()
    cot_copy.wait()
    pad_ref[EDGE : EDGE + ROWS, :] = cot_ref[...].astype(F32)
    for i in range(KERNEL):
        shifted = pad_ref[i : i + EDGE + ROWS, :].astype(BF16)
        w_copies[i].wait()
        part = mul(shifted, w_ref[i], ((1,), (1,)))
        if i == 0:
            sum_ref[HALO - EDGE :, :] = part
        else:
            sum_ref[HALO - EDGE :, :] += part
    sum_ref[: HALO - EDGE, :] = jnp.zeros((HALO - EDGE, WIDTH), F32)
    ga_ref[...] = jnp.transpose(sum_ref[...]).astype(BF16)
    ga_out = pltpu.make_async_copy(ga_ref, out_hbm.at[:, pl.ds(ROWS, SPAN)], sems.at[3 + KERNEL])
    ga_out.start()
    x_out.wait()
    ga_out.wait()


def taps_kernel(wp_ref, wf_ref, lr_ref, gain_ref, feat_ref, *rest):
    tabs = rest[:8]
    hid_out, cos_out, taps_out, spec_out, par_out = rest[8:13]
    hid_ref, cos_ref, taps_ref, spec_ref, par_ref, stack_ref, vh_ref, vl_ref, sems = rest[13:]
    first = lax.axis_index("tm") * OWN
    lane = lax.broadcasted_iota(jnp.int32, (OWN, WIDTH), 1)
    chosen = lane == first + lax.broadcasted_iota(jnp.int32, (OWN, WIDTH), 0)
    wf_own = lax.dot_general(
        chosen.astype(F32),
        wf_ref[...],
        (((1,), (1,)), ((), ())),
        precision=lax.Precision.HIGHEST,
        preferred_element_type=F32,
    )
    rates = jnp.exp(jnp.sum(jnp.where(chosen, lr_ref[...], 0.0), axis=1, keepdims=True))
    gain = jnp.sum(jnp.where(chosen, gain_ref[...], 0.0), axis=1, keepdims=True)
    spot = lax.broadcasted_iota(jnp.int32, (OWN, LANES), 1)
    par_ref[...] = jnp.where(spot == FEAT, rates, jnp.where(spot == FEAT + 1, gain, 0.0))
    par_ref[:, :FEAT] = wf_own
    wp_high, wp_low = split(wp_ref[...])
    wp = jnp.concatenate([wp_high, wp_low, wp_high], axis=0)
    wf_high, wf_low = split(wf_own)
    for start in range(0, LENGTH, BLOCK):
        cut = slice(start, start + BLOCK)
        feat = feat_ref[:, cut]
        sin, cos = sin_cos(mul(wp, jnp.concatenate([feat[:FEAT], feat], axis=0), ((0,), (0,))))
        high, low = split(sin)
        hid_ref[:FEAT, cut] = high
        hid_ref[FEAT:, cut] = low
        cos_ref[:, cut] = cos
        decay, _ = envelope(rates, start, BLOCK)
        taps = mul3((wf_high, wf_low), (high, low)) * decay
        taps_ref[:, cut] = taps
        rounded = taps.astype(BF16).astype(F32)
        for j in range(BLOCK // LANES):
            a = start // LANES + j
            row = ((a % 2) * SHARDS + a // 2) * OWN
            stack_ref[row : row + OWN, :] = rounded[:, j * LANES : (j + 1) * LANES]
    saves = [
        pltpu.make_async_copy(source, target, sems.at[k])
        for k, (source, target) in enumerate(((hid_ref, hid_out), (cos_ref, cos_out), (taps_ref, taps_out), (par_ref, par_out)))
    ]
    for save in saves:
        save.start()
    spec_ref[...] = spectrum(stack_ref, vh_ref, vl_ref, tabs)
    saves.append(pltpu.make_async_copy(spec_ref, spec_out, sems.at[4]))
    saves[-1].start()
    for save in saves:
        save.wait()


def gelu_parts(before):
    root = math.sqrt(2.0 / math.pi)
    square = before * before
    th = jnp.tanh(root * (before + 0.044715 * square * before))
    half_cdf = 0.5 * (1.0 + th)
    slope = half_cdf + 0.5 * before * (1.0 - th * th) * (root * (1.0 + 3.0 * 0.044715 * square))
    return before * half_cdf, slope


def forward_kernel(recv_hbm, tspec_hbm, par_hbm, *rest):
    tabs_hbm = rest[:8]
    act_hbm, before_hbm, xspec_hbm = rest[8:11]
    xin_ref, tspec_ref, spec_ref, act_ref = rest[11:15]
    tabs = rest[15:23]
    x_ref, y_ref, vh_ref, vl_ref, par_ref, sems = rest[23:]
    x_load = pltpu.make_async_copy(recv_hbm.at[:, :, pl.ds(0, ROWS)], xin_ref, sems.at[0])
    x_load.start()
    loads = [pltpu.make_async_copy(tabs_hbm[k], tabs[k], sems.at[1 + k]) for k in range(8)]
    for k in (0, 2, 3, 4, 5, 6, 7, 1):
        loads[k].start()
    tspec_load = pltpu.make_async_copy(tspec_hbm, tspec_ref, sems.at[9])
    tspec_load.start()
    par_load = pltpu.make_async_copy(par_hbm, par_ref, sems.at[10])
    par_load.start()
    x_load.wait()
    for h in range(2):
        part = xin_ref[:, :, h * LANES : (h + 1) * LANES].astype(F32)
        x_ref[h * STACK // 2 : (h + 1) * STACK // 2, :] = part.reshape(STACK // 2, LANES)
    spec = spectrum(x_ref, vh_ref, vl_ref, tabs, loads)
    spec_ref[...] = spec
    spec_save = pltpu.make_async_copy(spec_ref, xspec_hbm, sems.at[11])
    spec_save.start()
    tspec_load.wait()
    from_spectrum(product(tspec_ref[...], spec, False), y_ref, tabs, loads)
    par_load.wait()
    gain = par_ref[:, FEAT + 1 : FEAT + 2][None]
    before = y_ref[...].reshape(STEPS, OWN, LANES) + gain * x_ref[...].reshape(STEPS, OWN, LANES)
    y_ref[...] = before.reshape(STACK, LANES)
    before_save = pltpu.make_async_copy(y_ref, before_hbm, sems.at[12])
    before_save.start()
    active = gelu_parts(before)[0].astype(BF16)
    act_ref[:, :, HALO : HALO + LANES] = active[:SHARDS]
    act_ref[:, :, HALO + LANES :] = active[SHARDS:]
    act_ref[:, :, :HALO] = jnp.concatenate([jnp.zeros((1, OWN, LANES), BF16), active[SHARDS:-1]], axis=0)
    act_save = pltpu.make_async_copy(act_ref, act_hbm, sems.at[13])
    act_save.start()
    spec_save.wait()
    before_save.wait()
    act_save.wait()


def backward_kernel(*rest):
    arrays_hbm, tabs_hbm = rest[:9], rest[9:17]
    ig_hbm, small_hbm = rest[17:19]
    arrays, tabs = rest[19:28], rest[28:36]
    recv_ref, before_ref, xspec_ref, tspec_ref, par_ref, hid_ref, cos_ref, feat_ref, taps_ref = arrays
    gb_ref, ig_ref, small_ref, y_ref, vh_ref, vl_ref, g_ref, sems = rest[36:]
    first = [pltpu.make_async_copy(arrays_hbm[k], arrays[k], sems.at[k]) for k in range(9)]
    table = [pltpu.make_async_copy(tabs_hbm[k], tabs[k], sems.at[9 + k]) for k in range(8)]
    for copy in (*first[:2], *table, *first[2:]):
        copy.start()
    wait_for(first, 0, 1)
    early = recv_ref[:, :, ROWS + HALO : ROWS + HALO + LANES].astype(F32)
    late = recv_ref[:, :, ROWS + HALO + LANES :].astype(F32)
    edge = recv_ref[:, :, ROWS : ROWS + HALO].astype(F32)
    edge = jnp.concatenate([edge[1:], jnp.zeros((1, OWN, LANES), F32)], axis=0)
    grad_active = jnp.concatenate([early, late + edge], axis=0)
    slope = gelu_parts(before_ref[...])[1].reshape(STEPS, OWN, LANES)
    grad = (grad_active * slope).astype(BF16).astype(F32)
    gb_ref[...] = grad.reshape(STACK, LANES)
    x = jnp.concatenate([recv_ref[:, :, :LANES].astype(F32), recv_ref[:, :, LANES:ROWS].astype(F32)], axis=0)
    skip = jnp.sum(jnp.sum(grad * x, axis=0), axis=1, keepdims=True)
    spec = spectrum(gb_ref, vh_ref, vl_ref, tabs, table)
    wait_for(first, 2, 3, 4)
    from_spectrum(product(tspec_ref[...], spec, True), y_ref, tabs, table)
    gain = par_ref[:, FEAT + 1 : FEAT + 2][None]
    result = (y_ref[...].reshape(STEPS, OWN, LANES) + gain * grad).astype(BF16)
    ig_ref[:, :, :LANES] = result[:SHARDS]
    ig_ref[:, :, LANES:] = result[SHARDS:]
    save = pltpu.make_async_copy(ig_ref, ig_hbm, sems.at[17])
    save.start()
    from_spectrum(product(xspec_ref[...], spec, True), y_ref, tabs)
    for a in range(STEPS):
        row = ((a % 2) * SHARDS + a // 2) * OWN
        g_ref[:, a * LANES : (a + 1) * LANES] = y_ref[row : row + OWN, :]
    wf_high, wf_low = split(par_ref[:, :FEAT])
    wf = jnp.concatenate([wf_high, wf_low, wf_high], axis=0)
    rates = par_ref[:, FEAT : FEAT + 1]
    wait_for(first, 5, 6, 7, 8)
    filt = jnp.zeros((2 * OWN, 2 * FEAT), F32)
    pos = jnp.zeros((2 * FEAT, 2 * FEAT), F32)
    rate = jnp.zeros((OWN, 1), F32)
    for start in range(0, LENGTH, BLOCK):
        cut = slice(start, start + BLOCK)
        grad_taps = g_ref[:, cut]
        decay, steps = envelope(rates, start, BLOCK)
        high, low = split(grad_taps * decay)
        rate = rate + jnp.sum(grad_taps * taps_ref[:, cut] * (0.5 - rates * steps), axis=1, keepdims=True)
        filt = filt + mul(jnp.concatenate([high, low], axis=0), hid_ref[:, cut], ((1,), (1,)))
        inner = mul(wf, jnp.concatenate([high, high, low], axis=0), ((0,), (0,))) * cos_ref[:, cut]
        pos = pos + mul(feat_ref[:, cut], jnp.concatenate(split(inner), axis=0), ((1,), (1,)))
    filt = filt[:OWN, :FEAT] + filt[OWN:, :FEAT] + filt[:OWN, FEAT:]
    pos = pos[:FEAT, :FEAT] + pos[FEAT:, :FEAT] + pos[:FEAT, FEAT:]
    small_ref[...] = jnp.zeros((2, 2 * OWN, LANES), F32)
    for e, stat in enumerate((rate, skip)):
        small_ref[e, :OWN, :32] = filt[:, 32 * e : 32 * e + 32]
        small_ref[e, :OWN, 32:33] = stat
        small_ref[e, OWN:, :FEAT] = pos[32 * e : 32 * e + 16]
        small_ref[e, OWN:, FEAT:] = pos[32 * e + 16 : 32 * e + 32]
    small_save = pltpu.make_async_copy(small_ref, small_hbm, sems.at[18])
    small_save.start()
    save.wait()
    small_save.wait()


def conv_kernel(
    act_hbm, peer_act_hbm, cot_hbm, peer_cot_hbm, ig_hbm, small_hbm, peer_small_hbm, out_hbm,
    act_ref, cot_ref, ig_ref, small_ref, pad_ref, part_ref, tile_ref, sems,
):
    core = lax.axis_index("batch") % 2
    half = pl.ds(pl.multiple_of(core * HALF, HALF), HALF)
    sources = [
        (cot_hbm.at[:, half], cot_ref.at[0]),
        (peer_cot_hbm.at[:, half], cot_ref.at[1]),
        (act_hbm, act_ref.at[0]),
        (peer_act_hbm, act_ref.at[1]),
        (ig_hbm, ig_ref),
        (small_hbm.at[core], small_ref.at[0]),
        (peer_small_hbm.at[core], small_ref.at[1]),
    ]
    loads = [pltpu.make_async_copy(a, b, sems.at[k]) for k, (a, b) in enumerate(sources)]
    for load in loads:
        load.start()
    pad_ref[:, :HALO, :] = jnp.zeros((2, HALO, HALF), F32)
    pad_ref[:, HALO + ROWS :, :] = jnp.zeros((2, 8, HALF), F32)
    wait_for(loads, 0, 1)
    pad_ref[:, HALO : HALO + ROWS, :] = cot_ref[...].astype(F32)
    wait_for(loads, 2, 3)
    copies = []
    for i in range(KERNEL):
        own = pad_ref[0, i : i + SPAN, :].astype(BF16)
        peer = pad_ref[1, i : i + SPAN, :].astype(BF16)
        part_ref[i] = (mul(act_ref[0], own) + mul(act_ref[1], peer)).astype(BF16)
        copies.append(pltpu.make_async_copy(part_ref.at[i], out_hbm.at[:, pl.ds(i * HALF, HALF)], sems.at[9 + i]))
        copies[-1].start()
        if i == 0:
            wait_for(loads, 4, 5, 6)
            tile_ref[:, :ROWS] = ig_ref[...]
            small = small_ref[0] + small_ref[1]
            high, low = split(small[:OWN])
            filt = high.astype(F32) + pltpu.roll(low.astype(F32), FEAT, 1)
            tile = jnp.concatenate([filt, small[OWN:]], axis=1).astype(BF16)
            for p in range(SHARDS):
                tile_ref[p * OWN : (p + 1) * OWN, ROWS:] = tile
            target = out_hbm.at[:, pl.ds(CONV, ROWS + 2 * LANES)]
            copies.append(pltpu.make_async_copy(tile_ref, target, sems.at[9 + KERNEL]))
            copies[-1].start()
    for copy in copies:
        copy.wait()


def mixed_kernel(act_hbm, w_hbm, _, out_hbm, act_ref, w_ref, part_ref, out_ref, sems):
    loads = [pltpu.make_async_copy(w_hbm.at[i], w_ref.at[i], sems.at[i]) for i in range(KERNEL)]
    loads.append(pltpu.make_async_copy(act_hbm, act_ref, sems.at[KERNEL]))
    for load in loads:
        load.start()
    wait_for(loads, KERNEL)
    act = jnp.transpose(act_ref[...].astype(F32)).astype(BF16)[HALO - EDGE :]
    total = jnp.zeros((ROWS, WIDTH), F32)
    for i in range(KERNEL):
        wait_for(loads, i)
        part_ref[...] = mul(act, w_ref[i])
        total = total + part_ref[EDGE - i : EDGE - i + ROWS, :]
    out_ref[...] = total.astype(BF16)
    save = pltpu.make_async_copy(out_ref, out_hbm, sems.at[KERNEL + 1])
    save.start()
    save.wait()


def fold(block):
    return jnp.concatenate([block[:8], block[8:]], axis=1)


def gather_kernel(recv_ref, out_ref):
    conv = jnp.sum(recv_ref[:, :, :CONV].astype(F32), axis=0)
    blocks = [conv[:, :WIDTH], conv[:, WIDTH : 2 * WIDTH], fold(conv[:, 2 * WIDTH :])]
    base = CONV + ROWS
    both = recv_ref[:, :, base : base + LANES].astype(F32).reshape(WIDTH, LANES)
    filt = jnp.transpose(both + pltpu.roll(both, FEAT, 1))
    pos = jnp.sum(recv_ref[:, :, base + LANES : base + 2 * LANES].astype(F32), axis=0)
    stat = filt[32:33]
    pieces = [stat[:, j * LANES : (j + 1) * LANES] for j in range(4)]
    stat = jnp.concatenate([*pieces, jnp.zeros((4, LANES), F32)], axis=0)
    last = jnp.concatenate([fold(pos), stat, jnp.zeros((8, LANES), F32)], axis=1)
    out_ref[...] = jnp.concatenate([*blocks, filt[:32], last], axis=0).astype(BF16)


def pair_kernel(own_ref, other_ref, out_ref):
    out_ref[...] = (own_ref[...].astype(F32) + other_ref[...].astype(F32)).astype(BF16)


def final_kernel(own_ref, other_ref, out_ref):
    out_ref[...] = (own_ref[...].astype(F32) + other_ref[...].astype(F32)) * SCALE


def input_kernel(recv_ref, out_hbm, out_ref, sem):
    out_ref[...] = jnp.transpose(recv_ref[:, :, CONV : CONV + ROWS].astype(F32).reshape(WIDTH, ROWS)).astype(BF16)
    save = pltpu.make_async_copy(out_ref, out_hbm, sem)
    save.start()
    save.wait()


def join_kernel(mine_ref, other_ref, conv_ref, pos_ref, filt_ref, rates_ref, skip_ref):
    core = lax.axis_index("batch") % 2

    def write(low, high):
        for e, part in enumerate((low, high)):
            lanes = slice(e * HALF, (e + 1) * HALF)
            for i in range(KERNEL - 1):
                row, lane = 16 * (i // 2), HALF * (i % 2)
                conv_ref[i, :, lanes] = part[row : row + 16, lane : lane + HALF]
            conv_ref[KERNEL - 1, :8, lanes] = part[32:40, :HALF]
            conv_ref[KERNEL - 1, 8:, lanes] = part[32:40, HALF:]
            filt_ref[32 * e : 32 * e + 32, :] = part[40:72, :]
            for j in range(2):
                pos = part[72:80, j * LANES : (j + 1) * LANES]
                pos_ref[32 * e + 8 * j : 32 * e + 8 * j + 8, :] = pos[:, :FEAT]
                pos_ref[32 * e + 16 + 8 * j : 32 * e + 24 + 8 * j, :] = pos[:, FEAT:]
            for j in range(4):
                (rates_ref, skip_ref)[e][:, j * LANES : (j + 1) * LANES] = part[72 + j : 73 + j, HALF : HALF + LANES]

    @pl.when(core == 0)
    def _():
        write(mine_ref, other_ref)

    @pl.when(core == 1)
    def _():
        write(other_ref, mine_ref)


VMEM = pl.BlockSpec(memory_space=pltpu.VMEM)
HBM = pl.BlockSpec(memory_space=pltpu.HBM)


def call(kernel, out_shape, args, scratch=(), flops=0, name=None, specs=None, out_specs=None, limit=60):
    single = not isinstance(out_shape, (list, tuple))
    outs = [out_shape] if single else out_shape
    moved = sum(math.prod(a.shape) * a.dtype.itemsize for a in (*args, *outs))
    return pl.pallas_call(
        kernel,
        out_shape=out_shape,
        in_specs=specs or [VMEM] * len(args),
        out_specs=out_specs or (VMEM if single else [VMEM] * len(outs)),
        scratch_shapes=list(scratch),
        compiler_params=pltpu.CompilerParams(vmem_limit_bytes=limit * 1024 * 1024),
        cost_estimate=pl.CostEstimate(flops=flops, bytes_accessed=moved, transcendentals=0),
        name=name,
    )(*args)


def shape(dims, kind=F32):
    return jax.ShapeDtypeStruct(dims, kind)


def regroup(blocks):
    return lax.all_to_all(blocks, "tm", split_axis=0, concat_axis=0, tiled=True)


def on_device(inputs, cotangent, w_pos, w_filt, log_rates, skip_gain, w_conv):
    swap = [(i, i ^ 1) for i in range(lax.axis_size("batch"))]
    signal, upstream = inputs[0], cotangent[0]
    w_taps = jnp.transpose(w_conv, (1, 0, 2))
    tabs = tuple(jnp.asarray(t) for t in transform_tables())
    feat = jnp.asarray(np.concatenate(feature_tables(), axis=0))

    message = call(
        prep_kernel,
        shape((WIDTH, ROWS + SPAN), BF16),
        (signal, upstream, w_taps),
        [
            pltpu.VMEM((ROWS, WIDTH), BF16),
            pltpu.VMEM((ROWS, WIDTH), BF16),
            pltpu.VMEM((KERNEL, WIDTH, WIDTH), BF16),
            pltpu.VMEM((EDGE + ROWS + 8, WIDTH), F32),
            pltpu.VMEM((SPAN, WIDTH), F32),
            pltpu.VMEM((WIDTH, ROWS), BF16),
            pltpu.VMEM((WIDTH, SPAN), BF16),
            pltpu.SemaphoreType.DMA((4 + KERNEL,)),
        ],
        flops=2 * KERNEL * WIDTH * WIDTH * (ROWS + EDGE),
        name="prep",
        specs=[HBM] * 3,
        out_specs=HBM,
    )
    received = regroup(message.reshape(SHARDS, OWN, ROWS + SPAN))
    cot_peer = lax.ppermute(upstream, "batch", swap)
    received, cot_peer = lax.optimization_barrier((received, cot_peer))

    stack = pltpu.VMEM((STACK, LANES), F32)
    wide = pltpu.VMEM((STACK, 2 * LANES), BF16)
    saved = [pltpu.VMEM((2 * FEAT, LENGTH), BF16), pltpu.VMEM((FEAT, LENGTH), F32), pltpu.VMEM((OWN, LENGTH), F32)]
    flops = 2 * 3 * (2 * STACK * LANES * LANES + STACK * 4 * LANES * LANES)
    hidden, cosines, taps, tap_spec, par = call(
        taps_kernel,
        [
            shape((2 * FEAT, LENGTH), BF16),
            shape((FEAT, LENGTH)),
            shape((OWN, LENGTH)),
            shape((STACK, 2 * LANES)),
            shape((OWN, LANES)),
        ],
        (w_pos, w_filt, log_rates[None], skip_gain[None], feat, *tabs),
        [*saved, pltpu.VMEM((STACK, 2 * LANES), F32), pltpu.VMEM((OWN, LANES), F32), stack, wide, wide, pltpu.SemaphoreType.DMA((5,))],
        flops=flops * 2,
        name="taps",
        out_specs=[HBM] * 5,
    )
    act_message, before, sig_spec = call(
        forward_kernel,
        [shape((SHARDS, OWN, SPAN), BF16), shape((STACK, LANES)), shape((STACK, 2 * LANES))],
        (received, tap_spec, par, *tabs),
        [
            pltpu.VMEM((SHARDS, OWN, ROWS), BF16),
            pltpu.VMEM((STACK, 2 * LANES), F32),
            pltpu.VMEM((STACK, 2 * LANES), F32),
            pltpu.VMEM((SHARDS, OWN, SPAN), BF16),
            *[pltpu.VMEM(t.shape, t.dtype) for t in tabs],
            stack,
            stack,
            wide,
            wide,
            pltpu.VMEM((OWN, LANES), F32),
            pltpu.SemaphoreType.DMA((14,)),
        ],
        flops=flops * 2,
        name="forward",
        specs=[HBM] * 11,
        out_specs=[HBM] * 3,
    )
    act = regroup(act_message).reshape(WIDTH, SPAN)
    ig_message, small = call(
        backward_kernel,
        [shape((SHARDS, OWN, ROWS), BF16), shape((2, 2 * OWN, LANES))],
        (received, before, sig_spec, tap_spec, par, hidden, cosines, feat, taps, *tabs),
        [
            pltpu.VMEM((SHARDS, OWN, ROWS + SPAN), BF16),
            stack,
            pltpu.VMEM((STACK, 2 * LANES), F32),
            pltpu.VMEM((STACK, 2 * LANES), F32),
            pltpu.VMEM((OWN, LANES), F32),
            *saved[:2],
            saved[0],
            saved[2],
            *[pltpu.VMEM(t.shape, t.dtype) for t in tabs],
            stack,
            pltpu.VMEM((SHARDS, OWN, ROWS), BF16),
            pltpu.VMEM((2, 2 * OWN, LANES), F32),
            stack,
            wide,
            wide,
            pltpu.VMEM((OWN, LENGTH), F32),
            pltpu.SemaphoreType.DMA((19,)),
        ],
        flops=flops * 4,
        name="backward",
        specs=[HBM] * 17,
        out_specs=[HBM] * 2,
    )
    act, ig_message, small = lax.optimization_barrier((act, ig_message, small))
    act_peer = lax.ppermute(act, "batch", swap)
    small_peer = lax.ppermute(small, "batch", swap)
    lanes = CONV + ROWS + 2 * LANES
    sums = call(
        conv_kernel,
        shape((WIDTH, lanes), BF16),
        (act, act_peer, upstream, cot_peer, ig_message.reshape(WIDTH, ROWS), small, small_peer),
        [
            pltpu.VMEM((2, WIDTH, SPAN), BF16),
            pltpu.VMEM((2, ROWS, HALF), BF16),
            pltpu.VMEM((WIDTH, ROWS), BF16),
            pltpu.VMEM((2, 2 * OWN, LANES), F32),
            pltpu.VMEM((2, HALO + ROWS + 8, HALF), F32),
            pltpu.VMEM((KERNEL, WIDTH, HALF), BF16),
            pltpu.VMEM((WIDTH, ROWS + 2 * LANES), BF16),
            pltpu.SemaphoreType.DMA((10 + KERNEL,)),
        ],
        flops=2 * KERNEL * WIDTH * HALF * 2 * ROWS,
        name="conv_grad",
        specs=[HBM] * 7,
        out_specs=HBM,
    )
    spread = regroup(sums.reshape(SHARDS, OWN, lanes))
    mixed = call(
        mixed_kernel,
        shape((ROWS, WIDTH), BF16),
        (act, w_taps, sums),
        [
            pltpu.VMEM((WIDTH, SPAN), BF16),
            pltpu.VMEM((KERNEL, WIDTH, WIDTH), BF16),
            pltpu.VMEM((ROWS + EDGE, WIDTH), F32),
            pltpu.VMEM((ROWS, WIDTH), BF16),
            pltpu.SemaphoreType.DMA((2 + KERNEL,)),
        ],
        flops=2 * KERNEL * WIDTH * WIDTH * (ROWS + EDGE),
        name="mixed",
        specs=[HBM] * 3,
        out_specs=HBM,
    )
    spread, mixed = lax.optimization_barrier((spread, mixed))
    payload = call(gather_kernel, shape((80, WIDTH), BF16), (spread,), name="gather", limit=12)
    met = lax.ppermute(payload, "batch", [(i, i ^ 2) for i in range(8)])
    pair = call(pair_kernel, shape((80, WIDTH), BF16), (payload, met), name="pair", limit=12)
    met = lax.ppermute(pair, "batch", [(i, i ^ 6) for i in range(8)])
    spread, pair = lax.optimization_barrier((spread, pair))
    input_grad = call(
        input_kernel,
        shape((ROWS, WIDTH), BF16),
        (spread,),
        [pltpu.VMEM((ROWS, WIDTH), BF16), pltpu.SemaphoreType.DMA],
        name="input",
        out_specs=HBM,
        limit=12,
    )
    pair, input_grad = lax.optimization_barrier((pair, input_grad))
    mine = call(final_kernel, shape((80, WIDTH)), (pair, met), name="final", limit=12)
    other = lax.ppermute(mine, "batch", swap)
    conv_grad, pos_grad, filt_grad, rates_grad, skip_grad = call(
        join_kernel,
        [
            shape((KERNEL, OWN, WIDTH)),
            shape((FEAT, FEAT)),
            shape((FEAT, WIDTH)),
            shape((1, WIDTH)),
            shape((1, WIDTH)),
        ],
        (mine, other),
        name="join",
        limit=12,
    )
    return (
        mixed[None],
        input_grad[None],
        jnp.transpose(conv_grad, (1, 0, 2)),
        pos_grad,
        filt_grad,
        rates_grad[0],
        skip_grad[0],
    )


def solution(mesh):
    in_specs = (P("batch", "tm", None), P("batch", "tm", None), P(), P(), P(), P(), P())
    out_specs = (P("batch", "tm", None), P("batch", "tm", None), P("tm", None, None), P(), P(), P(), P())
    return jax.shard_map(on_device, mesh=mesh, in_specs=in_specs, out_specs=out_specs, check_vma=False)
```

```python
import math

import jax
import jax.numpy as jnp
import ml_dtypes
import numpy as np
from jax import lax
from jax.experimental import pallas as pl
from jax.experimental.pallas import tpu as pltpu
from jax.sharding import PartitionSpec as P

F32 = jnp.float32
BF16 = jnp.bfloat16

SHARDS = 32
ROWS = 256
LENGTH = SHARDS * ROWS
WIDTH = 512
KERNEL = 5
FEAT = 64
OWN = WIDTH // SHARDS
LANES = 128
STEPS = LENGTH // LANES
STACK = STEPS * OWN
HALO = LANES
SPAN = ROWS + HALO
HALF = WIDTH // 2
EDGE = 16
CONV = KERNEL * HALF
BLOCK = 4096
CHUNK = 128
SCALE = 1.0 / math.sqrt(8 * LENGTH)


def split_table(values):
    high = values.astype(ml_dtypes.bfloat16)
    low = (values - high.astype(np.float64)).astype(ml_dtypes.bfloat16)
    return high, low


def feature_tables():
    half = FEAT // 2
    factor = np.array([1 + i * i * LENGTH // (2 * half * half) for i in range(half)], dtype=np.int64)
    steps = np.arange(LENGTH, dtype=np.int64)
    angles = 2.0 * np.pi * ((factor[:, None] * steps[None, :]) % LENGTH) / LENGTH
    return split_table(np.concatenate([np.sin(angles), np.cos(angles)], axis=0))


def transform_tables():
    order = np.array([2 * p + h for h in range(2) for p in range(STEPS // 2)])
    k1 = np.arange(STEPS)
    alpha = np.pi * order[None, :] / STEPS / 2 - 2.0 * np.pi * ((order[None, :] * k1[:, None]) % STEPS) / STEPS
    outer = np.concatenate([np.cos(alpha), np.sin(alpha)], axis=0)
    outer_high, outer_low = split_table(outer)
    first = np.concatenate([outer_high, outer_low], axis=1)
    back_high, back_low = split_table(outer.T / LENGTH)
    last = np.concatenate([back_high, back_low, back_high], axis=1)
    b = np.arange(LANES)
    beta = np.pi * b[None, :] / (2 * LENGTH) - 2.0 * np.pi * ((b[None, :] * k1[:, None]) % LENGTH) / LENGTH
    twist_cos = np.cos(beta).astype(np.float32)
    twist_sin = np.sin(beta).astype(np.float32)
    gamma = 2.0 * np.pi * ((b[:, None] * b[None, :]) % LANES) / LANES
    cos, sin = np.cos(gamma), np.sin(gamma)
    ahead = split_table(np.block([[cos, -sin], [sin, cos]]))
    behind = split_table(np.block([[cos, sin], [-sin, cos]]))
    return (first, last, twist_cos, twist_sin, *ahead, *behind)


def split(values):
    high = values.astype(BF16)
    return high, (values - high.astype(F32)).astype(BF16)


def mul(left, right, dims=((1,), (0,))):
    return lax.dot_general(left, right, (dims, ((), ())), preferred_element_type=F32)


def mul3(left, right, dims=((1,), (0,))):
    lh, ll = left
    rh, rl = right
    return mul(lh, rh, dims) + mul(ll, rh, dims) + mul(lh, rl, dims)


def wait_for(loads, *which):
    for k in which:
        if loads is not None:
            loads[k].wait()


def spectrum(stack_ref, high_ref, low_ref, tabs, loads=None):
    first, _, tc_ref, ts_ref, ahead_high, ahead_low, _, _ = tabs
    wait_for(loads, 0, 2, 3)
    tc, ts = tc_ref[...], ts_ref[...]
    for c in range(0, OWN, 2):
        pair = [stack_ref[pl.ds(c + k, STEPS, stride=OWN), :] for k in range(2)]
        wide = jnp.concatenate(pair, axis=1).astype(BF16)
        u = mul(first[...], jnp.concatenate([wide, wide], axis=0))
        for k in range(2):
            ur = u[:STEPS, k * LANES : (k + 1) * LANES]
            ui = u[STEPS:, k * LANES : (k + 1) * LANES]
            v = jnp.concatenate([ur * tc - ui * ts, ur * ts + ui * tc], axis=1)
            high, low = split(v)
            high_ref[(c + k) * STEPS : (c + k + 1) * STEPS, :] = high
            low_ref[(c + k) * STEPS : (c + k + 1) * STEPS, :] = low
    wait_for(loads, 4, 5)
    table = (ahead_high[...], ahead_low[...])
    parts = [mul3((high_ref[r : r + CHUNK, :], low_ref[r : r + CHUNK, :]), table) for r in range(0, STACK, CHUNK)]
    return jnp.concatenate(parts, axis=0)


def from_spectrum(values, stack_ref, tabs, loads=None):
    _, last, tc_ref, ts_ref, _, _, behind_high, behind_low = tabs
    wait_for(loads, 6, 7, 1)
    tc, ts = tc_ref[...], ts_ref[...]
    table = (behind_high[...], behind_low[...])
    q = jnp.concatenate([mul3(split(values[r : r + CHUNK]), table) for r in range(0, STACK, CHUNK)], axis=0)
    for c in range(0, OWN, 2):
        pair = []
        for k in range(2):
            rows = q[(c + k) * STEPS : (c + k + 1) * STEPS]
            qr, qi = rows[:, :LANES], rows[:, LANES:]
            pair.append(jnp.concatenate([qr * tc + qi * ts, qi * tc - qr * ts], axis=0))
        high, low = split(jnp.concatenate(pair, axis=1))
        y = mul(last[...], jnp.concatenate([high, high, low], axis=0))
        for k in range(2):
            stack_ref[pl.ds(c + k, STEPS, stride=OWN), :] = y[:, k * LANES : (k + 1) * LANES]


def product(left, right, conjugate):
    lr, li = left[:, :LANES], left[:, LANES:]
    rr, ri = right[:, :LANES], right[:, LANES:]
    if conjugate:
        return jnp.concatenate([lr * rr + li * ri, lr * ri - li * rr], axis=1)
    return jnp.concatenate([lr * rr - li * ri, lr * ri + li * rr], axis=1)


def sin_cos(x):
    turns = jnp.floor(x * (2.0 / math.pi) + 0.5)
    r = x - turns * 1.5703125
    r = r - turns * 4.837512969970703125e-4
    r = r - turns * 7.549789948768648e-8
    z = r * r
    s = r + r * z * (-1.6666654611e-1 + z * (8.3321608736e-3 - z * 1.9515295891e-4))
    c = 1.0 - 0.5 * z + z * z * (4.166664568298827e-2 + z * (-1.388731625493765e-3 + z * 2.443315711809948e-5))
    quad = turns.astype(jnp.int32)
    odd = (quad & 1) == 1
    sin = jnp.where(odd, c, s)
    cos = jnp.where(odd, s, c)
    sin = jnp.where((quad & 2) == 2, -sin, sin)
    cos = jnp.where(((quad + 1) & 2) == 2, -cos, cos)
    return sin, cos


def envelope(rates, start, size):
    steps = (start + lax.broadcasted_iota(jnp.int32, (OWN, size), 1)).astype(F32)
    return jnp.sqrt(rates) * jnp.exp(-steps * rates), steps


def prep_kernel(x_hbm, cot_hbm, w_hbm, out_hbm, x_ref, cot_ref, w_ref, pad_ref, sum_ref, xt_ref, ga_ref, sems):
    x_copy = pltpu.make_async_copy(x_hbm, x_ref, sems.at[0])
    x_copy.start()
    cot_copy = pltpu.make_async_copy(cot_hbm, cot_ref, sems.at[1])
    cot_copy.start()
    w_copies = [pltpu.make_async_copy(w_hbm.at[i], w_ref.at[i], sems.at[2 + i]) for i in range(KERNEL)]
    for copy in w_copies:
        copy.start()
    pad_ref[:EDGE, :] = jnp.zeros((EDGE, WIDTH), F32)
    pad_ref[EDGE + ROWS :, :] = jnp.zeros((8, WIDTH), F32)
    x_copy.wait()
    xt_ref[...] = jnp.transpose(x_ref[...].astype(F32)).astype(BF16)
    x_out = pltpu.make_async_copy(xt_ref, out_hbm.at[:, pl.ds(0, ROWS)], sems.at[2 + KERNEL])
    x_out.start()
    cot_copy.wait()
    pad_ref[EDGE : EDGE + ROWS, :] = cot_ref[...].astype(F32)
    for i in range(KERNEL):
        shifted = pad_ref[i : i + EDGE + ROWS, :].astype(BF16)
        w_copies[i].wait()
        part = mul(shifted, w_ref[i], ((1,), (1,)))
        if i == 0:
            sum_ref[HALO - EDGE :, :] = part
        else:
            sum_ref[HALO - EDGE :, :] += part
    sum_ref[: HALO - EDGE, :] = jnp.zeros((HALO - EDGE, WIDTH), F32)
    ga_ref[...] = jnp.transpose(sum_ref[...]).astype(BF16)
    ga_out = pltpu.make_async_copy(ga_ref, out_hbm.at[:, pl.ds(ROWS, SPAN)], sems.at[3 + KERNEL])
    ga_out.start()
    x_out.wait()
    ga_out.wait()


def taps_kernel(wp_ref, wf_ref, lr_ref, gain_ref, feat_ref, *rest):
    tabs = rest[:8]
    hid_out, cos_out, taps_out, spec_out, par_out = rest[8:13]
    hid_ref, cos_ref, taps_ref, spec_ref, par_ref, stack_ref, vh_ref, vl_ref, sems = rest[13:]
    first = lax.axis_index("tm") * OWN
    lane = lax.broadcasted_iota(jnp.int32, (OWN, WIDTH), 1)
    chosen = lane == first + lax.broadcasted_iota(jnp.int32, (OWN, WIDTH), 0)
    wf_own = lax.dot_general(
        chosen.astype(F32),
        wf_ref[...],
        (((1,), (1,)), ((), ())),
        precision=lax.Precision.HIGHEST,
        preferred_element_type=F32,
    )
    rates = jnp.exp(jnp.sum(jnp.where(chosen, lr_ref[...], 0.0), axis=1, keepdims=True))
    gain = jnp.sum(jnp.where(chosen, gain_ref[...], 0.0), axis=1, keepdims=True)
    spot = lax.broadcasted_iota(jnp.int32, (OWN, LANES), 1)
    par_ref[...] = jnp.where(spot == FEAT, rates, jnp.where(spot == FEAT + 1, gain, 0.0))
    par_ref[:, :FEAT] = wf_own
    wp_high, wp_low = split(wp_ref[...])
    wp = jnp.concatenate([wp_high, wp_low, wp_high], axis=0)
    wf_high, wf_low = split(wf_own)
    for start in range(0, LENGTH, BLOCK):
        cut = slice(start, start + BLOCK)
        feat = feat_ref[:, cut]
        sin, cos = sin_cos(mul(wp, jnp.concatenate([feat[:FEAT], feat], axis=0), ((0,), (0,))))
        high, low = split(sin)
        hid_ref[:FEAT, cut] = high
        hid_ref[FEAT:, cut] = low
        cos_ref[:, cut] = cos
        decay, _ = envelope(rates, start, BLOCK)
        taps = mul3((wf_high, wf_low), (high, low)) * decay
        taps_ref[:, cut] = taps
        rounded = taps.astype(BF16).astype(F32)
        for j in range(BLOCK // LANES):
            a = start // LANES + j
            row = ((a % 2) * SHARDS + a // 2) * OWN
            stack_ref[row : row + OWN, :] = rounded[:, j * LANES : (j + 1) * LANES]
    saves = [
        pltpu.make_async_copy(source, target, sems.at[k])
        for k, (source, target) in enumerate(((hid_ref, hid_out), (cos_ref, cos_out), (taps_ref, taps_out), (par_ref, par_out)))
    ]
    for save in saves:
        save.start()
    spec_ref[...] = spectrum(stack_ref, vh_ref, vl_ref, tabs)
    saves.append(pltpu.make_async_copy(spec_ref, spec_out, sems.at[4]))
    saves[-1].start()
    for save in saves:
        save.wait()


def gelu_parts(before):
    root = math.sqrt(2.0 / math.pi)
    square = before * before
    th = jnp.tanh(root * (before + 0.044715 * square * before))
    half_cdf = 0.5 * (1.0 + th)
    slope = half_cdf + 0.5 * before * (1.0 - th * th) * (root * (1.0 + 3.0 * 0.044715 * square))
    return before * half_cdf, slope


def forward_kernel(recv_hbm, tspec_hbm, par_hbm, *rest):
    tabs_hbm = rest[:8]
    act_hbm, before_hbm, xspec_hbm = rest[8:11]
    xin_ref, tspec_ref, spec_ref, act_ref = rest[11:15]
    tabs = rest[15:23]
    x_ref, y_ref, vh_ref, vl_ref, par_ref, sems = rest[23:]
    x_load = pltpu.make_async_copy(recv_hbm.at[:, :, pl.ds(0, ROWS)], xin_ref, sems.at[0])
    x_load.start()
    loads = [pltpu.make_async_copy(tabs_hbm[k], tabs[k], sems.at[1 + k]) for k in range(8)]
    for k in (0, 2, 3, 4, 5, 6, 7, 1):
        loads[k].start()
    tspec_load = pltpu.make_async_copy(tspec_hbm, tspec_ref, sems.at[9])
    tspec_load.start()
    par_load = pltpu.make_async_copy(par_hbm, par_ref, sems.at[10])
    par_load.start()
    x_load.wait()
    for h in range(2):
        part = xin_ref[:, :, h * LANES : (h + 1) * LANES].astype(F32)
        x_ref[h * STACK // 2 : (h + 1) * STACK // 2, :] = part.reshape(STACK // 2, LANES)
    spec = spectrum(x_ref, vh_ref, vl_ref, tabs, loads)
    spec_ref[...] = spec
    spec_save = pltpu.make_async_copy(spec_ref, xspec_hbm, sems.at[11])
    spec_save.start()
    tspec_load.wait()
    from_spectrum(product(tspec_ref[...], spec, False), y_ref, tabs, loads)
    par_load.wait()
    gain = par_ref[:, FEAT + 1 : FEAT + 2][None]
    before = y_ref[...].reshape(STEPS, OWN, LANES) + gain * x_ref[...].reshape(STEPS, OWN, LANES)
    y_ref[...] = before.reshape(STACK, LANES)
    before_save = pltpu.make_async_copy(y_ref, before_hbm, sems.at[12])
    before_save.start()
    active = gelu_parts(before)[0].astype(BF16)
    act_ref[:, :, HALO : HALO + LANES] = active[:SHARDS]
    act_ref[:, :, HALO + LANES :] = active[SHARDS:]
    act_ref[:, :, :HALO] = jnp.concatenate([jnp.zeros((1, OWN, LANES), BF16), active[SHARDS:-1]], axis=0)
    act_save = pltpu.make_async_copy(act_ref, act_hbm, sems.at[13])
    act_save.start()
    spec_save.wait()
    before_save.wait()
    act_save.wait()


def backward_kernel(*rest):
    arrays_hbm, tabs_hbm = rest[:9], rest[9:17]
    ig_hbm, small_hbm = rest[17:19]
    arrays, tabs = rest[19:28], rest[28:36]
    recv_ref, before_ref, xspec_ref, tspec_ref, par_ref, hid_ref, cos_ref, feat_ref, taps_ref = arrays
    gb_ref, ig_ref, small_ref, y_ref, vh_ref, vl_ref, g_ref, sems = rest[36:]
    first = [pltpu.make_async_copy(arrays_hbm[k], arrays[k], sems.at[k]) for k in range(9)]
    table = [pltpu.make_async_copy(tabs_hbm[k], tabs[k], sems.at[9 + k]) for k in range(8)]
    for copy in (*first[:2], *table, *first[2:]):
        copy.start()
    wait_for(first, 0, 1)
    early = recv_ref[:, :, ROWS + HALO : ROWS + HALO + LANES].astype(F32)
    late = recv_ref[:, :, ROWS + HALO + LANES :].astype(F32)
    edge = recv_ref[:, :, ROWS : ROWS + HALO].astype(F32)
    edge = jnp.concatenate([edge[1:], jnp.zeros((1, OWN, LANES), F32)], axis=0)
    grad_active = jnp.concatenate([early, late + edge], axis=0)
    slope = gelu_parts(before_ref[...])[1].reshape(STEPS, OWN, LANES)
    grad = (grad_active * slope).astype(BF16).astype(F32)
    gb_ref[...] = grad.reshape(STACK, LANES)
    x = jnp.concatenate([recv_ref[:, :, :LANES].astype(F32), recv_ref[:, :, LANES:ROWS].astype(F32)], axis=0)
    skip = jnp.sum(jnp.sum(grad * x, axis=0), axis=1, keepdims=True)
    spec = spectrum(gb_ref, vh_ref, vl_ref, tabs, table)
    wait_for(first, 2, 3, 4)
    from_spectrum(product(tspec_ref[...], spec, True), y_ref, tabs, table)
    gain = par_ref[:, FEAT + 1 : FEAT + 2][None]
    result = (y_ref[...].reshape(STEPS, OWN, LANES) + gain * grad).astype(BF16)
    ig_ref[:, :, :LANES] = result[:SHARDS]
    ig_ref[:, :, LANES:] = result[SHARDS:]
    save = pltpu.make_async_copy(ig_ref, ig_hbm, sems.at[17])
    save.start()
    from_spectrum(product(xspec_ref[...], spec, True), y_ref, tabs)
    for a in range(STEPS):
        row = ((a % 2) * SHARDS + a // 2) * OWN
        g_ref[:, a * LANES : (a + 1) * LANES] = y_ref[row : row + OWN, :]
    wf_high, wf_low = split(par_ref[:, :FEAT])
    wf = jnp.concatenate([wf_high, wf_low, wf_high], axis=0)
    rates = par_ref[:, FEAT : FEAT + 1]
    wait_for(first, 5, 6, 7, 8)
    filt = jnp.zeros((2 * OWN, 2 * FEAT), F32)
    pos = jnp.zeros((2 * FEAT, 2 * FEAT), F32)
    rate = jnp.zeros((OWN, 1), F32)
    for start in range(0, LENGTH, BLOCK):
        cut = slice(start, start + BLOCK)
        grad_taps = g_ref[:, cut]
        decay, steps = envelope(rates, start, BLOCK)
        high, low = split(grad_taps * decay)
        rate = rate + jnp.sum(grad_taps * taps_ref[:, cut] * (0.5 - rates * steps), axis=1, keepdims=True)
        filt = filt + mul(jnp.concatenate([high, low], axis=0), hid_ref[:, cut], ((1,), (1,)))
        inner = mul(wf, jnp.concatenate([high, high, low], axis=0), ((0,), (0,))) * cos_ref[:, cut]
        pos = pos + mul(feat_ref[:, cut], jnp.concatenate(split(inner), axis=0), ((1,), (1,)))
    filt = filt[:OWN, :FEAT] + filt[OWN:, :FEAT] + filt[:OWN, FEAT:]
    pos = pos[:FEAT, :FEAT] + pos[FEAT:, :FEAT] + pos[:FEAT, FEAT:]
    small_ref[...] = jnp.zeros((2, 2 * OWN, LANES), F32)
    for e, stat in enumerate((rate, skip)):
        small_ref[e, :OWN, :32] = filt[:, 32 * e : 32 * e + 32]
        small_ref[e, :OWN, 32:33] = stat
        small_ref[e, OWN:, :FEAT] = pos[32 * e : 32 * e + 16]
        small_ref[e, OWN:, FEAT:] = pos[32 * e + 16 : 32 * e + 32]
    small_save = pltpu.make_async_copy(small_ref, small_hbm, sems.at[18])
    small_save.start()
    save.wait()
    small_save.wait()


def conv_kernel(
    act_hbm, peer_act_hbm, cot_hbm, peer_cot_hbm, ig_hbm, small_hbm, peer_small_hbm, out_hbm,
    act_ref, cot_ref, ig_ref, small_ref, pad_ref, part_ref, tile_ref, sems,
):
    core = lax.axis_index("batch") % 2
    half = pl.ds(pl.multiple_of(core * HALF, HALF), HALF)
    sources = [
        (cot_hbm.at[:, half], cot_ref.at[0]),
        (peer_cot_hbm.at[:, half], cot_ref.at[1]),
        (act_hbm, act_ref.at[0]),
        (peer_act_hbm, act_ref.at[1]),
        (ig_hbm, ig_ref),
        (small_hbm.at[core], small_ref.at[0]),
        (peer_small_hbm.at[core], small_ref.at[1]),
    ]
    loads = [pltpu.make_async_copy(a, b, sems.at[k]) for k, (a, b) in enumerate(sources)]
    for load in loads:
        load.start()
    pad_ref[:, :HALO, :] = jnp.zeros((2, HALO, HALF), F32)
    pad_ref[:, HALO + ROWS :, :] = jnp.zeros((2, 8, HALF), F32)
    wait_for(loads, 0, 1)
    pad_ref[:, HALO : HALO + ROWS, :] = cot_ref[...].astype(F32)
    wait_for(loads, 2, 3)
    copies = []
    for i in range(KERNEL):
        own = pad_ref[0, i : i + SPAN, :].astype(BF16)
        peer = pad_ref[1, i : i + SPAN, :].astype(BF16)
        both = jnp.concatenate([own, peer], axis=0)
        for r in range(0, WIDTH, CHUNK):
            rows = slice(r, r + CHUNK)
            wide = jnp.concatenate([act_ref[0, rows, :], act_ref[1, rows, :]], axis=1)
            part_ref[i, rows, :] = mul(wide, both).astype(BF16)
        copies.append(pltpu.make_async_copy(part_ref.at[i], out_hbm.at[:, pl.ds(i * HALF, HALF)], sems.at[9 + i]))
        copies[-1].start()
        if i == 0:
            wait_for(loads, 4, 5, 6)
            tile_ref[:, :ROWS] = ig_ref[...]
            small = small_ref[0] + small_ref[1]
            high, low = split(small[:OWN])
            filt = high.astype(F32) + pltpu.roll(low.astype(F32), FEAT, 1)
            tile = jnp.concatenate([filt, small[OWN:]], axis=1).astype(BF16)
            for p in range(SHARDS):
                tile_ref[p * OWN : (p + 1) * OWN, ROWS:] = tile
            target = out_hbm.at[:, pl.ds(CONV, ROWS + 2 * LANES)]
            copies.append(pltpu.make_async_copy(tile_ref, target, sems.at[9 + KERNEL]))
            copies[-1].start()
    for copy in copies:
        copy.wait()


def mixed_kernel(act_hbm, w_hbm, _, out_hbm, act_ref, w_ref, part_ref, out_ref, sems):
    loads = [pltpu.make_async_copy(w_hbm.at[i], w_ref.at[i], sems.at[i]) for i in range(KERNEL)]
    loads.append(pltpu.make_async_copy(act_hbm, act_ref, sems.at[KERNEL]))
    for load in loads:
        load.start()
    wait_for(loads, KERNEL)
    act = jnp.transpose(act_ref[...].astype(F32)).astype(BF16)[HALO - EDGE :]
    total = jnp.zeros((ROWS, WIDTH), F32)
    for i in range(KERNEL):
        wait_for(loads, i)
        part_ref[...] = mul(act, w_ref[i])
        total = total + part_ref[EDGE - i : EDGE - i + ROWS, :]
    out_ref[...] = total.astype(BF16)
    save = pltpu.make_async_copy(out_ref, out_hbm, sems.at[KERNEL + 1])
    save.start()
    save.wait()


def fold(block):
    return jnp.concatenate([block[:8], block[8:]], axis=1)


def two_parts(rows):
    high, low = split(rows)
    return jnp.concatenate([high.astype(F32), low.astype(F32)], axis=0)


def gather_kernel(recv_ref, out_ref):
    conv = jnp.sum(recv_ref[:, :, :CONV].astype(F32), axis=0)
    blocks = [conv[:, :WIDTH], conv[:, WIDTH : 2 * WIDTH], fold(conv[:, 2 * WIDTH :])]
    base = CONV + ROWS
    both = recv_ref[:, :, base : base + LANES].astype(F32).reshape(WIDTH, LANES)
    filt = jnp.transpose(both + pltpu.roll(both, FEAT, 1))
    pos = jnp.sum(recv_ref[:, :, base + LANES : base + 2 * LANES].astype(F32), axis=0)
    stat = filt[32:33]
    pieces = [stat[:, j * LANES : (j + 1) * LANES] for j in range(4)]
    last = jnp.concatenate([fold(pos), two_parts(jnp.concatenate(pieces, axis=0)), jnp.zeros((8, LANES), F32)], axis=1)
    out_ref[...] = jnp.concatenate([*blocks, filt[:32], last], axis=0).astype(BF16)


def pair_kernel(own_ref, other_ref, out_ref):
    total = own_ref[...].astype(F32) + other_ref[...].astype(F32)
    last = total[72:]
    stat = last[:4, HALF : HALF + LANES] + last[4:, HALF : HALF + LANES]
    last = jnp.concatenate([last[:, :HALF], two_parts(stat), last[:, HALF + LANES :]], axis=1)
    out_ref[...] = jnp.concatenate([total[:72], last], axis=0).astype(BF16)


def final_kernel(own_ref, other_ref, out_ref):
    out_ref[...] = (own_ref[...].astype(F32) + other_ref[...].astype(F32)) * SCALE


def input_kernel(recv_ref, out_hbm, out_ref, sem):
    out_ref[...] = jnp.transpose(recv_ref[:, :, CONV : CONV + ROWS].astype(F32).reshape(WIDTH, ROWS)).astype(BF16)
    save = pltpu.make_async_copy(out_ref, out_hbm, sem)
    save.start()
    save.wait()


def join_kernel(mine_ref, other_ref, conv_ref, pos_ref, filt_ref, rates_ref, skip_ref):
    core = lax.axis_index("batch") % 2

    def write(low, high):
        for e, part in enumerate((low, high)):
            lanes = slice(e * HALF, (e + 1) * HALF)
            for i in range(KERNEL - 1):
                row, lane = 16 * (i // 2), HALF * (i % 2)
                conv_ref[i, :, lanes] = part[row : row + 16, lane : lane + HALF]
            conv_ref[KERNEL - 1, :8, lanes] = part[32:40, :HALF]
            conv_ref[KERNEL - 1, 8:, lanes] = part[32:40, HALF:]
            filt_ref[32 * e : 32 * e + 32, :] = part[40:72, :]
            for j in range(2):
                pos = part[72:80, j * LANES : (j + 1) * LANES]
                pos_ref[32 * e + 8 * j : 32 * e + 8 * j + 8, :] = pos[:, :FEAT]
                pos_ref[32 * e + 16 + 8 * j : 32 * e + 24 + 8 * j, :] = pos[:, FEAT:]
            for j in range(4):
                stat = part[72 + j : 73 + j, HALF : HALF + LANES] + part[76 + j : 77 + j, HALF : HALF + LANES]
                (rates_ref, skip_ref)[e][:, j * LANES : (j + 1) * LANES] = stat

    @pl.when(core == 0)
    def _():
        write(mine_ref, other_ref)

    @pl.when(core == 1)
    def _():
        write(other_ref, mine_ref)


VMEM = pl.BlockSpec(memory_space=pltpu.VMEM)
HBM = pl.BlockSpec(memory_space=pltpu.HBM)


def call(kernel, out_shape, args, scratch=(), flops=0, name=None, specs=None, out_specs=None, limit=60):
    single = not isinstance(out_shape, (list, tuple))
    outs = [out_shape] if single else out_shape
    moved = sum(math.prod(a.shape) * a.dtype.itemsize for a in (*args, *outs))
    return pl.pallas_call(
        kernel,
        out_shape=out_shape,
        in_specs=specs or [VMEM] * len(args),
        out_specs=out_specs or (VMEM if single else [VMEM] * len(outs)),
        scratch_shapes=list(scratch),
        compiler_params=pltpu.CompilerParams(vmem_limit_bytes=limit * 1024 * 1024),
        cost_estimate=pl.CostEstimate(flops=flops, bytes_accessed=moved, transcendentals=0),
        name=name,
    )(*args)


def shape(dims, kind=F32):
    return jax.ShapeDtypeStruct(dims, kind)


def regroup(blocks):
    return lax.all_to_all(blocks, "tm", split_axis=0, concat_axis=0, tiled=True)


def on_device(inputs, cotangent, w_pos, w_filt, log_rates, skip_gain, w_conv):
    swap = [(i, i ^ 1) for i in range(lax.axis_size("batch"))]
    signal, upstream = inputs[0], cotangent[0]
    w_taps = jnp.transpose(w_conv, (1, 0, 2))
    tabs = tuple(jnp.asarray(t) for t in transform_tables())
    feat = jnp.asarray(np.concatenate(feature_tables(), axis=0))

    message = call(
        prep_kernel,
        shape((WIDTH, ROWS + SPAN), BF16),
        (signal, upstream, w_taps),
        [
            pltpu.VMEM((ROWS, WIDTH), BF16),
            pltpu.VMEM((ROWS, WIDTH), BF16),
            pltpu.VMEM((KERNEL, WIDTH, WIDTH), BF16),
            pltpu.VMEM((EDGE + ROWS + 8, WIDTH), F32),
            pltpu.VMEM((SPAN, WIDTH), F32),
            pltpu.VMEM((WIDTH, ROWS), BF16),
            pltpu.VMEM((WIDTH, SPAN), BF16),
            pltpu.SemaphoreType.DMA((4 + KERNEL,)),
        ],
        flops=2 * KERNEL * WIDTH * WIDTH * (ROWS + EDGE),
        name="prep",
        specs=[HBM] * 3,
        out_specs=HBM,
    )
    received = regroup(message.reshape(SHARDS, OWN, ROWS + SPAN))
    cot_peer = lax.ppermute(upstream, "batch", swap)
    received, cot_peer = lax.optimization_barrier((received, cot_peer))

    stack = pltpu.VMEM((STACK, LANES), F32)
    wide = pltpu.VMEM((STACK, 2 * LANES), BF16)
    saved = [pltpu.VMEM((2 * FEAT, LENGTH), BF16), pltpu.VMEM((FEAT, LENGTH), F32), pltpu.VMEM((OWN, LENGTH), F32)]
    flops = 2 * 3 * (2 * STACK * LANES * LANES + STACK * 4 * LANES * LANES)
    hidden, cosines, taps, tap_spec, par = call(
        taps_kernel,
        [
            shape((2 * FEAT, LENGTH), BF16),
            shape((FEAT, LENGTH)),
            shape((OWN, LENGTH)),
            shape((STACK, 2 * LANES)),
            shape((OWN, LANES)),
        ],
        (w_pos, w_filt, log_rates[None], skip_gain[None], feat, *tabs),
        [*saved, pltpu.VMEM((STACK, 2 * LANES), F32), pltpu.VMEM((OWN, LANES), F32), stack, wide, wide, pltpu.SemaphoreType.DMA((5,))],
        flops=flops * 2,
        name="taps",
        out_specs=[HBM] * 5,
    )
    act_message, before, sig_spec = call(
        forward_kernel,
        [shape((SHARDS, OWN, SPAN), BF16), shape((STACK, LANES)), shape((STACK, 2 * LANES))],
        (received, tap_spec, par, *tabs),
        [
            pltpu.VMEM((SHARDS, OWN, ROWS), BF16),
            pltpu.VMEM((STACK, 2 * LANES), F32),
            pltpu.VMEM((STACK, 2 * LANES), F32),
            pltpu.VMEM((SHARDS, OWN, SPAN), BF16),
            *[pltpu.VMEM(t.shape, t.dtype) for t in tabs],
            stack,
            stack,
            wide,
            wide,
            pltpu.VMEM((OWN, LANES), F32),
            pltpu.SemaphoreType.DMA((14,)),
        ],
        flops=flops * 2,
        name="forward",
        specs=[HBM] * 11,
        out_specs=[HBM] * 3,
    )
    act = regroup(act_message).reshape(WIDTH, SPAN)
    ig_message, small = call(
        backward_kernel,
        [shape((SHARDS, OWN, ROWS), BF16), shape((2, 2 * OWN, LANES))],
        (received, before, sig_spec, tap_spec, par, hidden, cosines, feat, taps, *tabs),
        [
            pltpu.VMEM((SHARDS, OWN, ROWS + SPAN), BF16),
            stack,
            pltpu.VMEM((STACK, 2 * LANES), F32),
            pltpu.VMEM((STACK, 2 * LANES), F32),
            pltpu.VMEM((OWN, LANES), F32),
            *saved[:2],
            saved[0],
            saved[2],
            *[pltpu.VMEM(t.shape, t.dtype) for t in tabs],
            stack,
            pltpu.VMEM((SHARDS, OWN, ROWS), BF16),
            pltpu.VMEM((2, 2 * OWN, LANES), F32),
            stack,
            wide,
            wide,
            pltpu.VMEM((OWN, LENGTH), F32),
            pltpu.SemaphoreType.DMA((19,)),
        ],
        flops=flops * 4,
        name="backward",
        specs=[HBM] * 17,
        out_specs=[HBM] * 2,
    )
    act, ig_message, small = lax.optimization_barrier((act, ig_message, small))
    act_peer = lax.ppermute(act, "batch", swap)
    small_peer = lax.ppermute(small, "batch", swap)
    lanes = CONV + ROWS + 2 * LANES
    sums = call(
        conv_kernel,
        shape((WIDTH, lanes), BF16),
        (act, act_peer, upstream, cot_peer, ig_message.reshape(WIDTH, ROWS), small, small_peer),
        [
            pltpu.VMEM((2, WIDTH, SPAN), BF16),
            pltpu.VMEM((2, ROWS, HALF), BF16),
            pltpu.VMEM((WIDTH, ROWS), BF16),
            pltpu.VMEM((2, 2 * OWN, LANES), F32),
            pltpu.VMEM((2, HALO + ROWS + 8, HALF), F32),
            pltpu.VMEM((KERNEL, WIDTH, HALF), BF16),
            pltpu.VMEM((WIDTH, ROWS + 2 * LANES), BF16),
            pltpu.SemaphoreType.DMA((10 + KERNEL,)),
        ],
        flops=2 * KERNEL * WIDTH * HALF * 2 * ROWS,
        name="conv_grad",
        specs=[HBM] * 7,
        out_specs=HBM,
    )
    spread = regroup(sums.reshape(SHARDS, OWN, lanes))
    mixed = call(
        mixed_kernel,
        shape((ROWS, WIDTH), BF16),
        (act, w_taps, sums),
        [
            pltpu.VMEM((WIDTH, SPAN), BF16),
            pltpu.VMEM((KERNEL, WIDTH, WIDTH), BF16),
            pltpu.VMEM((ROWS + EDGE, WIDTH), F32),
            pltpu.VMEM((ROWS, WIDTH), BF16),
            pltpu.SemaphoreType.DMA((2 + KERNEL,)),
        ],
        flops=2 * KERNEL * WIDTH * WIDTH * (ROWS + EDGE),
        name="mixed",
        specs=[HBM] * 3,
        out_specs=HBM,
    )
    spread, mixed = lax.optimization_barrier((spread, mixed))
    payload = call(gather_kernel, shape((80, WIDTH), BF16), (spread,), name="gather", limit=12)
    met = lax.ppermute(payload, "batch", [(i, i ^ 2) for i in range(8)])
    pair = call(pair_kernel, shape((80, WIDTH), BF16), (payload, met), name="pair", limit=12)
    met = lax.ppermute(pair, "batch", [(i, i ^ 6) for i in range(8)])
    spread, pair = lax.optimization_barrier((spread, pair))
    input_grad = call(
        input_kernel,
        shape((ROWS, WIDTH), BF16),
        (spread,),
        [pltpu.VMEM((ROWS, WIDTH), BF16), pltpu.SemaphoreType.DMA],
        name="input",
        out_specs=HBM,
        limit=12,
    )
    pair, input_grad = lax.optimization_barrier((pair, input_grad))
    mine = call(final_kernel, shape((80, WIDTH)), (pair, met), name="final", limit=12)
    other = lax.ppermute(mine, "batch", swap)
    conv_grad, pos_grad, filt_grad, rates_grad, skip_grad = call(
        join_kernel,
        [
            shape((KERNEL, OWN, WIDTH)),
            shape((FEAT, FEAT)),
            shape((FEAT, WIDTH)),
            shape((1, WIDTH)),
            shape((1, WIDTH)),
        ],
        (mine, other),
        name="join",
        limit=12,
    )
    return (
        mixed[None],
        input_grad[None],
        jnp.transpose(conv_grad, (1, 0, 2)),
        pos_grad,
        filt_grad,
        rates_grad[0],
        skip_grad[0],
    )


def solution(mesh):
    in_specs = (P("batch", "tm", None), P("batch", "tm", None), P(), P(), P(), P(), P())
    out_specs = (P("batch", "tm", None), P("batch", "tm", None), P("tm", None, None), P(), P(), P(), P())
    return jax.shard_map(on_device, mesh=mesh, in_specs=in_specs, out_specs=out_specs, check_vma=False)
```

```python
import math

import jax
import jax.numpy as jnp
import ml_dtypes
import numpy as np
from jax import lax
from jax.experimental import pallas as pl
from jax.experimental.pallas import tpu as pltpu
from jax.sharding import PartitionSpec as P

F32 = jnp.float32
BF16 = jnp.bfloat16

SHARDS = 32
ROWS = 256
LENGTH = SHARDS * ROWS
WIDTH = 512
KERNEL = 5
FEAT = 64
OWN = WIDTH // SHARDS
LANES = 128
STEPS = LENGTH // LANES
STACK = STEPS * OWN
HALO = LANES
SPAN = ROWS + HALO
HALF = WIDTH // 2
EDGE = 16
CONV = KERNEL * HALF
BLOCK = 4096
CHUNK = 128
SLICE = 8
SCALE = 1.0 / math.sqrt(8 * LENGTH)


def split_table(values):
    high = values.astype(ml_dtypes.bfloat16)
    low = (values - high.astype(np.float64)).astype(ml_dtypes.bfloat16)
    return high, low


def feature_tables():
    half = FEAT // 2
    factor = np.array([1 + i * i * LENGTH // (2 * half * half) for i in range(half)], dtype=np.int64)
    steps = np.arange(LENGTH, dtype=np.int64)
    angles = 2.0 * np.pi * ((factor[:, None] * steps[None, :]) % LENGTH) / LENGTH
    return split_table(np.concatenate([np.sin(angles), np.cos(angles)], axis=0))


def transform_tables():
    order = np.array([2 * p + h for h in range(2) for p in range(STEPS // 2)])
    k1 = np.arange(STEPS)
    alpha = np.pi * order[None, :] / STEPS / 2 - 2.0 * np.pi * ((order[None, :] * k1[:, None]) % STEPS) / STEPS
    outer = np.concatenate([np.cos(alpha), np.sin(alpha)], axis=0)
    outer_high, outer_low = split_table(outer)
    first = np.concatenate([outer_high, outer_low], axis=1)
    back_high, back_low = split_table(outer.T / LENGTH)
    last = np.concatenate([back_high, back_low, back_high], axis=1)
    b = np.arange(LANES)
    beta = np.pi * b[None, :] / (2 * LENGTH) - 2.0 * np.pi * ((b[None, :] * k1[:, None]) % LENGTH) / LENGTH
    twist_cos = np.cos(beta).astype(np.float32)
    twist_sin = np.sin(beta).astype(np.float32)
    gamma = 2.0 * np.pi * ((b[:, None] * b[None, :]) % LANES) / LANES
    cos, sin = np.cos(gamma), np.sin(gamma)
    ahead = split_table(np.block([[cos, -sin], [sin, cos]]))
    behind = split_table(np.block([[cos, sin], [-sin, cos]]))
    return (first, last, twist_cos, twist_sin, *ahead, *behind)


def split(values):
    high = values.astype(BF16)
    return high, (values - high.astype(F32)).astype(BF16)


def mul(left, right, dims=((1,), (0,))):
    return lax.dot_general(left, right, (dims, ((), ())), preferred_element_type=F32)


def mul3(left, right, dims=((1,), (0,))):
    lh, ll = left
    rh, rl = right
    return mul(lh, rh, dims) + mul(ll, rh, dims) + mul(lh, rl, dims)


def wait_for(loads, *which):
    for k in which:
        if loads is not None:
            loads[k].wait()


def spectrum(stack_ref, high_ref, low_ref, tabs, loads=None):
    first, _, tc_ref, ts_ref, ahead_high, ahead_low, _, _ = tabs
    wait_for(loads, 0, 2, 3)
    tc, ts = tc_ref[...], ts_ref[...]
    for c in range(0, OWN, 2):
        pair = [stack_ref[pl.ds(c + k, STEPS, stride=OWN), :] for k in range(2)]
        wide = jnp.concatenate(pair, axis=1).astype(BF16)
        u = mul(first[...], jnp.concatenate([wide, wide], axis=0))
        for k in range(2):
            ur = u[:STEPS, k * LANES : (k + 1) * LANES]
            ui = u[STEPS:, k * LANES : (k + 1) * LANES]
            v = jnp.concatenate([ur * tc - ui * ts, ur * ts + ui * tc], axis=1)
            high, low = split(v)
            high_ref[(c + k) * STEPS : (c + k + 1) * STEPS, :] = high
            low_ref[(c + k) * STEPS : (c + k + 1) * STEPS, :] = low
    wait_for(loads, 4, 5)
    table = (ahead_high[...], ahead_low[...])
    parts = [mul3((high_ref[r : r + CHUNK, :], low_ref[r : r + CHUNK, :]), table) for r in range(0, STACK, CHUNK)]
    return jnp.concatenate(parts, axis=0)


def from_spectrum(values, stack_ref, tabs, loads=None):
    _, last, tc_ref, ts_ref, _, _, behind_high, behind_low = tabs
    wait_for(loads, 6, 7, 1)
    tc, ts = tc_ref[...], ts_ref[...]
    table = (behind_high[...], behind_low[...])
    q = jnp.concatenate([mul3(split(values[r : r + CHUNK]), table) for r in range(0, STACK, CHUNK)], axis=0)
    for c in range(0, OWN, 2):
        pair = []
        for k in range(2):
            rows = q[(c + k) * STEPS : (c + k + 1) * STEPS]
            qr, qi = rows[:, :LANES], rows[:, LANES:]
            pair.append(jnp.concatenate([qr * tc + qi * ts, qi * tc - qr * ts], axis=0))
        high, low = split(jnp.concatenate(pair, axis=1))
        y = mul(last[...], jnp.concatenate([high, high, low], axis=0))
        for k in range(2):
            stack_ref[pl.ds(c + k, STEPS, stride=OWN), :] = y[:, k * LANES : (k + 1) * LANES]


def product(left, right, conjugate):
    lr, li = left[:, :LANES], left[:, LANES:]
    rr, ri = right[:, :LANES], right[:, LANES:]
    if conjugate:
        return jnp.concatenate([lr * rr + li * ri, lr * ri - li * rr], axis=1)
    return jnp.concatenate([lr * rr - li * ri, lr * ri + li * rr], axis=1)


def sin_cos(x):
    turns = jnp.floor(x * (2.0 / math.pi) + 0.5)
    r = x - turns * 1.5703125
    r = r - turns * 4.837512969970703125e-4
    r = r - turns * 7.549789948768648e-8
    z = r * r
    s = r + r * z * (-1.6666654611e-1 + z * (8.3321608736e-3 - z * 1.9515295891e-4))
    c = 1.0 - 0.5 * z + z * z * (4.166664568298827e-2 + z * (-1.388731625493765e-3 + z * 2.443315711809948e-5))
    quad = turns.astype(jnp.int32)
    odd = (quad & 1) == 1
    sin = jnp.where(odd, c, s)
    cos = jnp.where(odd, s, c)
    sin = jnp.where((quad & 2) == 2, -sin, sin)
    cos = jnp.where(((quad + 1) & 2) == 2, -cos, cos)
    return sin, cos


def envelope(rates, start, size):
    steps = (start + lax.broadcasted_iota(jnp.int32, (OWN, size), 1)).astype(F32)
    return jnp.sqrt(rates) * jnp.exp(-steps * rates), steps


def prep_kernel(x_hbm, cot_hbm, w_hbm, out_hbm, x_ref, cot_ref, w_ref, pad_ref, sum_ref, xt_ref, ga_ref, sems):
    x_copy = pltpu.make_async_copy(x_hbm, x_ref, sems.at[0])
    x_copy.start()
    cot_copy = pltpu.make_async_copy(cot_hbm, cot_ref, sems.at[1])
    cot_copy.start()
    w_copies = [pltpu.make_async_copy(w_hbm.at[i], w_ref.at[i], sems.at[2 + i]) for i in range(KERNEL)]
    for copy in w_copies:
        copy.start()
    pad_ref[:EDGE, :] = jnp.zeros((EDGE, WIDTH), F32)
    pad_ref[EDGE + ROWS :, :] = jnp.zeros((8, WIDTH), F32)
    x_copy.wait()
    xt_ref[...] = jnp.transpose(x_ref[...].astype(F32)).astype(BF16)
    x_out = pltpu.make_async_copy(xt_ref, out_hbm.at[:, pl.ds(0, ROWS)], sems.at[2 + KERNEL])
    x_out.start()
    cot_copy.wait()
    pad_ref[EDGE : EDGE + ROWS, :] = cot_ref[...].astype(F32)
    for i in range(KERNEL):
        shifted = pad_ref[i : i + EDGE + ROWS, :].astype(BF16)
        w_copies[i].wait()
        part = mul(shifted, w_ref[i], ((1,), (1,)))
        if i == 0:
            sum_ref[HALO - EDGE :, :] = part
        else:
            sum_ref[HALO - EDGE :, :] += part
    sum_ref[: HALO - EDGE, :] = jnp.zeros((HALO - EDGE, WIDTH), F32)
    ga_ref[...] = jnp.transpose(sum_ref[...]).astype(BF16)
    ga_out = pltpu.make_async_copy(ga_ref, out_hbm.at[:, pl.ds(ROWS, SPAN)], sems.at[3 + KERNEL])
    ga_out.start()
    x_out.wait()
    ga_out.wait()


def taps_kernel(wp_ref, wf_ref, lr_ref, gain_ref, feat_ref, *rest):
    tabs = rest[:8]
    hid_out, cos_out, taps_out, spec_out, par_out = rest[8:13]
    hid_ref, cos_ref, taps_ref, spec_ref, par_ref, stack_ref, vh_ref, vl_ref, sems = rest[13:]
    first = lax.axis_index("tm") * OWN
    lane = lax.broadcasted_iota(jnp.int32, (OWN, WIDTH), 1)
    chosen = lane == first + lax.broadcasted_iota(jnp.int32, (OWN, WIDTH), 0)
    wf_own = lax.dot_general(
        chosen.astype(F32),
        wf_ref[...],
        (((1,), (1,)), ((), ())),
        precision=lax.Precision.HIGHEST,
        preferred_element_type=F32,
    )
    rates = jnp.exp(jnp.sum(jnp.where(chosen, lr_ref[...], 0.0), axis=1, keepdims=True))
    gain = jnp.sum(jnp.where(chosen, gain_ref[...], 0.0), axis=1, keepdims=True)
    spot = lax.broadcasted_iota(jnp.int32, (OWN, LANES), 1)
    par_ref[...] = jnp.where(spot == FEAT, rates, jnp.where(spot == FEAT + 1, gain, 0.0))
    par_ref[:, :FEAT] = wf_own
    wp_high, wp_low = split(wp_ref[...])
    wp = jnp.concatenate([wp_high, wp_low, wp_high], axis=0)
    wf_high, wf_low = split(wf_own)
    for start in range(0, LENGTH, BLOCK):
        cut = slice(start, start + BLOCK)
        feat = feat_ref[:, cut]
        sin, cos = sin_cos(mul(wp, jnp.concatenate([feat[:FEAT], feat], axis=0), ((0,), (0,))))
        high, low = split(sin)
        hid_ref[:FEAT, cut] = high
        hid_ref[FEAT:, cut] = low
        cos_ref[:, cut] = cos
        decay, _ = envelope(rates, start, BLOCK)
        taps = mul3((wf_high, wf_low), (high, low)) * decay
        taps_ref[:, cut] = taps
        rounded = taps.astype(BF16).astype(F32)
        for j in range(BLOCK // LANES):
            a = start // LANES + j
            row = ((a % 2) * SHARDS + a // 2) * OWN
            stack_ref[row : row + OWN, :] = rounded[:, j * LANES : (j + 1) * LANES]
    saves = [
        pltpu.make_async_copy(source, target, sems.at[k])
        for k, (source, target) in enumerate(((hid_ref, hid_out), (cos_ref, cos_out), (taps_ref, taps_out), (par_ref, par_out)))
    ]
    for save in saves:
        save.start()
    spec_ref[...] = spectrum(stack_ref, vh_ref, vl_ref, tabs)
    saves.append(pltpu.make_async_copy(spec_ref, spec_out, sems.at[4]))
    saves[-1].start()
    for save in saves:
        save.wait()


def gelu_parts(before):
    root = math.sqrt(2.0 / math.pi)
    square = before * before
    th = jnp.tanh(root * (before + 0.044715 * square * before))
    half_cdf = 0.5 * (1.0 + th)
    slope = half_cdf + 0.5 * before * (1.0 - th * th) * (root * (1.0 + 3.0 * 0.044715 * square))
    return before * half_cdf, slope


def forward_kernel(recv_hbm, tspec_hbm, par_hbm, *rest):
    tabs_hbm = rest[:8]
    act_hbm, before_hbm, xspec_hbm = rest[8:11]
    xin_ref, tspec_ref, spec_ref, act_ref = rest[11:15]
    tabs = rest[15:23]
    x_ref, y_ref, vh_ref, vl_ref, par_ref, sems = rest[23:]
    x_load = pltpu.make_async_copy(recv_hbm.at[:, :, pl.ds(0, ROWS)], xin_ref, sems.at[0])
    x_load.start()
    loads = [pltpu.make_async_copy(tabs_hbm[k], tabs[k], sems.at[1 + k]) for k in range(8)]
    for k in (0, 2, 3, 4, 5, 6, 7, 1):
        loads[k].start()
    tspec_load = pltpu.make_async_copy(tspec_hbm, tspec_ref, sems.at[9])
    tspec_load.start()
    par_load = pltpu.make_async_copy(par_hbm, par_ref, sems.at[10])
    par_load.start()
    x_load.wait()
    for h in range(2):
        part = xin_ref[:, :, h * LANES : (h + 1) * LANES].astype(F32)
        x_ref[h * STACK // 2 : (h + 1) * STACK // 2, :] = part.reshape(STACK // 2, LANES)
    spec = spectrum(x_ref, vh_ref, vl_ref, tabs, loads)
    spec_ref[...] = spec
    spec_save = pltpu.make_async_copy(spec_ref, xspec_hbm, sems.at[11])
    spec_save.start()
    tspec_load.wait()
    from_spectrum(product(tspec_ref[...], spec, False), y_ref, tabs, loads)
    par_load.wait()
    gain = par_ref[:, FEAT + 1 : FEAT + 2][None]
    act_ref[0, :, :HALO] = jnp.zeros((OWN, LANES), BF16)
    for p in range(0, STEPS, SLICE):
        rows = slice(p * OWN, (p + SLICE) * OWN)
        before = y_ref[rows, :].reshape(SLICE, OWN, LANES) + gain * x_ref[rows, :].reshape(SLICE, OWN, LANES)
        y_ref[rows, :] = before.reshape(SLICE * OWN, LANES)
        active = gelu_parts(before)[0].astype(BF16)
        h, at = divmod(p, SHARDS)
        act_ref[at : at + SLICE, :, HALO + h * LANES : HALO + (h + 1) * LANES] = active
        if h == 1:
            kept = min(SLICE, SHARDS - 1 - at)
            act_ref[at + 1 : at + 1 + kept, :, :HALO] = active[:kept]
    before_save = pltpu.make_async_copy(y_ref, before_hbm, sems.at[12])
    before_save.start()
    act_save = pltpu.make_async_copy(act_ref, act_hbm, sems.at[13])
    act_save.start()
    spec_save.wait()
    before_save.wait()
    act_save.wait()


def backward_kernel(*rest):
    arrays_hbm, tabs_hbm = rest[:9], rest[9:17]
    ig_hbm, small_hbm = rest[17:19]
    arrays, tabs = rest[19:28], rest[28:36]
    recv_ref, before_ref, xspec_ref, tspec_ref, par_ref, hid_ref, cos_ref, feat_ref, taps_ref = arrays
    gb_ref, ig_ref, small_ref, y_ref, vh_ref, vl_ref, g_ref, sems = rest[36:]
    first = [pltpu.make_async_copy(arrays_hbm[k], arrays[k], sems.at[k]) for k in range(9)]
    table = [pltpu.make_async_copy(tabs_hbm[k], tabs[k], sems.at[9 + k]) for k in range(8)]
    for copy in (*first[:2], *table, *first[2:]):
        copy.start()
    wait_for(first, 0, 1)
    skip = jnp.zeros((OWN, LANES), F32)
    for p in range(0, STEPS, SLICE):
        rows = slice(p * OWN, (p + SLICE) * OWN)
        h, at = divmod(p, SHARDS)
        part = slice(at, at + SLICE)
        grad = recv_ref[part, :, ROWS + HALO + h * LANES : ROWS + HALO + (h + 1) * LANES].astype(F32)
        if h == 1:
            edge = recv_ref[at + 1 : min(at + 1 + SLICE, SHARDS), :, ROWS : ROWS + HALO].astype(F32)
            if at + SLICE == SHARDS:
                edge = jnp.concatenate([edge, jnp.zeros((1, OWN, LANES), F32)], axis=0)
            grad = grad + edge
        grad = grad * gelu_parts(before_ref[rows, :].reshape(SLICE, OWN, LANES))[1]
        grad = grad.astype(BF16).astype(F32)
        gb_ref[rows, :] = grad.reshape(SLICE * OWN, LANES)
        skip = skip + jnp.sum(grad * recv_ref[part, :, h * LANES : (h + 1) * LANES].astype(F32), axis=0)
    skip = jnp.sum(skip, axis=1, keepdims=True)
    spec = spectrum(gb_ref, vh_ref, vl_ref, tabs, table)
    wait_for(first, 2, 3, 4)
    from_spectrum(product(tspec_ref[...], spec, True), y_ref, tabs, table)
    gain = par_ref[:, FEAT + 1 : FEAT + 2][None]
    for p in range(0, STEPS, SLICE):
        rows = slice(p * OWN, (p + SLICE) * OWN)
        h, at = divmod(p, SHARDS)
        result = y_ref[rows, :].reshape(SLICE, OWN, LANES) + gain * gb_ref[rows, :].reshape(SLICE, OWN, LANES)
        ig_ref[at : at + SLICE, :, h * LANES : (h + 1) * LANES] = result.astype(BF16)
    save = pltpu.make_async_copy(ig_ref, ig_hbm, sems.at[17])
    save.start()
    from_spectrum(product(xspec_ref[...], spec, True), y_ref, tabs)
    for a in range(STEPS):
        row = ((a % 2) * SHARDS + a // 2) * OWN
        g_ref[:, a * LANES : (a + 1) * LANES] = y_ref[row : row + OWN, :]
    wf_high, wf_low = split(par_ref[:, :FEAT])
    wf = jnp.concatenate([wf_high, wf_low, wf_high], axis=0)
    rates = par_ref[:, FEAT : FEAT + 1]
    wait_for(first, 5, 6, 7, 8)
    filt = jnp.zeros((2 * OWN, 2 * FEAT), F32)
    pos = jnp.zeros((2 * FEAT, 2 * FEAT), F32)
    rate = jnp.zeros((OWN, 1), F32)
    for start in range(0, LENGTH, BLOCK):
        cut = slice(start, start + BLOCK)
        grad_taps = g_ref[:, cut]
        decay, steps = envelope(rates, start, BLOCK)
        high, low = split(grad_taps * decay)
        rate = rate + jnp.sum(grad_taps * taps_ref[:, cut] * (0.5 - rates * steps), axis=1, keepdims=True)
        filt = filt + mul(jnp.concatenate([high, low], axis=0), hid_ref[:, cut], ((1,), (1,)))
        inner = mul(wf, jnp.concatenate([high, high, low], axis=0), ((0,), (0,))) * cos_ref[:, cut]
        pos = pos + mul(feat_ref[:, cut], jnp.concatenate(split(inner), axis=0), ((1,), (1,)))
    filt = filt[:OWN, :FEAT] + filt[OWN:, :FEAT] + filt[:OWN, FEAT:]
    pos = pos[:FEAT, :FEAT] + pos[FEAT:, :FEAT] + pos[:FEAT, FEAT:]
    small_ref[...] = jnp.zeros((2, 2 * OWN, LANES), F32)
    for e, stat in enumerate((rate, skip)):
        small_ref[e, :OWN, :32] = filt[:, 32 * e : 32 * e + 32]
        small_ref[e, :OWN, 32:33] = stat
        small_ref[e, OWN:, :FEAT] = pos[32 * e : 32 * e + 16]
        small_ref[e, OWN:, FEAT:] = pos[32 * e + 16 : 32 * e + 32]
    small_save = pltpu.make_async_copy(small_ref, small_hbm, sems.at[18])
    small_save.start()
    save.wait()
    small_save.wait()


def conv_kernel(
    act_hbm, peer_act_hbm, cot_hbm, peer_cot_hbm, ig_hbm, small_hbm, peer_small_hbm, out_hbm,
    act_ref, cot_ref, ig_ref, small_ref, pad_ref, part_ref, tile_ref, sems,
):
    core = lax.axis_index("batch") % 2
    half = pl.ds(pl.multiple_of(core * HALF, HALF), HALF)
    sources = [
        (cot_hbm.at[:, half], cot_ref.at[0]),
        (peer_cot_hbm.at[:, half], cot_ref.at[1]),
        (act_hbm, act_ref.at[0]),
        (peer_act_hbm, act_ref.at[1]),
        (ig_hbm, ig_ref),
        (small_hbm.at[core], small_ref.at[0]),
        (peer_small_hbm.at[core], small_ref.at[1]),
    ]
    loads = [pltpu.make_async_copy(a, b, sems.at[k]) for k, (a, b) in enumerate(sources)]
    for load in loads:
        load.start()
    pad_ref[:, :HALO, :] = jnp.zeros((2, HALO, HALF), F32)
    pad_ref[:, HALO + ROWS :, :] = jnp.zeros((2, 8, HALF), F32)
    wait_for(loads, 0, 1)
    pad_ref[:, HALO : HALO + ROWS, :] = cot_ref[...].astype(F32)
    wait_for(loads, 2, 3)
    copies = []
    for i in range(KERNEL):
        own = pad_ref[0, i : i + SPAN, :].astype(BF16)
        peer = pad_ref[1, i : i + SPAN, :].astype(BF16)
        both = jnp.concatenate([own, peer], axis=0)
        for r in range(0, WIDTH, CHUNK):
            rows = slice(r, r + CHUNK)
            wide = jnp.concatenate([act_ref[0, rows, :], act_ref[1, rows, :]], axis=1)
            part_ref[i, rows, :] = mul(wide, both).astype(BF16)
        copies.append(pltpu.make_async_copy(part_ref.at[i], out_hbm.at[:, pl.ds(i * HALF, HALF)], sems.at[9 + i]))
        copies[-1].start()
        if i == 0:
            wait_for(loads, 4, 5, 6)
            tile_ref[:, :ROWS] = ig_ref[...]
            small = small_ref[0] + small_ref[1]
            high, low = split(small[:OWN])
            filt = high.astype(F32) + pltpu.roll(low.astype(F32), FEAT, 1)
            tile = jnp.concatenate([filt, small[OWN:]], axis=1).astype(BF16)
            for p in range(SHARDS):
                tile_ref[p * OWN : (p + 1) * OWN, ROWS:] = tile
            target = out_hbm.at[:, pl.ds(CONV, ROWS + 2 * LANES)]
            copies.append(pltpu.make_async_copy(tile_ref, target, sems.at[9 + KERNEL]))
            copies[-1].start()
    for copy in copies:
        copy.wait()


def mixed_kernel(act_hbm, w_hbm, _, out_hbm, act_ref, w_ref, part_ref, out_ref, sems):
    loads = [pltpu.make_async_copy(w_hbm.at[i], w_ref.at[i], sems.at[i]) for i in range(KERNEL)]
    loads.append(pltpu.make_async_copy(act_hbm, act_ref, sems.at[KERNEL]))
    for load in loads:
        load.start()
    wait_for(loads, KERNEL)
    act = jnp.transpose(act_ref[...].astype(F32)).astype(BF16)[HALO - EDGE :]
    total = jnp.zeros((ROWS, WIDTH), F32)
    for i in range(KERNEL):
        wait_for(loads, i)
        part_ref[...] = mul(act, w_ref[i])
        total = total + part_ref[EDGE - i : EDGE - i + ROWS, :]
    out_ref[...] = total.astype(BF16)
    save = pltpu.make_async_copy(out_ref, out_hbm, sems.at[KERNEL + 1])
    save.start()
    save.wait()


def fold(block):
    return jnp.concatenate([block[:8], block[8:]], axis=1)


def two_parts(rows):
    high, low = split(rows)
    return jnp.concatenate([high.astype(F32), low.astype(F32)], axis=0)


def gather_kernel(recv_ref, out_ref):
    conv = jnp.sum(recv_ref[:, :, :CONV].astype(F32), axis=0)
    blocks = [conv[:, :WIDTH], conv[:, WIDTH : 2 * WIDTH], fold(conv[:, 2 * WIDTH :])]
    base = CONV + ROWS
    both = recv_ref[:, :, base : base + LANES].astype(F32).reshape(WIDTH, LANES)
    filt = jnp.transpose(both + pltpu.roll(both, FEAT, 1))
    pos = jnp.sum(recv_ref[:, :, base + LANES : base + 2 * LANES].astype(F32), axis=0)
    stat = filt[32:33]
    pieces = [stat[:, j * LANES : (j + 1) * LANES] for j in range(4)]
    last = jnp.concatenate([fold(pos), two_parts(jnp.concatenate(pieces, axis=0)), jnp.zeros((8, LANES), F32)], axis=1)
    out_ref[...] = jnp.concatenate([*blocks, filt[:32], last], axis=0).astype(BF16)


def pair_kernel(own_ref, other_ref, out_ref):
    total = own_ref[...].astype(F32) + other_ref[...].astype(F32)
    last = total[72:]
    stat = last[:4, HALF : HALF + LANES] + last[4:, HALF : HALF + LANES]
    last = jnp.concatenate([last[:, :HALF], two_parts(stat), last[:, HALF + LANES :]], axis=1)
    out_ref[...] = jnp.concatenate([total[:72], last], axis=0).astype(BF16)


def final_kernel(own_ref, other_ref, out_ref):
    out_ref[...] = (own_ref[...].astype(F32) + other_ref[...].astype(F32)) * SCALE


def input_kernel(recv_ref, out_hbm, out_ref, sem):
    out_ref[...] = jnp.transpose(recv_ref[:, :, CONV : CONV + ROWS].astype(F32).reshape(WIDTH, ROWS)).astype(BF16)
    save = pltpu.make_async_copy(out_ref, out_hbm, sem)
    save.start()
    save.wait()


def join_kernel(mine_ref, other_ref, conv_ref, pos_ref, filt_ref, rates_ref, skip_ref):
    core = lax.axis_index("batch") % 2

    def write(low, high):
        for e, part in enumerate((low, high)):
            lanes = slice(e * HALF, (e + 1) * HALF)
            for i in range(KERNEL - 1):
                row, lane = 16 * (i // 2), HALF * (i % 2)
                conv_ref[i, :, lanes] = part[row : row + 16, lane : lane + HALF]
            conv_ref[KERNEL - 1, :8, lanes] = part[32:40, :HALF]
            conv_ref[KERNEL - 1, 8:, lanes] = part[32:40, HALF:]
            filt_ref[32 * e : 32 * e + 32, :] = part[40:72, :]
            for j in range(2):
                pos = part[72:80, j * LANES : (j + 1) * LANES]
                pos_ref[32 * e + 8 * j : 32 * e + 8 * j + 8, :] = pos[:, :FEAT]
                pos_ref[32 * e + 16 + 8 * j : 32 * e + 24 + 8 * j, :] = pos[:, FEAT:]
            for j in range(4):
                stat = part[72 + j : 73 + j, HALF : HALF + LANES] + part[76 + j : 77 + j, HALF : HALF + LANES]
                (rates_ref, skip_ref)[e][:, j * LANES : (j + 1) * LANES] = stat

    @pl.when(core == 0)
    def _():
        write(mine_ref, other_ref)

    @pl.when(core == 1)
    def _():
        write(other_ref, mine_ref)


VMEM = pl.BlockSpec(memory_space=pltpu.VMEM)
HBM = pl.BlockSpec(memory_space=pltpu.HBM)


def call(kernel, out_shape, args, scratch=(), flops=0, name=None, specs=None, out_specs=None, limit=60):
    single = not isinstance(out_shape, (list, tuple))
    outs = [out_shape] if single else out_shape
    moved = sum(math.prod(a.shape) * a.dtype.itemsize for a in (*args, *outs))
    return pl.pallas_call(
        kernel,
        out_shape=out_shape,
        in_specs=specs or [VMEM] * len(args),
        out_specs=out_specs or (VMEM if single else [VMEM] * len(outs)),
        scratch_shapes=list(scratch),
        compiler_params=pltpu.CompilerParams(vmem_limit_bytes=int(limit * 1024 * 1024)),
        cost_estimate=pl.CostEstimate(flops=flops, bytes_accessed=moved, transcendentals=0),
        name=name,
    )(*args)


def shape(dims, kind=F32):
    return jax.ShapeDtypeStruct(dims, kind)


def regroup(blocks):
    return lax.all_to_all(blocks, "tm", split_axis=0, concat_axis=0, tiled=True)


def on_device(inputs, cotangent, w_pos, w_filt, log_rates, skip_gain, w_conv):
    swap = [(i, i ^ 1) for i in range(lax.axis_size("batch"))]
    signal, upstream = inputs[0], cotangent[0]
    w_taps = jnp.transpose(w_conv, (1, 0, 2))
    tabs = tuple(jnp.asarray(t) for t in transform_tables())
    feat = jnp.asarray(np.concatenate(feature_tables(), axis=0))

    message = call(
        prep_kernel,
        shape((WIDTH, ROWS + SPAN), BF16),
        (signal, upstream, w_taps),
        [
            pltpu.VMEM((ROWS, WIDTH), BF16),
            pltpu.VMEM((ROWS, WIDTH), BF16),
            pltpu.VMEM((KERNEL, WIDTH, WIDTH), BF16),
            pltpu.VMEM((EDGE + ROWS + 8, WIDTH), F32),
            pltpu.VMEM((SPAN, WIDTH), F32),
            pltpu.VMEM((WIDTH, ROWS), BF16),
            pltpu.VMEM((WIDTH, SPAN), BF16),
            pltpu.SemaphoreType.DMA((4 + KERNEL,)),
        ],
        flops=2 * KERNEL * WIDTH * WIDTH * (ROWS + EDGE),
        name="prep",
        specs=[HBM] * 3,
        out_specs=HBM,
    )
    received = regroup(message.reshape(SHARDS, OWN, ROWS + SPAN))
    cot_peer = lax.ppermute(upstream, "batch", swap)
    received, cot_peer = lax.optimization_barrier((received, cot_peer))

    stack = pltpu.VMEM((STACK, LANES), F32)
    wide = pltpu.VMEM((STACK, 2 * LANES), BF16)
    saved = [pltpu.VMEM((2 * FEAT, LENGTH), BF16), pltpu.VMEM((FEAT, LENGTH), F32), pltpu.VMEM((OWN, LENGTH), F32)]
    flops = 2 * 3 * (2 * STACK * LANES * LANES + STACK * 4 * LANES * LANES)
    hidden, cosines, taps, tap_spec, par = call(
        taps_kernel,
        [
            shape((2 * FEAT, LENGTH), BF16),
            shape((FEAT, LENGTH)),
            shape((OWN, LENGTH)),
            shape((STACK, 2 * LANES)),
            shape((OWN, LANES)),
        ],
        (w_pos, w_filt, log_rates[None], skip_gain[None], feat, *tabs),
        [*saved, pltpu.VMEM((STACK, 2 * LANES), F32), pltpu.VMEM((OWN, LANES), F32), stack, wide, wide, pltpu.SemaphoreType.DMA((5,))],
        flops=flops * 2,
        name="taps",
        out_specs=[HBM] * 5,
        limit=63.5,
    )
    act_message, before, sig_spec = call(
        forward_kernel,
        [shape((SHARDS, OWN, SPAN), BF16), shape((STACK, LANES)), shape((STACK, 2 * LANES))],
        (received, tap_spec, par, *tabs),
        [
            pltpu.VMEM((SHARDS, OWN, ROWS), BF16),
            pltpu.VMEM((STACK, 2 * LANES), F32),
            pltpu.VMEM((STACK, 2 * LANES), F32),
            pltpu.VMEM((SHARDS, OWN, SPAN), BF16),
            *[pltpu.VMEM(t.shape, t.dtype) for t in tabs],
            stack,
            stack,
            wide,
            wide,
            pltpu.VMEM((OWN, LANES), F32),
            pltpu.SemaphoreType.DMA((14,)),
        ],
        flops=flops * 2,
        name="forward",
        specs=[HBM] * 11,
        out_specs=[HBM] * 3,
    )
    act = regroup(act_message).reshape(WIDTH, SPAN)
    ig_message, small = call(
        backward_kernel,
        [shape((SHARDS, OWN, ROWS), BF16), shape((2, 2 * OWN, LANES))],
        (received, before, sig_spec, tap_spec, par, hidden, cosines, feat, taps, *tabs),
        [
            pltpu.VMEM((SHARDS, OWN, ROWS + SPAN), BF16),
            stack,
            pltpu.VMEM((STACK, 2 * LANES), F32),
            pltpu.VMEM((STACK, 2 * LANES), F32),
            pltpu.VMEM((OWN, LANES), F32),
            *saved[:2],
            saved[0],
            saved[2],
            *[pltpu.VMEM(t.shape, t.dtype) for t in tabs],
            stack,
            pltpu.VMEM((SHARDS, OWN, ROWS), BF16),
            pltpu.VMEM((2, 2 * OWN, LANES), F32),
            stack,
            wide,
            wide,
            pltpu.VMEM((OWN, LENGTH), F32),
            pltpu.SemaphoreType.DMA((19,)),
        ],
        flops=flops * 4,
        name="backward",
        specs=[HBM] * 17,
        out_specs=[HBM] * 2,
        limit=63.75,
    )
    act, ig_message, small = lax.optimization_barrier((act, ig_message, small))
    act_peer = lax.ppermute(act, "batch", swap)
    small_peer = lax.ppermute(small, "batch", swap)
    lanes = CONV + ROWS + 2 * LANES
    sums = call(
        conv_kernel,
        shape((WIDTH, lanes), BF16),
        (act, act_peer, upstream, cot_peer, ig_message.reshape(WIDTH, ROWS), small, small_peer),
        [
            pltpu.VMEM((2, WIDTH, SPAN), BF16),
            pltpu.VMEM((2, ROWS, HALF), BF16),
            pltpu.VMEM((WIDTH, ROWS), BF16),
            pltpu.VMEM((2, 2 * OWN, LANES), F32),
            pltpu.VMEM((2, HALO + ROWS + 8, HALF), F32),
            pltpu.VMEM((KERNEL, WIDTH, HALF), BF16),
            pltpu.VMEM((WIDTH, ROWS + 2 * LANES), BF16),
            pltpu.SemaphoreType.DMA((10 + KERNEL,)),
        ],
        flops=2 * KERNEL * WIDTH * HALF * 2 * ROWS,
        name="conv_grad",
        specs=[HBM] * 7,
        out_specs=HBM,
    )
    spread = regroup(sums.reshape(SHARDS, OWN, lanes))
    mixed = call(
        mixed_kernel,
        shape((ROWS, WIDTH), BF16),
        (act, w_taps, sums),
        [
            pltpu.VMEM((WIDTH, SPAN), BF16),
            pltpu.VMEM((KERNEL, WIDTH, WIDTH), BF16),
            pltpu.VMEM((ROWS + EDGE, WIDTH), F32),
            pltpu.VMEM((ROWS, WIDTH), BF16),
            pltpu.SemaphoreType.DMA((2 + KERNEL,)),
        ],
        flops=2 * KERNEL * WIDTH * WIDTH * (ROWS + EDGE),
        name="mixed",
        specs=[HBM] * 3,
        out_specs=HBM,
    )
    spread, mixed = lax.optimization_barrier((spread, mixed))
    payload = call(gather_kernel, shape((80, WIDTH), BF16), (spread,), name="gather", limit=12)
    met = lax.ppermute(payload, "batch", [(i, i ^ 2) for i in range(8)])
    pair = call(pair_kernel, shape((80, WIDTH), BF16), (payload, met), name="pair", limit=12)
    met = lax.ppermute(pair, "batch", [(i, i ^ 6) for i in range(8)])
    spread, pair = lax.optimization_barrier((spread, pair))
    input_grad = call(
        input_kernel,
        shape((ROWS, WIDTH), BF16),
        (spread,),
        [pltpu.VMEM((ROWS, WIDTH), BF16), pltpu.SemaphoreType.DMA],
        name="input",
        out_specs=HBM,
        limit=12,
    )
    pair, input_grad = lax.optimization_barrier((pair, input_grad))
    mine = call(final_kernel, shape((80, WIDTH)), (pair, met), name="final", limit=12)
    other = lax.ppermute(mine, "batch", swap)
    conv_grad, pos_grad, filt_grad, rates_grad, skip_grad = call(
        join_kernel,
        [
            shape((KERNEL, OWN, WIDTH)),
            shape((FEAT, FEAT)),
            shape((FEAT, WIDTH)),
            shape((1, WIDTH)),
            shape((1, WIDTH)),
        ],
        (mine, other),
        name="join",
        limit=12,
    )
    return (
        mixed[None],
        input_grad[None],
        jnp.transpose(conv_grad, (1, 0, 2)),
        pos_grad,
        filt_grad,
        rates_grad[0],
        skip_grad[0],
    )


def solution(mesh):
    in_specs = (P("batch", "tm", None), P("batch", "tm", None), P(), P(), P(), P(), P())
    out_specs = (P("batch", "tm", None), P("batch", "tm", None), P("tm", None, None), P(), P(), P(), P())
    return jax.shard_map(on_device, mesh=mesh, in_specs=in_specs, out_specs=out_specs, check_vma=False)
```

```python
import math

import jax
import jax.numpy as jnp
import ml_dtypes
import numpy as np
from jax import lax
from jax.experimental import pallas as pl
from jax.experimental.pallas import tpu as pltpu
from jax.sharding import PartitionSpec as P

F32 = jnp.float32
BF16 = jnp.bfloat16

SHARDS = 32
ROWS = 256
LENGTH = SHARDS * ROWS
WIDTH = 512
KERNEL = 5
FEAT = 64
OWN = WIDTH // SHARDS
LANES = 128
STEPS = LENGTH // LANES
STACK = STEPS * OWN
HALO = LANES
SPAN = ROWS + HALO
HALF = WIDTH // 2
EDGE = 16
CONV = KERNEL * HALF
BLOCK = 4096
CHUNK = 128
SLICE = 8
SCALE = 1.0 / math.sqrt(8 * LENGTH)


def split_table(values):
    high = values.astype(ml_dtypes.bfloat16)
    low = (values - high.astype(np.float64)).astype(ml_dtypes.bfloat16)
    return high, low


def feature_tables():
    half = FEAT // 2
    factor = np.array([1 + i * i * LENGTH // (2 * half * half) for i in range(half)], dtype=np.int64)
    steps = np.arange(LENGTH, dtype=np.int64)
    angles = 2.0 * np.pi * ((factor[:, None] * steps[None, :]) % LENGTH) / LENGTH
    return split_table(np.concatenate([np.sin(angles), np.cos(angles)], axis=0))


def transform_tables():
    order = np.array([2 * p + h for h in range(2) for p in range(STEPS // 2)])
    k1 = np.arange(STEPS)
    alpha = np.pi * order[None, :] / STEPS / 2 - 2.0 * np.pi * ((order[None, :] * k1[:, None]) % STEPS) / STEPS
    outer = np.concatenate([np.cos(alpha), np.sin(alpha)], axis=0)
    outer_high, outer_low = split_table(outer)
    first = np.concatenate([outer_high, outer_low], axis=1)
    back_high, back_low = split_table(outer.T / LENGTH)
    last = np.concatenate([back_high, back_low, back_high], axis=1)
    b = np.arange(LANES)
    beta = np.pi * b[None, :] / (2 * LENGTH) - 2.0 * np.pi * ((b[None, :] * k1[:, None]) % LENGTH) / LENGTH
    twist_cos = np.cos(beta).astype(np.float32)
    twist_sin = np.sin(beta).astype(np.float32)
    gamma = 2.0 * np.pi * ((b[:, None] * b[None, :]) % LANES) / LANES
    cos, sin = np.cos(gamma), np.sin(gamma)
    ahead = split_table(np.block([[cos, -sin], [sin, cos]]))
    behind = split_table(np.block([[cos, sin], [-sin, cos]]))
    return (first, last, twist_cos, twist_sin, *ahead, *behind)


def split(values):
    high = values.astype(BF16)
    return high, (values - high.astype(F32)).astype(BF16)


def mul(left, right, dims=((1,), (0,))):
    return lax.dot_general(left, right, (dims, ((), ())), preferred_element_type=F32)


def mul3(left, right, dims=((1,), (0,))):
    lh, ll = left
    rh, rl = right
    return mul(lh, rh, dims) + mul(ll, rh, dims) + mul(lh, rl, dims)


def wait_for(loads, *which):
    for k in which:
        if loads is not None:
            loads[k].wait()


def spectrum(stack_ref, high_ref, low_ref, tabs, loads=None):
    first, _, tc_ref, ts_ref, ahead_high, ahead_low, _, _ = tabs
    wait_for(loads, 0, 2, 3)
    tc, ts = tc_ref[...], ts_ref[...]
    for c in range(0, OWN, 2):
        pair = [stack_ref[pl.ds(c + k, STEPS, stride=OWN), :] for k in range(2)]
        wide = jnp.concatenate(pair, axis=1).astype(BF16)
        u = mul(first[...], jnp.concatenate([wide, wide], axis=0))
        for k in range(2):
            ur = u[:STEPS, k * LANES : (k + 1) * LANES]
            ui = u[STEPS:, k * LANES : (k + 1) * LANES]
            v = jnp.concatenate([ur * tc - ui * ts, ur * ts + ui * tc], axis=1)
            high, low = split(v)
            high_ref[(c + k) * STEPS : (c + k + 1) * STEPS, :] = high
            low_ref[(c + k) * STEPS : (c + k + 1) * STEPS, :] = low
    wait_for(loads, 4, 5)
    table = (ahead_high[...], ahead_low[...])
    parts = [mul3((high_ref[r : r + CHUNK, :], low_ref[r : r + CHUNK, :]), table) for r in range(0, STACK, CHUNK)]
    return jnp.concatenate(parts, axis=0)


def from_spectrum(values, stack_ref, tabs, loads=None):
    _, last, tc_ref, ts_ref, _, _, behind_high, behind_low = tabs
    wait_for(loads, 6, 7, 1)
    tc, ts = tc_ref[...], ts_ref[...]
    table = (behind_high[...], behind_low[...])
    q = jnp.concatenate([mul3(split(values[r : r + CHUNK]), table) for r in range(0, STACK, CHUNK)], axis=0)
    for c in range(0, OWN, 2):
        pair = []
        for k in range(2):
            rows = q[(c + k) * STEPS : (c + k + 1) * STEPS]
            qr, qi = rows[:, :LANES], rows[:, LANES:]
            pair.append(jnp.concatenate([qr * tc + qi * ts, qi * tc - qr * ts], axis=0))
        high, low = split(jnp.concatenate(pair, axis=1))
        y = mul(last[...], jnp.concatenate([high, high, low], axis=0))
        for k in range(2):
            stack_ref[pl.ds(c + k, STEPS, stride=OWN), :] = y[:, k * LANES : (k + 1) * LANES]


def product(left, right, conjugate):
    lr, li = left[:, :LANES], left[:, LANES:]
    rr, ri = right[:, :LANES], right[:, LANES:]
    if conjugate:
        return jnp.concatenate([lr * rr + li * ri, lr * ri - li * rr], axis=1)
    return jnp.concatenate([lr * rr - li * ri, lr * ri + li * rr], axis=1)


def sin_cos(x):
    turns = jnp.floor(x * (2.0 / math.pi) + 0.5)
    r = x - turns * 1.5703125
    r = r - turns * 4.837512969970703125e-4
    r = r - turns * 7.549789948768648e-8
    z = r * r
    s = r + r * z * (-1.6666654611e-1 + z * (8.3321608736e-3 - z * 1.9515295891e-4))
    c = 1.0 - 0.5 * z + z * z * (4.166664568298827e-2 + z * (-1.388731625493765e-3 + z * 2.443315711809948e-5))
    quad = turns.astype(jnp.int32)
    odd = (quad & 1) == 1
    sin = jnp.where(odd, c, s)
    cos = jnp.where(odd, s, c)
    sin = jnp.where((quad & 2) == 2, -sin, sin)
    cos = jnp.where(((quad + 1) & 2) == 2, -cos, cos)
    return sin, cos


def envelope(rates, start, size):
    steps = (start + lax.broadcasted_iota(jnp.int32, (OWN, size), 1)).astype(F32)
    return jnp.sqrt(rates) * jnp.exp(-steps * rates), steps


def prep_kernel(x_hbm, cot_hbm, w_hbm, out_hbm, x_ref, cot_ref, w_ref, pad_ref, sum_ref, xt_ref, ga_ref, sems):
    x_copy = pltpu.make_async_copy(x_hbm, x_ref, sems.at[0])
    x_copy.start()
    cot_copy = pltpu.make_async_copy(cot_hbm, cot_ref, sems.at[1])
    cot_copy.start()
    w_copies = [pltpu.make_async_copy(w_hbm.at[i], w_ref.at[i], sems.at[2 + i]) for i in range(KERNEL)]
    for copy in w_copies:
        copy.start()
    pad_ref[:EDGE, :] = jnp.zeros((EDGE, WIDTH), F32)
    pad_ref[EDGE + ROWS :, :] = jnp.zeros((8, WIDTH), F32)
    x_copy.wait()
    xt_ref[...] = jnp.transpose(x_ref[...].astype(F32)).astype(BF16)
    x_out = pltpu.make_async_copy(xt_ref, out_hbm.at[:, pl.ds(0, ROWS)], sems.at[2 + KERNEL])
    x_out.start()
    cot_copy.wait()
    pad_ref[EDGE : EDGE + ROWS, :] = cot_ref[...].astype(F32)
    for i in range(KERNEL):
        shifted = pad_ref[i : i + EDGE + ROWS, :].astype(BF16)
        w_copies[i].wait()
        part = mul(shifted, w_ref[i], ((1,), (1,)))
        if i == 0:
            sum_ref[HALO - EDGE :, :] = part
        else:
            sum_ref[HALO - EDGE :, :] += part
    sum_ref[: HALO - EDGE, :] = jnp.zeros((HALO - EDGE, WIDTH), F32)
    ga_ref[...] = jnp.transpose(sum_ref[...]).astype(BF16)
    ga_out = pltpu.make_async_copy(ga_ref, out_hbm.at[:, pl.ds(ROWS, SPAN)], sems.at[3 + KERNEL])
    ga_out.start()
    x_out.wait()
    ga_out.wait()


def taps_kernel(wp_ref, wf_ref, lr_ref, gain_ref, feat_ref, *rest):
    tabs = rest[:8]
    hid_out, cos_out, taps_out, spec_out, par_out = rest[8:13]
    hid_ref, cos_ref, taps_ref, spec_ref, par_ref, stack_ref, vh_ref, vl_ref, sems = rest[13:]
    first = lax.axis_index("tm") * OWN
    lane = lax.broadcasted_iota(jnp.int32, (OWN, WIDTH), 1)
    chosen = lane == first + lax.broadcasted_iota(jnp.int32, (OWN, WIDTH), 0)
    wf_own = lax.dot_general(
        chosen.astype(F32),
        wf_ref[...],
        (((1,), (1,)), ((), ())),
        precision=lax.Precision.HIGHEST,
        preferred_element_type=F32,
    )
    rates = jnp.exp(jnp.sum(jnp.where(chosen, lr_ref[...], 0.0), axis=1, keepdims=True))
    gain = jnp.sum(jnp.where(chosen, gain_ref[...], 0.0), axis=1, keepdims=True)
    spot = lax.broadcasted_iota(jnp.int32, (OWN, LANES), 1)
    par_ref[...] = jnp.where(spot == FEAT, rates, jnp.where(spot == FEAT + 1, gain, 0.0))
    par_ref[:, :FEAT] = wf_own
    wp_high, wp_low = split(wp_ref[...])
    wp = jnp.concatenate([wp_high, wp_low, wp_high], axis=0)
    wf_high, wf_low = split(wf_own)
    for start in range(0, LENGTH, BLOCK):
        cut = slice(start, start + BLOCK)
        feat = feat_ref[:, cut]
        sin, cos = sin_cos(mul(wp, jnp.concatenate([feat[:FEAT], feat], axis=0), ((0,), (0,))))
        high, low = split(sin)
        hid_ref[:FEAT, cut] = high
        hid_ref[FEAT:, cut] = low
        cos_ref[:, cut] = cos
        decay, _ = envelope(rates, start, BLOCK)
        taps = mul3((wf_high, wf_low), (high, low)) * decay
        taps_ref[:, cut] = taps
        rounded = taps.astype(BF16).astype(F32)
        for j in range(BLOCK // LANES):
            a = start // LANES + j
            row = ((a % 2) * SHARDS + a // 2) * OWN
            stack_ref[row : row + OWN, :] = rounded[:, j * LANES : (j + 1) * LANES]
    saves = [
        pltpu.make_async_copy(source, target, sems.at[k])
        for k, (source, target) in enumerate(((hid_ref, hid_out), (cos_ref, cos_out), (taps_ref, taps_out), (par_ref, par_out)))
    ]
    for save in saves:
        save.start()
    spec_ref[...] = spectrum(stack_ref, vh_ref, vl_ref, tabs)
    saves.append(pltpu.make_async_copy(spec_ref, spec_out, sems.at[4]))
    saves[-1].start()
    for save in saves:
        save.wait()


def gelu_parts(before):
    root = math.sqrt(2.0 / math.pi)
    square = before * before
    th = jnp.tanh(root * (before + 0.044715 * square * before))
    half_cdf = 0.5 * (1.0 + th)
    slope = half_cdf + 0.5 * before * (1.0 - th * th) * (root * (1.0 + 3.0 * 0.044715 * square))
    return before * half_cdf, slope


def forward_kernel(recv_hbm, tspec_hbm, par_hbm, *rest):
    tabs_hbm = rest[:8]
    act_hbm, before_hbm, xspec_hbm = rest[8:11]
    xin_ref, tspec_ref, spec_ref, act_ref = rest[11:15]
    tabs = rest[15:23]
    x_ref, y_ref, vh_ref, vl_ref, par_ref, sems = rest[23:]
    x_load = pltpu.make_async_copy(recv_hbm.at[:, :, pl.ds(0, ROWS)], xin_ref, sems.at[0])
    x_load.start()
    loads = [pltpu.make_async_copy(tabs_hbm[k], tabs[k], sems.at[1 + k]) for k in range(8)]
    for k in (0, 2, 3, 4, 5, 6, 7, 1):
        loads[k].start()
    tspec_load = pltpu.make_async_copy(tspec_hbm, tspec_ref, sems.at[9])
    tspec_load.start()
    par_load = pltpu.make_async_copy(par_hbm, par_ref, sems.at[10])
    par_load.start()
    x_load.wait()
    for h in range(2):
        part = xin_ref[:, :, h * LANES : (h + 1) * LANES].astype(F32)
        x_ref[h * STACK // 2 : (h + 1) * STACK // 2, :] = part.reshape(STACK // 2, LANES)
    spec = spectrum(x_ref, vh_ref, vl_ref, tabs, loads)
    spec_ref[...] = spec
    spec_save = pltpu.make_async_copy(spec_ref, xspec_hbm, sems.at[11])
    spec_save.start()
    tspec_load.wait()
    from_spectrum(product(tspec_ref[...], spec, False), y_ref, tabs, loads)
    par_load.wait()
    gain = par_ref[:, FEAT + 1 : FEAT + 2][None]
    act_ref[0, :, :HALO] = jnp.zeros((OWN, LANES), BF16)
    for p in range(0, STEPS, SLICE):
        rows = slice(p * OWN, (p + SLICE) * OWN)
        before = y_ref[rows, :].reshape(SLICE, OWN, LANES) + gain * x_ref[rows, :].reshape(SLICE, OWN, LANES)
        y_ref[rows, :] = before.reshape(SLICE * OWN, LANES)
        active = gelu_parts(before)[0].astype(BF16)
        h, at = divmod(p, SHARDS)
        act_ref[at : at + SLICE, :, HALO + h * LANES : HALO + (h + 1) * LANES] = active
        if h == 1:
            kept = min(SLICE, SHARDS - 1 - at)
            act_ref[at + 1 : at + 1 + kept, :, :HALO] = active[:kept]
    before_save = pltpu.make_async_copy(y_ref, before_hbm, sems.at[12])
    before_save.start()
    act_save = pltpu.make_async_copy(act_ref, act_hbm, sems.at[13])
    act_save.start()
    spec_save.wait()
    before_save.wait()
    act_save.wait()


def backward_kernel(*rest):
    arrays_hbm, tabs_hbm = rest[:9], rest[9:17]
    ig_hbm, small_hbm = rest[17:19]
    arrays, tabs = rest[19:28], rest[28:36]
    recv_ref, before_ref, xspec_ref, tspec_ref, par_ref, hid_ref, cos_ref, feat_ref, taps_ref = arrays
    gb_ref, ig_ref, small_ref, y_ref, vh_ref, vl_ref, g_ref, sems = rest[36:]
    first = [pltpu.make_async_copy(arrays_hbm[k], arrays[k], sems.at[k]) for k in range(9)]
    table = [pltpu.make_async_copy(tabs_hbm[k], tabs[k], sems.at[9 + k]) for k in range(8)]
    for copy in (*first[:2], *table, *first[2:]):
        copy.start()
    wait_for(first, 0, 1)
    skip = jnp.zeros((OWN, LANES), F32)
    for p in range(0, STEPS, SLICE):
        rows = slice(p * OWN, (p + SLICE) * OWN)
        h, at = divmod(p, SHARDS)
        part = slice(at, at + SLICE)
        grad = recv_ref[part, :, ROWS + HALO + h * LANES : ROWS + HALO + (h + 1) * LANES].astype(F32)
        if h == 1:
            edge = recv_ref[at + 1 : min(at + 1 + SLICE, SHARDS), :, ROWS : ROWS + HALO].astype(F32)
            if at + SLICE == SHARDS:
                edge = jnp.concatenate([edge, jnp.zeros((1, OWN, LANES), F32)], axis=0)
            grad = grad + edge
        grad = grad * gelu_parts(before_ref[rows, :].reshape(SLICE, OWN, LANES))[1]
        grad = grad.astype(BF16).astype(F32)
        gb_ref[rows, :] = grad.reshape(SLICE * OWN, LANES)
        skip = skip + jnp.sum(grad * recv_ref[part, :, h * LANES : (h + 1) * LANES].astype(F32), axis=0)
    skip = jnp.sum(skip, axis=1, keepdims=True)
    spec = spectrum(gb_ref, vh_ref, vl_ref, tabs, table)
    wait_for(first, 2, 3, 4)
    from_spectrum(product(tspec_ref[...], spec, True), y_ref, tabs, table)
    gain = par_ref[:, FEAT + 1 : FEAT + 2][None]
    for p in range(0, STEPS, SLICE):
        rows = slice(p * OWN, (p + SLICE) * OWN)
        h, at = divmod(p, SHARDS)
        result = y_ref[rows, :].reshape(SLICE, OWN, LANES) + gain * gb_ref[rows, :].reshape(SLICE, OWN, LANES)
        ig_ref[at : at + SLICE, :, h * LANES : (h + 1) * LANES] = result.astype(BF16)
    save = pltpu.make_async_copy(ig_ref, ig_hbm, sems.at[17])
    save.start()
    from_spectrum(product(xspec_ref[...], spec, True), y_ref, tabs)
    for a in range(STEPS):
        row = ((a % 2) * SHARDS + a // 2) * OWN
        g_ref[:, a * LANES : (a + 1) * LANES] = y_ref[row : row + OWN, :]
    wf_high, wf_low = split(par_ref[:, :FEAT])
    wf = jnp.concatenate([wf_high, wf_low, wf_high], axis=0)
    rates = par_ref[:, FEAT : FEAT + 1]
    wait_for(first, 5, 6, 7, 8)
    filt = jnp.zeros((2 * OWN, 2 * FEAT), F32)
    pos = jnp.zeros((2 * FEAT, 2 * FEAT), F32)
    rate = jnp.zeros((OWN, 1), F32)
    for start in range(0, LENGTH, BLOCK):
        cut = slice(start, start + BLOCK)
        grad_taps = g_ref[:, cut]
        decay, steps = envelope(rates, start, BLOCK)
        high, low = split(grad_taps * decay)
        rate = rate + jnp.sum(grad_taps * taps_ref[:, cut] * (0.5 - rates * steps), axis=1, keepdims=True)
        filt = filt + mul(jnp.concatenate([high, low], axis=0), hid_ref[:, cut], ((1,), (1,)))
        inner = mul(wf, jnp.concatenate([high, high, low], axis=0), ((0,), (0,))) * cos_ref[:, cut]
        pos = pos + mul(feat_ref[:, cut], jnp.concatenate(split(inner), axis=0), ((1,), (1,)))
    filt = filt[:OWN, :FEAT] + filt[OWN:, :FEAT] + filt[:OWN, FEAT:]
    pos = pos[:FEAT, :FEAT] + pos[FEAT:, :FEAT] + pos[:FEAT, FEAT:]
    small_ref[...] = jnp.zeros((2, 2 * OWN, LANES), F32)
    for e, stat in enumerate((rate, skip)):
        small_ref[e, :OWN, :32] = filt[:, 32 * e : 32 * e + 32]
        small_ref[e, :OWN, 32:33] = stat
        small_ref[e, OWN:, :FEAT] = pos[32 * e : 32 * e + 16]
        small_ref[e, OWN:, FEAT:] = pos[32 * e + 16 : 32 * e + 32]
    small_save = pltpu.make_async_copy(small_ref, small_hbm, sems.at[18])
    small_save.start()
    save.wait()
    small_save.wait()


def conv_kernel(
    act_hbm, peer_act_hbm, cot_hbm, peer_cot_hbm, ig_hbm, small_hbm, peer_small_hbm, out_hbm,
    act_ref, cot_ref, ig_ref, small_ref, pad_ref, part_ref, tile_ref, sems,
):
    core = lax.axis_index("batch") % 2
    half = pl.ds(pl.multiple_of(core * HALF, HALF), HALF)
    sources = [
        (cot_hbm.at[:, half], cot_ref.at[0]),
        (peer_cot_hbm.at[:, half], cot_ref.at[1]),
        (act_hbm, act_ref.at[0]),
        (peer_act_hbm, act_ref.at[1]),
        (ig_hbm, ig_ref),
        (small_hbm.at[core], small_ref.at[0]),
        (peer_small_hbm.at[core], small_ref.at[1]),
    ]
    loads = [pltpu.make_async_copy(a, b, sems.at[k]) for k, (a, b) in enumerate(sources)]
    for load in loads:
        load.start()
    pad_ref[:, :HALO, :] = jnp.zeros((2, HALO, HALF), F32)
    pad_ref[:, HALO + ROWS :, :] = jnp.zeros((2, 8, HALF), F32)
    wait_for(loads, 0, 1)
    pad_ref[:, HALO : HALO + ROWS, :] = cot_ref[...].astype(F32)
    wait_for(loads, 2, 3)
    copies = []
    for i in range(KERNEL):
        own = pad_ref[0, i : i + SPAN, :].astype(BF16)
        peer = pad_ref[1, i : i + SPAN, :].astype(BF16)
        both = jnp.concatenate([own, peer], axis=0)
        for r in range(0, WIDTH, CHUNK):
            rows = slice(r, r + CHUNK)
            wide = jnp.concatenate([act_ref[0, rows, :], act_ref[1, rows, :]], axis=1)
            part_ref[i, rows, :] = mul(wide, both).astype(BF16)
        copies.append(pltpu.make_async_copy(part_ref.at[i], out_hbm.at[:, pl.ds(i * HALF, HALF)], sems.at[9 + i]))
        copies[-1].start()
        if i == 0:
            wait_for(loads, 4, 5, 6)
            tile_ref[:, :ROWS] = ig_ref[...]
            small = small_ref[0] + small_ref[1]
            high, low = split(small[:OWN])
            filt = high.astype(F32) + pltpu.roll(low.astype(F32), FEAT, 1)
            tile = jnp.concatenate([filt, small[OWN:]], axis=1).astype(BF16)
            for p in range(SHARDS):
                tile_ref[p * OWN : (p + 1) * OWN, ROWS:] = tile
            target = out_hbm.at[:, pl.ds(CONV, ROWS + 2 * LANES)]
            copies.append(pltpu.make_async_copy(tile_ref, target, sems.at[9 + KERNEL]))
            copies[-1].start()
    for copy in copies:
        copy.wait()


def mixed_kernel(act_hbm, w_hbm, _, out_hbm, act_ref, w_ref, part_ref, out_ref, sems):
    loads = [pltpu.make_async_copy(w_hbm.at[i], w_ref.at[i], sems.at[i]) for i in range(KERNEL)]
    loads.append(pltpu.make_async_copy(act_hbm, act_ref, sems.at[KERNEL]))
    for load in loads:
        load.start()
    wait_for(loads, KERNEL)
    act = jnp.transpose(act_ref[...].astype(F32)).astype(BF16)[HALO - EDGE :]
    total = jnp.zeros((ROWS, WIDTH), F32)
    for i in range(KERNEL):
        wait_for(loads, i)
        part_ref[...] = mul(act, w_ref[i])
        total = total + part_ref[EDGE - i : EDGE - i + ROWS, :]
    out_ref[...] = total.astype(BF16)
    save = pltpu.make_async_copy(out_ref, out_hbm, sems.at[KERNEL + 1])
    save.start()
    save.wait()


def fold(block):
    return jnp.concatenate([block[:8], block[8:]], axis=1)


def two_parts(rows):
    high, low = split(rows)
    return jnp.concatenate([high.astype(F32), low.astype(F32)], axis=0)


def gather_kernel(recv_ref, out_ref):
    conv = jnp.sum(recv_ref[:, :, :CONV].astype(F32), axis=0)
    blocks = [conv[:, :WIDTH], conv[:, WIDTH : 2 * WIDTH], fold(conv[:, 2 * WIDTH :])]
    base = CONV + ROWS
    both = recv_ref[:, :, base : base + LANES].astype(F32).reshape(WIDTH, LANES)
    filt = jnp.transpose(both + pltpu.roll(both, FEAT, 1))
    pos = jnp.sum(recv_ref[:, :, base + LANES : base + 2 * LANES].astype(F32), axis=0)
    stat = filt[32:33]
    pieces = [stat[:, j * LANES : (j + 1) * LANES] for j in range(4)]
    last = jnp.concatenate([fold(pos), two_parts(jnp.concatenate(pieces, axis=0)), jnp.zeros((8, LANES), F32)], axis=1)
    out_ref[...] = jnp.concatenate([*blocks, filt[:32], last], axis=0).astype(BF16)


def pair_kernel(own_ref, other_ref, out_ref):
    total = own_ref[...].astype(F32) + other_ref[...].astype(F32)
    last = total[72:]
    stat = last[:4, HALF : HALF + LANES] + last[4:, HALF : HALF + LANES]
    last = jnp.concatenate([last[:, :HALF], two_parts(stat), last[:, HALF + LANES :]], axis=1)
    out_ref[...] = jnp.concatenate([total[:72], last], axis=0).astype(BF16)


def input_kernel(recv_ref, out_hbm, out_ref, sem):
    out_ref[...] = jnp.transpose(recv_ref[:, :, CONV : CONV + ROWS].astype(F32).reshape(WIDTH, ROWS)).astype(BF16)
    save = pltpu.make_async_copy(out_ref, out_hbm, sem)
    save.start()
    save.wait()


def join_kernel(
    pair_ref, met_ref, peer_pair_ref, peer_met_ref, conv_ref, pos_ref, filt_ref, rates_ref, skip_ref, mine_ref, other_ref
):
    core = lax.axis_index("batch") % 2
    mine_ref[...] = (pair_ref[...].astype(F32) + met_ref[...].astype(F32)) * SCALE
    other_ref[...] = (peer_pair_ref[...].astype(F32) + peer_met_ref[...].astype(F32)) * SCALE

    def write(low, high):
        for e, part in enumerate((low, high)):
            lanes = slice(e * HALF, (e + 1) * HALF)
            for i in range(KERNEL - 1):
                row, lane = 16 * (i // 2), HALF * (i % 2)
                conv_ref[i, :, lanes] = part[row : row + 16, lane : lane + HALF]
            conv_ref[KERNEL - 1, :8, lanes] = part[32:40, :HALF]
            conv_ref[KERNEL - 1, 8:, lanes] = part[32:40, HALF:]
            filt_ref[32 * e : 32 * e + 32, :] = part[40:72, :]
            for j in range(2):
                pos = part[72:80, j * LANES : (j + 1) * LANES]
                pos_ref[32 * e + 8 * j : 32 * e + 8 * j + 8, :] = pos[:, :FEAT]
                pos_ref[32 * e + 16 + 8 * j : 32 * e + 24 + 8 * j, :] = pos[:, FEAT:]
            for j in range(4):
                stat = part[72 + j : 73 + j, HALF : HALF + LANES] + part[76 + j : 77 + j, HALF : HALF + LANES]
                (rates_ref, skip_ref)[e][:, j * LANES : (j + 1) * LANES] = stat

    @pl.when(core == 0)
    def _():
        write(mine_ref, other_ref)

    @pl.when(core == 1)
    def _():
        write(other_ref, mine_ref)


VMEM = pl.BlockSpec(memory_space=pltpu.VMEM)
HBM = pl.BlockSpec(memory_space=pltpu.HBM)


def call(kernel, out_shape, args, scratch=(), flops=0, name=None, specs=None, out_specs=None, limit=60):
    single = not isinstance(out_shape, (list, tuple))
    outs = [out_shape] if single else out_shape
    moved = sum(math.prod(a.shape) * a.dtype.itemsize for a in (*args, *outs))
    return pl.pallas_call(
        kernel,
        out_shape=out_shape,
        in_specs=specs or [VMEM] * len(args),
        out_specs=out_specs or (VMEM if single else [VMEM] * len(outs)),
        scratch_shapes=list(scratch),
        compiler_params=pltpu.CompilerParams(vmem_limit_bytes=int(limit * 1024 * 1024)),
        cost_estimate=pl.CostEstimate(flops=flops, bytes_accessed=moved, transcendentals=0),
        name=name,
    )(*args)


def shape(dims, kind=F32):
    return jax.ShapeDtypeStruct(dims, kind)


def regroup(blocks):
    return lax.all_to_all(blocks, "tm", split_axis=0, concat_axis=0, tiled=True)


def on_device(inputs, cotangent, w_pos, w_filt, log_rates, skip_gain, w_conv):
    swap = [(i, i ^ 1) for i in range(lax.axis_size("batch"))]
    signal, upstream = inputs[0], cotangent[0]
    w_taps = jnp.transpose(w_conv, (1, 0, 2))
    tabs = tuple(jnp.asarray(t) for t in transform_tables())
    feat = jnp.asarray(np.concatenate(feature_tables(), axis=0))

    message = call(
        prep_kernel,
        shape((WIDTH, ROWS + SPAN), BF16),
        (signal, upstream, w_taps),
        [
            pltpu.VMEM((ROWS, WIDTH), BF16),
            pltpu.VMEM((ROWS, WIDTH), BF16),
            pltpu.VMEM((KERNEL, WIDTH, WIDTH), BF16),
            pltpu.VMEM((EDGE + ROWS + 8, WIDTH), F32),
            pltpu.VMEM((SPAN, WIDTH), F32),
            pltpu.VMEM((WIDTH, ROWS), BF16),
            pltpu.VMEM((WIDTH, SPAN), BF16),
            pltpu.SemaphoreType.DMA((4 + KERNEL,)),
        ],
        flops=2 * KERNEL * WIDTH * WIDTH * (ROWS + EDGE),
        name="prep",
        specs=[HBM] * 3,
        out_specs=HBM,
    )
    received = regroup(message.reshape(SHARDS, OWN, ROWS + SPAN))
    cot_peer = lax.ppermute(upstream, "batch", swap)
    received, cot_peer = lax.optimization_barrier((received, cot_peer))

    stack = pltpu.VMEM((STACK, LANES), F32)
    wide = pltpu.VMEM((STACK, 2 * LANES), BF16)
    saved = [pltpu.VMEM((2 * FEAT, LENGTH), BF16), pltpu.VMEM((FEAT, LENGTH), F32), pltpu.VMEM((OWN, LENGTH), F32)]
    flops = 2 * 3 * (2 * STACK * LANES * LANES + STACK * 4 * LANES * LANES)
    hidden, cosines, taps, tap_spec, par = call(
        taps_kernel,
        [
            shape((2 * FEAT, LENGTH), BF16),
            shape((FEAT, LENGTH)),
            shape((OWN, LENGTH)),
            shape((STACK, 2 * LANES)),
            shape((OWN, LANES)),
        ],
        (w_pos, w_filt, log_rates[None], skip_gain[None], feat, *tabs),
        [*saved, pltpu.VMEM((STACK, 2 * LANES), F32), pltpu.VMEM((OWN, LANES), F32), stack, wide, wide, pltpu.SemaphoreType.DMA((5,))],
        flops=flops * 2,
        name="taps",
        out_specs=[HBM] * 5,
        limit=63.5,
    )
    act_message, before, sig_spec = call(
        forward_kernel,
        [shape((SHARDS, OWN, SPAN), BF16), shape((STACK, LANES)), shape((STACK, 2 * LANES))],
        (received, tap_spec, par, *tabs),
        [
            pltpu.VMEM((SHARDS, OWN, ROWS), BF16),
            pltpu.VMEM((STACK, 2 * LANES), F32),
            pltpu.VMEM((STACK, 2 * LANES), F32),
            pltpu.VMEM((SHARDS, OWN, SPAN), BF16),
            *[pltpu.VMEM(t.shape, t.dtype) for t in tabs],
            stack,
            stack,
            wide,
            wide,
            pltpu.VMEM((OWN, LANES), F32),
            pltpu.SemaphoreType.DMA((14,)),
        ],
        flops=flops * 2,
        name="forward",
        specs=[HBM] * 11,
        out_specs=[HBM] * 3,
    )
    act = regroup(act_message).reshape(WIDTH, SPAN)
    ig_message, small = call(
        backward_kernel,
        [shape((SHARDS, OWN, ROWS), BF16), shape((2, 2 * OWN, LANES))],
        (received, before, sig_spec, tap_spec, par, hidden, cosines, feat, taps, *tabs),
        [
            pltpu.VMEM((SHARDS, OWN, ROWS + SPAN), BF16),
            stack,
            pltpu.VMEM((STACK, 2 * LANES), F32),
            pltpu.VMEM((STACK, 2 * LANES), F32),
            pltpu.VMEM((OWN, LANES), F32),
            *saved[:2],
            saved[0],
            saved[2],
            *[pltpu.VMEM(t.shape, t.dtype) for t in tabs],
            stack,
            pltpu.VMEM((SHARDS, OWN, ROWS), BF16),
            pltpu.VMEM((2, 2 * OWN, LANES), F32),
            stack,
            wide,
            wide,
            pltpu.VMEM((OWN, LENGTH), F32),
            pltpu.SemaphoreType.DMA((19,)),
        ],
        flops=flops * 4,
        name="backward",
        specs=[HBM] * 17,
        out_specs=[HBM] * 2,
        limit=63.75,
    )
    act, ig_message, small = lax.optimization_barrier((act, ig_message, small))
    act_peer = lax.ppermute(act, "batch", swap)
    small_peer = lax.ppermute(small, "batch", swap)
    lanes = CONV + ROWS + 2 * LANES
    sums = call(
        conv_kernel,
        shape((WIDTH, lanes), BF16),
        (act, act_peer, upstream, cot_peer, ig_message.reshape(WIDTH, ROWS), small, small_peer),
        [
            pltpu.VMEM((2, WIDTH, SPAN), BF16),
            pltpu.VMEM((2, ROWS, HALF), BF16),
            pltpu.VMEM((WIDTH, ROWS), BF16),
            pltpu.VMEM((2, 2 * OWN, LANES), F32),
            pltpu.VMEM((2, HALO + ROWS + 8, HALF), F32),
            pltpu.VMEM((KERNEL, WIDTH, HALF), BF16),
            pltpu.VMEM((WIDTH, ROWS + 2 * LANES), BF16),
            pltpu.SemaphoreType.DMA((10 + KERNEL,)),
        ],
        flops=2 * KERNEL * WIDTH * HALF * 2 * ROWS,
        name="conv_grad",
        specs=[HBM] * 7,
        out_specs=HBM,
    )
    spread = regroup(sums.reshape(SHARDS, OWN, lanes))
    mixed = call(
        mixed_kernel,
        shape((ROWS, WIDTH), BF16),
        (act, w_taps, sums),
        [
            pltpu.VMEM((WIDTH, SPAN), BF16),
            pltpu.VMEM((KERNEL, WIDTH, WIDTH), BF16),
            pltpu.VMEM((ROWS + EDGE, WIDTH), F32),
            pltpu.VMEM((ROWS, WIDTH), BF16),
            pltpu.SemaphoreType.DMA((2 + KERNEL,)),
        ],
        flops=2 * KERNEL * WIDTH * WIDTH * (ROWS + EDGE),
        name="mixed",
        specs=[HBM] * 3,
        out_specs=HBM,
    )
    spread, mixed = lax.optimization_barrier((spread, mixed))
    payload = call(gather_kernel, shape((80, WIDTH), BF16), (spread,), name="gather", limit=12)
    met = lax.ppermute(payload, "batch", [(i, i ^ 2) for i in range(8)])
    pair = call(pair_kernel, shape((80, WIDTH), BF16), (payload, met), name="pair", limit=12)
    met = lax.ppermute(pair, "batch", [(i, i ^ 6) for i in range(8)])
    spread, pair = lax.optimization_barrier((spread, pair))
    input_grad = call(
        input_kernel,
        shape((ROWS, WIDTH), BF16),
        (spread,),
        [pltpu.VMEM((ROWS, WIDTH), BF16), pltpu.SemaphoreType.DMA],
        name="input",
        out_specs=HBM,
        limit=12,
    )
    pair, met, input_grad = lax.optimization_barrier((pair, met, input_grad))
    peer_met = lax.ppermute(met, "batch", swap)
    peer_pair = lax.ppermute(pair, "batch", swap)
    conv_grad, pos_grad, filt_grad, rates_grad, skip_grad = call(
        join_kernel,
        [
            shape((KERNEL, OWN, WIDTH)),
            shape((FEAT, FEAT)),
            shape((FEAT, WIDTH)),
            shape((1, WIDTH)),
            shape((1, WIDTH)),
        ],
        (pair, met, peer_pair, peer_met),
        [pltpu.VMEM((80, WIDTH), F32)] * 2,
        name="join",
        limit=12,
    )
    return (
        mixed[None],
        input_grad[None],
        jnp.transpose(conv_grad, (1, 0, 2)),
        pos_grad,
        filt_grad,
        rates_grad[0],
        skip_grad[0],
    )


def solution(mesh):
    in_specs = (P("batch", "tm", None), P("batch", "tm", None), P(), P(), P(), P(), P())
    out_specs = (P("batch", "tm", None), P("batch", "tm", None), P("tm", None, None), P(), P(), P(), P())
    return jax.shard_map(on_device, mesh=mesh, in_specs=in_specs, out_specs=out_specs, check_vma=False)
```
